32 devices in a mesh: section: 2 (over core), batch: 16 (over z, y, x).
Axes of the slice: x: 2, y: 2, z: 4, core: 2. Of those that a mesh axis runs over, the one named last changes fastest.
Arguments:
- tokens: bfloat16 [16384, 768], P('batch'), may hold values from -6 to 6
- cotangent: bfloat16 [16384, 768], P('batch'), may hold values from -6 to 6
- sentence_ids: int32 [16384], P('batch'), may hold values from 0 to 3, as said below
- query_weight: bfloat16 [2, 768, 768], P('section'), may hold values from -0.21875 to 0.21875
- query_bias: float32 [2, 768], P('section'), may hold values from -1.8 to 1.8
- keys_weight: bfloat16 [2, 768, 768], P('section'), may hold values from -0.21875 to 0.21875
- value_weight: bfloat16 [2, 768, 768], P('section'), may hold values from -0.21875 to 0.21875
- value_bias: float32 [2, 768], P('section'), may hold values from -1.8 to 1.8
- mixer_weight: bfloat16 [2, 768, 768], P('section'), may hold values from -0.875 to 0.875
- mixer_bias: float32 [2, 768], P('section'), may hold values from -1.8 to 1.8
- first_gain: float32 [2, 768], P('section'), may hold values from 0.5 to 1.5
- first_shift: float32 [2, 768], P('section'), may hold values from -1.8 to 1.8
- expand_weight: bfloat16 [2, 768, 3072], P('section'), may hold values from -0.21875 to 0.21875
- expand_bias: float32 [2, 3072], P('section'), may hold values from -1.8 to 1.8
- shrink_weight: bfloat16 [2, 3072, 768], P('section'), may hold values from -0.109375 to 0.109375
- shrink_bias: float32 [2, 768], P('section'), may hold values from -1.8 to 1.8
- second_gain: float32 [2, 768], P('section'), may hold values from 0.5 to 1.5
- second_shift: float32 [2, 768], P('section'), may hold values from -1.8 to 1.8
Outputs:
- layer_out: bfloat16 [2, 16384, 768], P('section', 'batch')
- layer_in_grad: bfloat16 [2, 16384, 768], P('section', 'batch')
- query_dweight: float32 [2, 768, 768], P('section')
- query_dbias: float32 [2, 768], P('section')
- keys_dweight: float32 [2, 768, 768], P('section')
- value_dweight: float32 [2, 768, 768], P('section')
- value_dbias: float32 [2, 768], P('section')
- mixer_dweight: float32 [2, 768, 768], P('section')
- mixer_dbias: float32 [2, 768], P('section')
- first_dgain: float32 [2, 768], P('section')
- first_dshift: float32 [2, 768], P('section')
- expand_dweight: float32 [2, 768, 3072], P('section')
- expand_dbias: float32 [2, 3072], P('section')
- shrink_dweight: float32 [2, 3072, 768], P('section')
- shrink_dbias: float32 [2, 768], P('section')
- second_dgain: float32 [2, 768], P('section')
- second_dshift: float32 [2, 768], P('section')
The draws below stay inside these ranges and needn't reach their ends.
Inputs may be any that keep to these rules, and one draw needn't show every extreme that they name: Within each aligned block of 512 tokens of sentence_ids, counted from the start, the ids number whole sentences in order from 0; each sentence holds 128, 256 or 512 tokens. Tokens attend only to tokens of the same block with the same id.
All inputs are finite; a program needn't handle non-finite values.
Results may differ from the reference program's by a relative error of at most 0.02.
Values may be sent and summed in bfloat16 or wider, within the bound.
A program may use at most 256 MiB of HBM per device.

```python
import jax
import jax.numpy as jnp
from jax import lax

D = 768
HEADS = 12
HEAD_DIM = 64
FF = 3072
ROWS = 512
TOKENS = 16384
N_SECTION = 2


def draw_sentence_ids(key, part):
    key = jax.random.fold_in(key, 11)
    blocks = TOKENS // ROWS
    pattern = jax.random.randint(key, (blocks,), 0, 5)
    pattern = pattern.at[0].set(4)
    lookup_table = jnp.array([[0, 0, 0, 0], [0, 0, 1, 1], [0, 0, 1, 2], [0, 1, 2, 2], [0, 1, 2, 3]], dtype=jnp.int32)
    quarter = jnp.arange(ROWS, dtype=jnp.int32) // (ROWS // 4)
    return lookup_table[pattern][:, quarter].reshape(TOKENS).astype(jnp.int32)


def level_of(stream_key, shape, cuts, least, high):
    gain = 1.0
    for position, shards_of in cuts:
        draws = jax.random.uniform(jax.random.fold_in(jax.random.fold_in(stream_key, 6), position), (shards_of,), jnp.float32, least / len(cuts), high / len(cuts))
        gain = gain * jnp.repeat(jnp.exp(draws), shape[position] // shards_of).reshape((-1,) + (1,) * (len(shape) - 1 - position))
    return gain


def bell_draw(own_key, extent, width, limit, split=(), kind=jnp.bfloat16):
    entries = width * jax.random.normal(own_key, extent, jnp.float32)
    if split:
        entries = entries * level_of(own_key, extent, split, -0.22, 0.18)
    return jnp.clip(entries, -limit, limit).astype(kind)


def setup_inputs(seed: int = 0) -> dict:
    seeds = jax.random.split(jax.random.key(seed), 19)
    return {
        "tokens": bell_draw(seeds[0], (TOKENS, D), 1.0, 6.0, ((0, 16),)),
        "cotangent": bell_draw(seeds[1], (TOKENS, D), 1.0, 6.0, ((0, 16),)),
        "sentence_ids": draw_sentence_ids(jax.random.fold_in(seeds[18], 71), 0),
        "query_weight": bell_draw(seeds[3], (N_SECTION, D, D), D ** -0.5, 0.21875, ((0, 2),)),
        "query_bias": bell_draw(seeds[4], (N_SECTION, D), 0.3, 1.8, ((0, 2),), jnp.float32),
        "keys_weight": bell_draw(seeds[5], (N_SECTION, D, D), D ** -0.5, 0.21875, ((0, 2),)),
        "value_weight": bell_draw(seeds[6], (N_SECTION, D, D), D ** -0.5, 0.21875, ((0, 2),)),
        "value_bias": bell_draw(seeds[7], (N_SECTION, D), 0.3, 1.8, ((0, 2),), jnp.float32),
        "mixer_weight": bell_draw(seeds[8], (N_SECTION, D, D), (D // 16) ** -0.5, 0.875, ((0, 2),)),
        "mixer_bias": bell_draw(seeds[9], (N_SECTION, D), 0.3, 1.8, ((0, 2),), jnp.float32),
        "first_gain": jnp.clip(1.0 + 0.1 * jax.random.normal(seeds[10], (N_SECTION, D), jnp.float32), 0.5, 1.5),
        "first_shift": bell_draw(seeds[11], (N_SECTION, D), 0.3, 1.8, ((0, 2),), jnp.float32),
        "expand_weight": bell_draw(seeds[12], (N_SECTION, D, FF), D ** -0.5, 0.21875, ((0, 2),)),
        "expand_bias": bell_draw(seeds[13], (N_SECTION, FF), 0.3, 1.8, ((0, 2),), jnp.float32),
        "shrink_weight": bell_draw(seeds[14], (N_SECTION, FF, D), FF ** -0.5, 0.109375, ((0, 2),)),
        "shrink_bias": bell_draw(seeds[15], (N_SECTION, D), 0.3, 1.8, ((0, 2),), jnp.float32),
        "second_gain": jnp.clip(1.0 + 0.1 * jax.random.normal(seeds[16], (N_SECTION, D), jnp.float32), 0.5, 1.5),
        "second_shift": bell_draw(seeds[17], (N_SECTION, D), 0.3, 1.8, ((0, 2),), jnp.float32),
    }


@jax.custom_vjp
def low(v):
    return lax.optimization_barrier(v.astype(jnp.bfloat16)).astype(jnp.float32)

@jax.custom_vjp
def low_back(v):
    return v

def low_keep(v):
    return (low(v), None)

def low_pass(kept, grad):
    return (grad,)

def back_keep(v):
    return (v, None)

def back_low(kept, grad):
    return (low(grad),)
low.defvjp(low_keep, low_pass)
low_back.defvjp(back_keep, back_low)

def both_low(values):
    return low_back(low(values))

def matmul(left_side, right_side):
    return jnp.dot(left_side, right_side, precision=lax.Precision.HIGHEST)

def normalize(values, gain_row, shift_row):
    centred = values - lax.optimization_barrier(jnp.mean(values, axis=-1, keepdims=True))
    spread = lax.optimization_barrier(jnp.mean(centred * centred, axis=-1, keepdims=True))
    return centred * lax.rsqrt(spread + 1e-06) * gain_row + shift_row

def gelu_exact(values):
    return 0.5 * values * (1.0 + jax.scipy.special.erf(values * 0.7071067811865476))

def attend_block(queries, keys_block, values, labels):
    scores = jnp.einsum('qhd,khd->hqk', queries, keys_block, precision=lax.Precision.HIGHEST) * HEAD_DIM ** (-0.5)
    scores = low_back(scores)
    same_sentence = labels[:, None] == labels[None, :]
    scores = jnp.where(same_sentence[None], scores, -1000000000.0)
    shifted = scores - lax.optimization_barrier(jnp.max(scores, axis=-1, keepdims=True))
    exponent = jnp.exp(shifted)
    probability = exponent / lax.optimization_barrier(jnp.sum(exponent, axis=-1, keepdims=True))
    return jnp.einsum('hqk,khd->qhd', low(probability), values, precision=lax.Precision.HIGHEST)

def attend_items(block_items):
    return jax.checkpoint(attend_block)(block_items[0], block_items[1], block_items[2], block_items[3])

def encoder_layer(hidden, params, layer_index, labels):
    query_w, query_b, keys_w, value_w, value_b, mixer_w, mixer_b, gain_one, shift_one, expand_w, expand_b, shrink_w, shrink_b, gain_two, shift_two = [stored[layer_index] for stored in params]
    queries = both_low(matmul(hidden, query_w) + query_b)
    keys_all = both_low(matmul(hidden, keys_w))
    values = both_low(matmul(hidden, value_w) + value_b)
    blocks = hidden.shape[0] // ROWS
    block_split = (blocks, ROWS, HEADS, HEAD_DIM)
    attended = lax.map(attend_items, (queries.reshape(block_split), keys_all.reshape(block_split), values.reshape(block_split), labels.reshape(blocks, ROWS)))
    attended = both_low(attended.reshape(hidden.shape))
    mixed_out = low_back(matmul(attended, mixer_w) + mixer_b)
    first_norm = normalize(hidden + mixed_out, gain_one, shift_one)
    inner_act = low_back(matmul(low(first_norm), expand_w) + expand_b)
    outer_act = low_back(matmul(low(gelu_exact(inner_act)), shrink_w) + shrink_b)
    return normalize(first_norm + outer_act, gain_two, shift_two)

def reference(tokens, cotangent, sentence_ids, query_weight, query_bias, keys_weight, value_weight, value_bias, mixer_weight, mixer_bias, first_gain, first_shift, expand_weight, expand_bias, shrink_weight, shrink_bias, second_gain, second_shift):
    params = tuple((stored.astype(jnp.float32) for stored in (query_weight, query_bias, keys_weight, value_weight, value_bias, mixer_weight, mixer_bias, first_gain, first_shift, expand_weight, expand_bias, shrink_weight, shrink_bias, second_gain, second_shift)))

    def forward(inputs, offset, weights):
        first_out = encoder_layer(inputs, weights, 0, sentence_ids)
        kept_first = low(first_out)
        second_out = encoder_layer(low_back(kept_first + offset), weights, 1, sentence_ids)
        return (second_out, kept_first)
    inputs = tokens.astype(jnp.float32)
    second_out, pullback, kept_first = jax.vjp(forward, inputs, jnp.zeros(inputs.shape, jnp.float32), params, has_aux=True)
    grad_in, grad_mid, weight_grads = pullback(cotangent.astype(jnp.float32))
    layer_out = jnp.stack([kept_first, second_out]).astype(jnp.bfloat16)
    layer_in_grad = jnp.stack([grad_in, grad_mid]).astype(jnp.bfloat16)
    return (layer_out, layer_in_grad, weight_grads[0], weight_grads[1], weight_grads[2], weight_grads[3], weight_grads[4], weight_grads[5], weight_grads[6], weight_grads[7], weight_grads[8], weight_grads[9], weight_grads[10], weight_grads[11], weight_grads[12], weight_grads[13], weight_grads[14])
```

```python
import functools

import jax
import jax.numpy as jnp
from jax import lax
from jax.experimental import pallas as pl
from jax.experimental.pallas import tpu as pltpu
from jax.sharding import PartitionSpec as P

HEADS = 12
HEAD_DIM = 64
ROWS = 512


epsilon = 1e-06
root_half = 0.7071067811865476
inv_root_tau = 0.3989422804014327


MESH = pl.DeviceIdType.MESH
NB = 12
BLK = 768
COL = 384
HALF = 384
CH = 96
SUB = 48
NSTAGE = 12


def when(cond, fn):
    if isinstance(cond, bool):
        if cond:
            fn()
    else:
        pl.when(cond)(fn)


def coords():
    s = lax.axis_index("section")
    b = lax.axis_index("batch")
    return s, b // 4, (b // 2) % 2, b % 2


def dev(s, z, y, x):
    return (s, z * 4 + y * 2 + x)


class Comm:
    def __init__(self, refs):
        self.__dict__.update(refs)
        s, z, y, x = coords()
        self.s, self.p = s, z
        self.core = dev(1 - s, z, y, x)
        xn, yn = dev(s, z, y, 1 - x), dev(s, z, 1 - y, x)
        self.u = (x, y)
        self.w = (y, x)
        self.n1 = (xn, yn)
        self.n3 = (yn, xn)
        self.up = dev(s, jnp.minimum(z + 1, 3), y, x)
        self.dn = dev(s, jnp.maximum(z - 1, 0), y, x)

    def barrier(self):
        s, z, y, x = coords()
        bar = pltpu.get_barrier_semaphore()
        peers = [self.core, self.n1[0], self.n1[1]] + [dev(s, lax.rem(z + k, 4), y, x) for k in (1, 2, 3)]
        for d in peers:
            pl.semaphore_signal(bar, inc=1, device_id=d, device_id_type=MESH)
        pl.semaphore_wait(bar, len(peers))

    def remote(self, src, dst, ss, rs, d):
        return pltpu.make_async_remote_copy(src_ref=src, dst_ref=dst, send_sem=ss, recv_sem=rs, device_id=d, device_id_type=MESH)

    def prt_copy(self, src, b):
        return self.remote(src, self.prt.at[b], self.prt_s.at[b], self.prt_r.at[b], self.core)

    def loads(self, st, b):
        sl = lax.rem(b, 2)
        cols = pl.ds(st * COL, COL)
        return (
            pltpu.make_async_copy(self.acc.at[b, :, cols], self.lda.at[st, sl], self.ld_sem.at[st, sl, 0]),
            pltpu.make_async_copy(self.prt.at[b, :, cols], self.ldp.at[st, sl], self.ld_sem.at[st, sl, 1]),
        )

    def s0(self, b):
        self.prt_copy(self.prt.at[b], b).wait_recv()
        for st in (0, 1):
            for c in self.loads(st, b):
                c.start()

    def r1_copy(self, st, b):
        sl = lax.rem(b, 2)
        rows = pl.ds(pl.multiple_of((1 - self.u[st]) * HALF, HALF), HALF)
        return self.remote(self.lda.at[st, sl, rows], self.r1.at[st, sl], self.r1_s.at[st, sl], self.r1_r.at[st, sl], self.n1[st])

    def s1(self, b):
        sl = lax.rem(b, 2)
        for st in (0, 1):
            for c in self.loads(st, b):
                c.wait()
            oth = pl.ds(pl.multiple_of((1 - self.u[st]) * HALF, HALF), HALF)
            own = pl.ds(pl.multiple_of(self.u[st] * HALF, HALF), HALF)
            self.lda[st, sl, oth] += self.ldp[st, sl, oth]
            self.r1_copy(st, b).start()
            self.lda[st, sl, own] += self.ldp[st, sl, own]

    def zsend(self, st, b, lo, hi, up):
        zs = lax.rem(b, 4)
        if up:
            return self.remote(self.zbuf.at[st, zs, pl.ds(lo, hi - lo)], self.ru.at[st, zs, pl.ds(lo - CH, hi - lo)],
                               self.ru_s.at[st, zs], self.ru_r.at[st, zs], self.up)
        return self.remote(self.zbuf.at[st, zs, pl.ds(lo, hi - lo)], self.rd.at[st, zs, pl.ds(lo, hi - lo)],
                           self.rd_s.at[st, zs], self.rd_r.at[st, zs], self.dn)

    def zadd(self, st, b, lo, hi, up):
        zs = lax.rem(b, 4)
        self.zsend(st, b, lo, hi, up).wait_recv()
        if up:
            self.zbuf[st, zs, lo:hi] += self.ru[st, zs, lo - CH:hi - CH]
        else:
            self.zbuf[st, zs, lo:hi] += self.rd[st, zs, lo:hi]

    def s2(self, b):
        sl, zs = lax.rem(b, 2), lax.rem(b, 4)
        for st in (0, 1):
            self.r1_copy(st, b).wait()
            own = pl.ds(pl.multiple_of(self.u[st] * HALF, HALF), HALF)
            self.zbuf[st, zs] = self.lda[st, sl, own] + self.r1[st, sl]
            pl.when(self.p == 0)(lambda: self.zsend(st, b, CH, 4 * CH, True).start())
            pl.when(self.p == 3)(lambda: self.zsend(st, b, 0, 3 * CH, False).start())

    def s3(self, b):
        for st in (0, 1):
            @pl.when(self.p == 1)
            def _():
                self.zadd(st, b, CH, 4 * CH, True)
                self.zsend(st, b, 2 * CH, 4 * CH, True).start()

            @pl.when(self.p == 2)
            def _():
                self.zadd(st, b, 0, 3 * CH, False)
                self.zsend(st, b, 0, 2 * CH, False).start()

    def s4(self, b):
        for st in (0, 1):
            @pl.when(self.p == 2)
            def _():
                self.zadd(st, b, 2 * CH, 4 * CH, True)
                self.zsend(st, b, 3 * CH, 4 * CH, True).start()

            @pl.when(self.p == 1)
            def _():
                self.zadd(st, b, 0, 2 * CH, False)
                self.zsend(st, b, 0, CH, False).start()

    def r3_copy(self, st, b):
        sl, zs = lax.rem(b, 2), lax.rem(b, 4)
        rows = pl.ds(pl.multiple_of(self.p * CH + (1 - self.w[st]) * SUB, SUB), SUB)
        return self.remote(self.zbuf.at[st, zs, rows], self.r3.at[st, sl], self.r3_s.at[st, sl], self.r3_r.at[st, sl], self.n3[st])

    def s5(self, b):
        for st in (0, 1):
            pl.when(self.p == 0)(lambda: self.zadd(st, b, 0, CH, False))
            pl.when(self.p == 3)(lambda: self.zadd(st, b, 3 * CH, 4 * CH, True))
            self.r3_copy(st, b).start()

    def res_at(self, st, b, c, lo, n, u):
        rows = pl.ds(pl.multiple_of(u * HALF + c * CH + lo, SUB), n)
        return self.res.at[b, rows, pl.ds(st * COL, COL)]

    def fin_copies(self, st, b):
        sl = lax.rem(b, 2)
        there = self.res_at(st, b, self.p, self.w[st] * SUB, SUB, self.u[st])
        return (
            self.remote(self.fin.at[st, sl], there, self.ag_s.at[st, 3, 0, lax.rem(b, 4)], self.wr.at[st, b], self.n3[st]),
            pltpu.make_async_copy(self.fin.at[st, sl], there, self.ag_s.at[st, 3, 1, lax.rem(b, 4)]),
        )

    def s6(self, b):
        sl, zs = lax.rem(b, 2), lax.rem(b, 4)
        for st in (0, 1):
            self.r3_copy(st, b).wait()
            pl.when(self.p == 0)(lambda: self.zsend(st, b, CH, 4 * CH, True).wait_send())
            pl.when(self.p == 3)(lambda: self.zsend(st, b, 0, 3 * CH, False).wait_send())

            @pl.when(self.p == 1)
            def _():
                self.zsend(st, b, 2 * CH, 4 * CH, True).wait_send()
                self.zsend(st, b, 0, CH, False).wait_send()

            @pl.when(self.p == 2)
            def _():
                self.zsend(st, b, 0, 2 * CH, False).wait_send()
                self.zsend(st, b, 3 * CH, 4 * CH, True).wait_send()

            rows = pl.ds(pl.multiple_of(self.p * CH + self.w[st] * SUB, SUB), SUB)
            self.fin[st, sl] = self.zbuf[st, zs, rows] + self.r3[st, sl]
            for c in self.fin_copies(st, b):
                c.start()

    def ag(self, st, b, c, d):
        here = self.res_at(st, b, c, 0, CH, self.u[st])
        to, sem = ((self.up, self.zr), (self.dn, self.zr), (self.n1[st], self.xr))[d]
        return self.remote(here, here, self.ag_s.at[st, d, c, lax.rem(b, 4)], sem.at[st, b, c], to)

    def spread(self, st, b, c, up, down):
        if up:
            pl.when(self.p < 3)(lambda: self.ag(st, b, c, 0).start())
        if down:
            pl.when(self.p > 0)(lambda: self.ag(st, b, c, 1).start())
        self.ag(st, b, c, 2).start()

    def s7(self, b):
        for st in (0, 1):
            far, near = self.fin_copies(st, b)
            far.wait()
            near.wait()
            self.spread(st, b, self.p, True, True)

    def hop(self, k, b):
        for st in (0, 1):
            @pl.when(self.p >= k)
            def _():
                self.ag(st, b, self.p - k, 0).wait_recv()
                self.spread(st, b, self.p - k, True, False)

            @pl.when(self.p <= 3 - k)
            def _():
                self.ag(st, b, self.p + k, 1).wait_recv()
                self.spread(st, b, self.p + k, False, True)

    def s8(self, b):
        self.hop(1, b)

    def s9(self, b):
        self.hop(2, b)

    def s10(self, b):
        self.hop(3, b)

    def s11(self, b):
        for st in (0, 1):
            for c in range(4):
                got = self.ag(st, b, c, 2)
                got.wait_send()
                got.wait_recv()
                pl.when((self.p < 3) & (self.p >= c))(lambda: self.ag(st, b, c, 0).wait_send())
                pl.when((self.p > 0) & (self.p <= c))(lambda: self.ag(st, b, c, 1).wait_send())

    def tick(self, t):
        stages = (self.s0, self.s1, self.s2, self.s3, self.s4, self.s5, self.s6, self.s7, self.s8, self.s9, self.s10, self.s11)
        for k in reversed(range(NSTAGE)):
            b = t - k
            when((b >= 0) & (b < NB), lambda: stages[k](b))

    def vec_copy(self, k):
        s, z, y, x = coords()
        to = (self.core, dev(s, z, y, 1 - x), dev(s, z, 1 - y, x), dev(s, z + 1 - 2 * lax.rem(z, 2), y, x), dev(s, lax.rem(z + 2, 4), y, x))[k]
        src = self.vec.at[1 - s] if k == 0 else self.vcur.at[k - 1]
        return self.remote(src, self.vrecv.at[k], self.v_s.at[k], self.v_r.at[k], to)

    def vec_step(self, k):
        self.vec_copy(k).wait()
        s = self.s
        before = self.vec[s] if k == 0 else self.vcur[k - 1]
        self.vcur[k] = before + self.vrecv[k]
        if k < 4:
            self.vec_copy(k + 1).start()


def scratch():
    bf = jnp.bfloat16
    dma = pltpu.SemaphoreType.DMA
    return dict(
        lda=pltpu.VMEM((2, 2, BLK, COL), bf), ldp=pltpu.VMEM((2, 2, BLK, COL), bf),
        r1=pltpu.VMEM((2, 2, HALF, COL), bf), zbuf=pltpu.VMEM((2, 4, HALF, COL), bf),
        ru=pltpu.VMEM((2, 4, 3 * CH, COL), bf), rd=pltpu.VMEM((2, 4, 3 * CH, COL), bf),
        r3=pltpu.VMEM((2, 2, SUB, COL), bf), fin=pltpu.VMEM((2, 2, SUB, COL), bf),
        vcur=pltpu.VMEM((5, 16, BLK), jnp.float32), vrecv=pltpu.VMEM((5, 16, BLK), jnp.float32),
        prt_s=dma((NB,)), prt_r=dma((NB,)), ld_sem=dma((2, 2, 2)), r1_s=dma((2, 2)), r1_r=dma((2, 2)),
        ru_s=dma((2, 4)), ru_r=dma((2, 4)), rd_s=dma((2, 4)), rd_r=dma((2, 4)), r3_s=dma((2, 2)), r3_r=dma((2, 2)),
        ag_s=dma((2, 4, 4, 4)), wr=dma((2, NB)), zr=dma((2, NB, 4)), xr=dma((2, NB, 4)), v_s=dma((5,)), v_r=dma((5,)),
    )


def reduce_kernel(names, grads, vec, res, out_vec, prt, *rest):
    refs = dict(zip(names, rest))
    s = lax.axis_index("section")
    c = Comm(dict(refs, acc=grads.at[s], prt=prt, res=res, vec=vec))
    c.barrier()
    for b in range(NB):
        c.prt_copy(grads.at[1 - s, b], b).start()
    c.vec_copy(0).start()

    def step(t, carry):
        c.tick(t)
        return carry

    lax.fori_loop(0, NB + NSTAGE - 1, step, 0)
    for k in range(5):
        c.vec_step(k)
    for b in range(NB):
        c.prt_copy(grads.at[1 - s, b], b).wait_send()
    out_vec[...] = c.vcur[4]


def reduce_grads(grads, vec):
    sc = scratch()
    hbm = pl.BlockSpec(memory_space=pl.ANY)
    vm = pl.BlockSpec(memory_space=pltpu.VMEM)
    blocks = jax.ShapeDtypeStruct((NB, BLK, BLK), jnp.bfloat16)
    res, out_vec, _ = pl.pallas_call(
        functools.partial(reduce_kernel, tuple(sc)),
        out_shape=(blocks, jax.ShapeDtypeStruct((16, BLK), jnp.float32), blocks),
        in_specs=[hbm, vm], out_specs=(hbm, vm, hbm),
        scratch_shapes=list(sc.values()),
        compiler_params=pltpu.CompilerParams(collective_id=0, has_side_effects=True, vmem_limit_bytes=48 * 2**20),
    )(grads, vec)
    return res, out_vec


def product(left_side, right_side):
    return jnp.dot(left_side, right_side, preferred_element_type=jnp.float32)


def product_left(left_side, right_side):
    return lax.dot_general(
        left_side, right_side, (((0,), (0,)), ((), ())), preferred_element_type=jnp.float32
    )


def product_right(left_side, right_side):
    return lax.dot_general(
        left_side, right_side, (((1,), (1,)), ((), ())), preferred_element_type=jnp.float32
    )


def column_total(values):
    return jnp.sum(values.astype(jnp.float32), axis=0)


def normalize(values, gain_row, shift_row):
    centred = values - jnp.mean(values, axis=-1, keepdims=True)
    inv_scale = lax.rsqrt(jnp.mean(centred * centred, axis=-1, keepdims=True) + epsilon)
    normed = centred * inv_scale
    return (normed * gain_row + shift_row, normed, inv_scale)


def normalize_back(grad_out, normed, inv_scale, gain_row):
    grad_normed = grad_out * gain_row
    first_mean = jnp.mean(grad_normed, axis=-1, keepdims=True)
    second_mean = jnp.mean(grad_normed * normed, axis=-1, keepdims=True)
    grad_values = inv_scale * (grad_normed - first_mean - normed * second_mean)
    return (grad_values, jnp.sum(grad_out * normed, axis=0), jnp.sum(grad_out, axis=0))


def attention_scores(queries, keys_low, labels):
    heads_split = (queries.shape[0], HEADS, HEAD_DIM)
    scores = jnp.einsum(
        "qhd,khd->hqk",
        queries.reshape(heads_split),
        keys_low.reshape(heads_split),
        preferred_element_type=jnp.float32,
    ) * HEAD_DIM ** (-0.5)
    same_sentence = labels[:, None] == labels[None, :]
    return jnp.where(same_sentence[None], scores, -1000000000.0)


def layer_forward(hidden, weights, labels):
    (
        query_w,
        query_b,
        keys_w,
        value_w,
        value_b,
        mixer_w,
        mixer_b,
        gain_one,
        shift_one,
        expand_w,
        expand_b,
        shrink_w,
        shrink_b,
        gain_two,
        shift_two,
    ) = weights
    row_count = hidden.shape[0]
    queries = (product(hidden, query_w) + query_b).astype(jnp.bfloat16)
    keys_low = product(hidden, keys_w).astype(jnp.bfloat16)
    values = (product(hidden, value_w) + value_b).astype(jnp.bfloat16)
    scores = attention_scores(queries, keys_low, labels)
    row_peak = jnp.max(scores, axis=-1, keepdims=True)
    exponent = jnp.exp(scores - row_peak)
    totals = jnp.sum(exponent, axis=-1, keepdims=True)
    probs_low = (exponent / totals).astype(jnp.bfloat16)
    logsum = row_peak + jnp.log(totals)
    attended = jnp.einsum(
        "hqk,khd->qhd",
        probs_low,
        values.reshape(row_count, HEADS, HEAD_DIM),
        preferred_element_type=jnp.float32,
    )
    attended = attended.reshape(row_count, HEADS * HEAD_DIM).astype(jnp.bfloat16)
    mixed_out = product(attended, mixer_w) + mixer_b
    first_norm, normed_one, scale_one = normalize(
        hidden.astype(jnp.float32) + mixed_out, gain_one, shift_one
    )
    first_low = first_norm.astype(jnp.bfloat16)
    inner_act = product(first_low, expand_w) + expand_b
    normal_cdf = 0.5 * (1.0 + lax.erf(inner_act * root_half))
    gelu_slope = normal_cdf + inner_act * inv_root_tau * jnp.exp(-0.5 * inner_act * inner_act)
    active_low = (inner_act * normal_cdf).astype(jnp.bfloat16)
    outer_act = product(active_low, shrink_w) + shrink_b
    layer_final, normed_two, scale_two = normalize(first_norm + outer_act, gain_two, shift_two)
    kept_state = (
        queries,
        keys_low,
        values,
        logsum,
        attended,
        normed_one,
        scale_one,
        first_low,
        gelu_slope,
        active_low,
        normed_two,
        scale_two,
    )
    return (layer_final, kept_state)


def upper_backward(grad_final, weights, kept_state):
    (
        query_w,
        query_b,
        keys_w,
        value_w,
        value_b,
        mixer_w,
        mixer_b,
        gain_one,
        shift_one,
        expand_w,
        expand_b,
        shrink_w,
        shrink_b,
        gain_two,
        shift_two,
    ) = weights
    (
        queries,
        keys_low,
        values,
        logsum,
        attended,
        normed_one,
        scale_one,
        first_low,
        gelu_slope,
        active_low,
        normed_two,
        scale_two,
    ) = kept_state
    grad_two, dgain_two, dshift_two = normalize_back(grad_final, normed_two, scale_two, gain_two)
    outer_grad = grad_two.astype(jnp.bfloat16)
    inner_grad = (product_right(outer_grad, shrink_w) * gelu_slope).astype(jnp.bfloat16)
    grad_first = grad_two + product_right(inner_grad, expand_w)
    grad_one, dgain_one, dshift_one = normalize_back(grad_first, normed_one, scale_one, gain_one)
    mixed_grad = grad_one.astype(jnp.bfloat16)
    attended_grad = product_right(mixed_grad, mixer_w).astype(jnp.bfloat16)
    upper_terms = (
        product_left(attended, mixed_grad),
        column_total(mixed_grad),
        dgain_one,
        dshift_one,
        product_left(first_low, inner_grad),
        column_total(inner_grad),
        product_left(active_low, outer_grad),
        column_total(outer_grad),
        dgain_two,
        dshift_two,
    )
    return (grad_one, attended_grad, upper_terms)


def lower_backward(grad_one, attended_grad, hidden, weights, labels, kept_state):
    query_w = weights[0]
    keys_w = weights[2]
    value_w = weights[3]
    queries, keys_low, values, logsum = (kept_state[0], kept_state[1], kept_state[2], kept_state[3])
    row_count = hidden.shape[0]
    heads_split = (row_count, HEADS, HEAD_DIM)
    scores = attention_scores(queries, keys_low, labels)
    probability = jnp.exp(scores - logsum)
    grad_heads = attended_grad.reshape(heads_split)
    grad_probs = jnp.einsum(
        "qhd,khd->hqk", grad_heads, values.reshape(heads_split), preferred_element_type=jnp.float32
    )
    row_total = jnp.sum(probability * grad_probs, axis=-1, keepdims=True)
    score_grad = (probability * (grad_probs - row_total)).astype(jnp.bfloat16)
    query_grad = (
        (
            jnp.einsum(
                "hqk,khd->qhd",
                score_grad,
                keys_low.reshape(heads_split),
                preferred_element_type=jnp.float32,
            )
            * HEAD_DIM ** (-0.5)
        )
        .reshape(row_count, HEADS * HEAD_DIM)
        .astype(jnp.bfloat16)
    )
    keys_grad = (
        (
            jnp.einsum(
                "hqk,qhd->khd",
                score_grad,
                queries.reshape(heads_split),
                preferred_element_type=jnp.float32,
            )
            * HEAD_DIM ** (-0.5)
        )
        .reshape(row_count, HEADS * HEAD_DIM)
        .astype(jnp.bfloat16)
    )
    value_grad = (
        jnp.einsum(
            "hqk,qhd->khd",
            probability.astype(jnp.bfloat16),
            grad_heads,
            preferred_element_type=jnp.float32,
        )
        .reshape(row_count, HEADS * HEAD_DIM)
        .astype(jnp.bfloat16)
    )
    grad_hidden = (
        grad_one
        + product_right(query_grad, query_w)
        + product_right(keys_grad, keys_w)
        + product_right(value_grad, value_w)
    )
    lower_terms = (
        product_left(hidden, query_grad),
        column_total(query_grad),
        product_left(hidden, keys_grad),
        product_left(hidden, value_grad),
        column_total(value_grad),
    )
    return (grad_hidden, lower_terms)


def grads_blocks(lower, upper):
    q_dw, q_db, k_dw, v_dw, v_db = lower
    m_dw, m_db, g1, s1, e_dw, e_db, sh_dw, sh_db, g2, s2 = upper
    low = lambda a: a.astype(jnp.bfloat16)
    blocks = jnp.concatenate([
        low(sh_dw).reshape(4, BLK, BLK),
        low(e_dw).reshape(BLK, 4, BLK).transpose(1, 0, 2),
        jnp.stack([low(m_dw), low(q_dw), low(k_dw), low(v_dw)]),
    ])
    rows = jnp.concatenate([
        jnp.stack([q_db, v_db, m_db, g1, s1, sh_db, g2, s2]), e_db.reshape(4, BLK), jnp.zeros((4, BLK), jnp.float32)])
    return blocks, rows


def outputs_of(res, vec):
    wide = lambda a: a.astype(jnp.float32)
    sh_dw = wide(res[0:4].reshape(4 * BLK, BLK))
    e_dw = wide(res[4:8].transpose(1, 0, 2).reshape(BLK, 4 * BLK))
    m_dw, q_dw, k_dw, v_dw = (wide(res[i]) for i in (8, 9, 10, 11))
    q_db, v_db, m_db, g1, s1, sh_db, g2, s2 = (vec[i] for i in range(8))
    e_db = vec[8:12].reshape(4 * BLK)
    return (q_dw, q_db, k_dw, v_dw, v_db, m_dw, m_db, g1, s1, e_dw, e_db, sh_dw, sh_db, g2, s2)


def body(tokens, cotangent, sentence_ids, *stored):
    s = lax.axis_index("section")
    own = tuple(w[0] for w in stored)
    other = tuple(lax.ppermute(w, "section", [(0, 1), (1, 0)]) for w in own)
    first = tuple(jnp.where(s == 0, a, b) for a, b in zip(own, other))
    second = tuple(jnp.where(s == 0, b, a) for a, b in zip(own, other))
    half = tokens.shape[0] // 2
    part = lambda a: lax.dynamic_slice_in_dim(a, s * half, half, 0)
    micro = half // ROWS
    h = part(tokens)
    dy = part(cotangent)
    labels = part(sentence_ids)
    assert micro == 1
    out0, kept0 = layer_forward(h, first, labels)
    out0 = out0.astype(jnp.bfloat16)
    out1, kept1 = layer_forward(out0, second, labels)
    out1 = out1.astype(jnp.bfloat16)
    go, ag, up1 = upper_backward(dy.astype(jnp.float32), second, kept1)
    gh, lo1 = lower_backward(go, ag, out0, second, labels, kept1)
    gin1 = gh.astype(jnp.bfloat16)
    go, ag, up0 = upper_backward(gin1.astype(jnp.float32), first, kept0)
    gh, lo0 = lower_backward(go, ag, h, first, labels, kept0)
    gin0 = gh.astype(jnp.bfloat16)

    def both(zero, one):
        mine = jnp.where(s == 0, zero, one)
        got = lax.ppermute(jnp.where(s == 0, one, zero), "section", [(0, 1), (1, 0)])
        return jnp.concatenate([jnp.where(s == 0, mine, got), jnp.where(s == 0, got, mine)])[None]

    if lax.axis_size("batch") == 16:
        b0, v0 = grads_blocks(lo0, up0)
        b1, v1 = grads_blocks(lo1, up1)
        sums = outputs_of(*reduce_grads(jnp.stack([b0, b1]), jnp.stack([v0, v1])))
    else:
        sums = lax.psum(tuple(lo0) + tuple(up0), ("section", "batch")), lax.psum(tuple(lo1) + tuple(up1), ("section", "batch"))
        sums = tuple(jnp.where(s == 0, a, b) for a, b in zip(*sums))
    return (both(out0, out1), both(gin0, gin1)) + tuple(total[None] for total in sums)


def solution(mesh):
    placed = (
        P("batch", None),
        P("batch", None),
        P("batch"),
        P("section", None, None),
        P("section", None),
        P("section", None, None),
        P("section", None, None),
        P("section", None),
        P("section", None, None),
        P("section", None),
        P("section", None),
        P("section", None),
        P("section", None, None),
        P("section", None),
        P("section", None, None),
        P("section", None),
        P("section", None),
        P("section", None),
    )
    return jax.shard_map(
        body,
        mesh=mesh,
        in_specs=placed,
        out_specs=(
            P("section", "batch", None),
            P("section", "batch", None),
            P("section", None, None),
            P("section", None),
            P("section", None, None),
            P("section", None, None),
            P("section", None),
            P("section", None, None),
            P("section", None),
            P("section", None),
            P("section", None),
            P("section", None, None),
            P("section", None),
            P("section", None, None),
            P("section", None),
            P("section", None),
            P("section", None),
        ),
        check_vma=False,
    )
```

```python
import functools

import jax
import jax.numpy as jnp
from jax import lax
from jax.experimental import pallas as pl
from jax.experimental.pallas import tpu as pltpu
from jax.sharding import PartitionSpec as P

T = 512
D = 768
FF = 3072
HEADS = 12
TILE = 256
PAIR = 128
EPS = 1e-06
F32, BF16 = jnp.float32, jnp.bfloat16
QB, VB, MB, G1, S1, SB, G2, S2, EB = 0, 1, 2, 3, 4, 5, 6, 7, 8


def dot(a, b):
    return jnp.dot(a, b, preferred_element_type=F32)


def dot_nt(a, b):
    return lax.dot_general(a, b, (((1,), (1,)), ((), ())), preferred_element_type=F32)


def tile(j, n=TILE):
    return pl.ds(pl.multiple_of(j * n, n), n)


def loop(n, fn, unroll=1):
    def step(i, c):
        fn(i)
        return c
    lax.fori_loop(0, n, step, 0, unroll=unroll)


def gelu_parts(u):
    a = jnp.abs(u)
    e = jnp.exp(-0.5 * u * u)
    t = 1.0 / (1.0 + (0.3275911 * 0.7071067811865476) * a)
    poly = t * (0.5 * 0.254829592 + t * (0.5 * -0.284496736 + t * (0.5 * 1.421413741 + t * (0.5 * -1.453152027 + t * (0.5 * 1.061405429)))))
    tail = poly * e
    cdf = jnp.where(u >= 0, 1.0 - tail, tail)
    return u * cdf, cdf + u * (0.3989422804014327 * e)


def fold(x):
    return jnp.sum(x.reshape(x.shape[0] // 8, 8, x.shape[1]), axis=0)


class Net:
    def __init__(self, refs):
        self.__dict__.update(refs)

    def row(self, l, r, cols=slice(None)):
        return self.par[l, r:r + 1, cols]

    def load(self, l, m):
        raise NotImplementedError

    def wait_load(self, l, m):
        raise NotImplementedError

    def point(self, name):
        pass

    def labels(self, ids):
        row = jnp.broadcast_to(ids, (PAIR, T))
        col = row.T[:, 0:1]
        self.mask[...] = jnp.where(col == ids, 0.0, -1e9).astype(F32)

    def qkv(self, l):
        def body(j):
            cols = tile(j)
            h = self.h[l]
            for m, out, b in ((0, self.q, QB), (1, self.k, None), (2, self.v, VB)):
                r = dot(h, self.w4[m, :, cols])
                if b is not None:
                    r = r + self.par[l, b:b + 1, cols]
                r = r.astype(BF16)
                out[l, :, cols] = r * BF16(0.125) if m == 0 else r
        loop(3, body)

    def attend(self, l):
        lane = lax.broadcasted_iota(jnp.int32, (1, PAIR), 1)
        R = 256

        def body(hp):
            cols = tile(hp, PAIR)
            k2, v2 = self.k[l, :, cols], self.v[l, :, cols]
            for r in range(T // R):
                rows = pl.ds(r * R, R)
                q2 = self.q[l, rows, cols]
                out = None
                for e in (0, 1):
                    keep = lane < 64 if e == 0 else lane >= 64
                    s = dot_nt(jnp.where(keep, q2, BF16(0)), k2) + self.mask[rows]
                    x = jnp.exp(s - jnp.max(s, axis=1, keepdims=True))
                    p = (x * (1.0 / jnp.sum(x, axis=1, keepdims=True))).astype(BF16)
                    self.probs[2 * hp + e, rows] = p
                    o = dot(p, jnp.where(keep, v2, BF16(0)))
                    out = o if out is None else out + o
                self.att[l, rows, cols] = out.astype(BF16)
        loop(HEADS // 2, body)

    def norm(self, l, n_ref, sc_ref, g, b, low):
        def body(i):
            rows = tile(i, 64)
            x = self.tmp[rows]
            c = x - jnp.mean(x, axis=1, keepdims=True)
            inv = lax.rsqrt(jnp.mean(c * c, axis=1, keepdims=True) + EPS)
            n = c * inv
            n_ref[l, rows] = n.astype(n_ref.dtype)
            sc_ref[l, rows] = inv
            y = n * self.row(l, g) + self.row(l, b)
            self.tmp[rows] = y
            low[rows] = y.astype(BF16)
        loop(T // 64, body)

    def mix(self, l):
        def body(j):
            cols = tile(j)
            self.tmp[:, cols] = dot(self.att[l], self.w4[3, :, cols]) + self.par[l, MB:MB + 1, cols] + self.h[l, :, cols].astype(F32)
        loop(3, body)
        self.norm(l, self.n1, self.sc1, G1, S1, self.fl.at[l])

    def expand(self, l):
        def body(j):
            for i in range(3):
                cols = pl.ds(pl.multiple_of(j * D + i * TILE, TILE), TILE)
                u = dot(self.fl[l], self.we[:, cols]) + self.par[l, pl.ds(EB + j, 1), i * TILE:(i + 1) * TILE]
                a, s = gelu_parts(u)
                self.act[:, cols] = a.astype(BF16)
                self.slope[:, cols] = s.astype(BF16)
        loop(4, body)

    def shrink(self, l, low):
        def body(j):
            cols = tile(j)
            self.tmp[:, cols] += dot(self.act[...], self.ws[:, cols]) + self.par[l, SB:SB + 1, cols]
        loop(3, body)
        self.norm(l, self.n2, self.sc2, G2, S2, low)

    def norm_back(self, l, src, n_ref, sc_ref, g, b, low, low_row):
        def body(i, c):
            rows = tile(i, 64)
            dy = src(rows)
            n = n_ref[l, rows].astype(F32)
            gr = dy * self.row(l, g)
            m1 = jnp.mean(gr, axis=1, keepdims=True)
            m2 = jnp.mean(gr * n, axis=1, keepdims=True)
            dx = sc_ref[l, rows] * (gr - m1 - n * m2)
            self.tmp[rows] = dx
            lw = dx.astype(BF16)
            low[rows] = lw
            return (c[0] + fold(dy * n), c[1] + fold(dy), c[2] + fold(lw.astype(F32)))
        z = jnp.zeros((8, D), F32)
        a, s, t = lax.fori_loop(0, T // 64, body, (z, z, z))
        for r, x in ((g, a), (b, s), (low_row, t)):
            self.vec[l, r:r + 1, :] = jnp.sum(x, axis=0, keepdims=True)

    def emit(self, l, b, rows_of):
        slot = self.emitted % 2
        for i in range(3):
            self.stage[slot, i * TILE:(i + 1) * TILE] = rows_of(i).astype(BF16)
        self.emit_out(l, b, slot)
        self.emitted += 1

    def top_back(self, l, src):
        self.norm_back(l, src, self.n2, self.sc2, G2, S2, self.og, SB)
        self.point("norm2")
        for b in range(4):
            self.emit(l, b, lambda i: dot(self.act[:, b * D + i * TILE:b * D + (i + 1) * TILE].T, self.og[...]))
        self.point("shrink")

    def inner_back(self, l, done_inner, need_expand):
        def body(j):
            for i in range(3):
                cols = pl.ds(pl.multiple_of(j * D + i * TILE, TILE), TILE)
                g = (dot_nt(self.og[...], self.ws[cols, :]) * self.slope[:, cols].astype(F32)).astype(BF16)
                self.ig[:, cols] = g
                self.vec[l, pl.ds(EB + j, 1), i * TILE:(i + 1) * TILE] = jnp.sum(g.astype(F32), axis=0, keepdims=True)
        loop(4, body)
        done_inner()
        self.point("inner")
        self.xt[...] = self.fl[l].T
        for b in range(4):
            self.emit(l, 4 + b, lambda i: dot(self.xt[i * TILE:(i + 1) * TILE], self.ig[:, b * D:(b + 1) * D]))
        self.point("expand")
        need_expand()

        def back(j):
            cols = tile(j)
            self.tmp[:, cols] += dot_nt(self.ig[...], self.we[cols, :])
        loop(3, back)
        self.point("first")

    def mid_back(self, l):
        self.norm_back(l, lambda rows: self.tmp[rows], self.n1, self.sc1, G1, S1, self.og, MB)
        self.emit(l, 8, lambda i: dot(self.att[l, :, i * TILE:(i + 1) * TILE].T, self.og[...]))

        def body(j):
            cols = tile(j)
            self.ag[:, cols] = dot_nt(self.og[...], self.w4[3, cols, :]).astype(BF16)
        loop(3, body)
        self.point("mixer")

    def attend_back(self, l):
        lane = lax.broadcasted_iota(jnp.int32, (1, PAIR), 1)

        def body(hp):
            cols = tile(hp, PAIR)
            q2, k2, v2 = self.q[l, :, cols], self.k[l, :, cols], self.v[l, :, cols]
            da = self.ag[:, cols]
            qt, dat = q2.T, da.T
            dq, dk, dv = None, [], []
            for e in (0, 1):
                keep = lane < 64 if e == 0 else lane >= 64
                p = self.probs[2 * hp + e]
                dp = dot_nt(jnp.where(keep, da, BF16(0)), v2)
                pf = p.astype(F32)
                t = pf * dp
                ds = (t - pf * jnp.sum(t, axis=1, keepdims=True)).astype(BF16)
                o = dot(ds, jnp.where(keep, k2, BF16(0)))
                dq = o if dq is None else dq + o
                dk.append(dot(qt[64 * e:64 * e + 64], ds).astype(BF16))
                dv.append(dot(dat[64 * e:64 * e + 64], p).astype(BF16))
            dq = (dq * 0.125).astype(BF16)
            dk = jnp.concatenate(dk, axis=0).T
            dv = jnp.concatenate(dv, axis=0).T
            for m, r in ((0, dq), (1, dk), (2, dv)):
                self.ig[:, pl.ds(pl.multiple_of(m * D + hp * PAIR, PAIR), PAIR)] = r
            for r, x in ((QB, dq), (VB, dv)):
                self.vec[l, r:r + 1, cols] = jnp.sum(x.astype(F32), axis=0, keepdims=True)
        loop(HEADS // 2, body)
        self.point("attend")

    def low_back(self, l, out):
        self.xt[...] = self.h[l].T
        for m in range(3):
            self.emit(l, 9 + m, lambda i: dot(self.xt[i * TILE:(i + 1) * TILE], self.ig[:, m * D:(m + 1) * D]))
        self.point("qkv")

        def body(j):
            cols = tile(j)
            x = self.tmp[:, cols]
            for m in range(3):
                x = x + dot_nt(self.ig[:, m * D:(m + 1) * D], self.w4[m, cols, :])
            out[:, cols] = x.astype(BF16)
        loop(3, body)
        self.point("end")


def net_scratch():
    return dict(
        w4=pltpu.VMEM((4, D, D), BF16), we=pltpu.VMEM((D, FF), BF16), ws=pltpu.VMEM((FF, D), BF16),
        par=pltpu.VMEM((2, 16, D), F32), vec=pltpu.VMEM((2, 16, D), F32), mask=pltpu.VMEM((T, T), F32),
        h=pltpu.VMEM((2, T, D), BF16), q=pltpu.VMEM((2, T, D), BF16), k=pltpu.VMEM((2, T, D), BF16), v=pltpu.VMEM((2, T, D), BF16),
        att=pltpu.VMEM((2, T, D), BF16), n1=pltpu.VMEM((2, T, D), BF16), n2=pltpu.VMEM((2, T, D), BF16), fl=pltpu.VMEM((2, T, D), BF16),
        sc1=pltpu.VMEM((2, T, 1), F32), sc2=pltpu.VMEM((2, T, 1), F32),
        probs=pltpu.VMEM((HEADS, T, T), BF16), slope=pltpu.VMEM((T, FF), BF16), act=pltpu.VMEM((T, FF), BF16),
        tmp=pltpu.VMEM((T, D), F32), og=pltpu.VMEM((T, D), BF16), ag=pltpu.VMEM((T, D), BF16), ig=pltpu.VMEM((T, FF), BF16),
        xt=pltpu.VMEM((D, T), BF16), gin=pltpu.VMEM((T, D), BF16), stage=pltpu.VMEM((2, D, D), BF16),
    )


MESH = pl.DeviceIdType.MESH
NB = 12
BLK = 768
COL = 384
HALF = 384
CH = 96
SUB = 48
NSTAGE = 12


def when(cond, fn):
    if isinstance(cond, bool):
        if cond:
            fn()
    else:
        pl.when(cond)(fn)


def coords():
    s = lax.axis_index("section")
    b = lax.axis_index("batch")
    return s, b // 4, (b // 2) % 2, b % 2


def dev(s, z, y, x):
    return (s, z * 4 + y * 2 + x)


class Comm:
    def __init__(self, refs):
        self.__dict__.update(refs)
        s, z, y, x = coords()
        self.s, self.p = s, z
        self.core = dev(1 - s, z, y, x)
        xn, yn = dev(s, z, y, 1 - x), dev(s, z, 1 - y, x)
        self.u = (x, y)
        self.w = (y, x)
        self.n1 = (xn, yn)
        self.n3 = (yn, xn)
        self.up = dev(s, jnp.minimum(z + 1, 3), y, x)
        self.dn = dev(s, jnp.maximum(z - 1, 0), y, x)

    def barrier(self):
        s, z, y, x = coords()
        bar = pltpu.get_barrier_semaphore()
        peers = [self.core, self.n1[0], self.n1[1]] + [dev(s, lax.rem(z + k, 4), y, x) for k in (1, 2, 3)]
        for d in peers:
            pl.semaphore_signal(bar, inc=1, device_id=d, device_id_type=MESH)
        pl.semaphore_wait(bar, len(peers))

    def remote(self, src, dst, ss, rs, d):
        return pltpu.make_async_remote_copy(src_ref=src, dst_ref=dst, send_sem=ss, recv_sem=rs, device_id=d, device_id_type=MESH)

    def prt_copy(self, src, b):
        return self.remote(src, self.prt.at[b], self.prt_s.at[b], self.prt_r.at[b], self.core)

    def loads(self, st, b):
        sl = lax.rem(b, 2)
        cols = pl.ds(st * COL, COL)
        return (
            pltpu.make_async_copy(self.acc.at[b, :, cols], self.lda.at[st, sl], self.ld_sem.at[st, sl, 0]),
            pltpu.make_async_copy(self.prt.at[b, :, cols], self.ldp.at[st], self.ld_sem.at[st, sl, 1]),
        )

    def s0(self, b):
        self.prt_copy(self.prt.at[b], b).wait_recv()
        for st in (0, 1):
            for c in self.loads(st, b):
                c.start()

    def r1_copy(self, st, b):
        sl = lax.rem(b, 2)
        rows = pl.ds(pl.multiple_of((1 - self.u[st]) * HALF, HALF), HALF)
        return self.remote(self.lda.at[st, sl, rows], self.r1.at[st, sl], self.r1_s.at[st, sl], self.r1_r.at[st, sl], self.n1[st])

    def s1(self, b):
        sl = lax.rem(b, 2)
        for st in (0, 1):
            for c in self.loads(st, b):
                c.wait()
            oth = pl.ds(pl.multiple_of((1 - self.u[st]) * HALF, HALF), HALF)
            own = pl.ds(pl.multiple_of(self.u[st] * HALF, HALF), HALF)
            self.lda[st, sl, oth] += self.ldp[st, oth]
            self.r1_copy(st, b).start()
            self.lda[st, sl, own] += self.ldp[st, own]

    def zsend(self, st, b, lo, hi, up):
        zs = lax.rem(b, 4)
        if up:
            return self.remote(self.zbuf.at[st, zs, pl.ds(lo, hi - lo)], self.ru.at[st, zs, pl.ds(lo - CH, hi - lo)],
                               self.ru_s.at[st, zs], self.ru_r.at[st, zs], self.up)
        return self.remote(self.zbuf.at[st, zs, pl.ds(lo, hi - lo)], self.rd.at[st, zs, pl.ds(lo, hi - lo)],
                           self.rd_s.at[st, zs], self.rd_r.at[st, zs], self.dn)

    def zadd(self, st, b, lo, hi, up):
        zs = lax.rem(b, 4)
        self.zsend(st, b, lo, hi, up).wait_recv()
        if up:
            self.zbuf[st, zs, lo:hi] += self.ru[st, zs, lo - CH:hi - CH]
        else:
            self.zbuf[st, zs, lo:hi] += self.rd[st, zs, lo:hi]

    def s2(self, b):
        sl, zs = lax.rem(b, 2), lax.rem(b, 4)
        for st in (0, 1):
            self.r1_copy(st, b).wait()
            own = pl.ds(pl.multiple_of(self.u[st] * HALF, HALF), HALF)
            self.zbuf[st, zs] = self.lda[st, sl, own] + self.r1[st, sl]
            pl.when(self.p == 0)(lambda: self.zsend(st, b, CH, 4 * CH, True).start())
            pl.when(self.p == 3)(lambda: self.zsend(st, b, 0, 3 * CH, False).start())

    def s3(self, b):
        for st in (0, 1):
            @pl.when(self.p == 1)
            def _():
                self.zadd(st, b, CH, 4 * CH, True)
                self.zsend(st, b, 2 * CH, 4 * CH, True).start()

            @pl.when(self.p == 2)
            def _():
                self.zadd(st, b, 0, 3 * CH, False)
                self.zsend(st, b, 0, 2 * CH, False).start()

    def s4(self, b):
        for st in (0, 1):
            @pl.when(self.p == 2)
            def _():
                self.zadd(st, b, 2 * CH, 4 * CH, True)
                self.zsend(st, b, 3 * CH, 4 * CH, True).start()

            @pl.when(self.p == 1)
            def _():
                self.zadd(st, b, 0, 2 * CH, False)
                self.zsend(st, b, 0, CH, False).start()

    def r3_copy(self, st, b):
        sl, zs = lax.rem(b, 2), lax.rem(b, 4)
        rows = pl.ds(pl.multiple_of(self.p * CH + (1 - self.w[st]) * SUB, SUB), SUB)
        return self.remote(self.zbuf.at[st, zs, rows], self.r3.at[st, sl], self.r3_s.at[st, sl], self.r3_r.at[st, sl], self.n3[st])

    def s5(self, b):
        for st in (0, 1):
            pl.when(self.p == 0)(lambda: self.zadd(st, b, 0, CH, False))
            pl.when(self.p == 3)(lambda: self.zadd(st, b, 3 * CH, 4 * CH, True))
            self.r3_copy(st, b).start()

    def res_at(self, st, b, c, lo, n, u):
        rows = pl.ds(pl.multiple_of(u * HALF + c * CH + lo, SUB), n)
        return self.res.at[b, rows, pl.ds(st * COL, COL)]

    def fin_copies(self, st, b):
        sl = lax.rem(b, 2)
        there = self.res_at(st, b, self.p, self.w[st] * SUB, SUB, self.u[st])
        return (
            self.remote(self.fin.at[st, sl], there, self.ag_s.at[st, 3, 0, lax.rem(b, 4)], self.wr.at[st, b], self.n3[st]),
            pltpu.make_async_copy(self.fin.at[st, sl], there, self.ag_s.at[st, 3, 1, lax.rem(b, 4)]),
        )

    def s6(self, b):
        sl, zs = lax.rem(b, 2), lax.rem(b, 4)
        for st in (0, 1):
            self.r3_copy(st, b).wait()
            pl.when(self.p == 0)(lambda: self.zsend(st, b, CH, 4 * CH, True).wait_send())
            pl.when(self.p == 3)(lambda: self.zsend(st, b, 0, 3 * CH, False).wait_send())

            @pl.when(self.p == 1)
            def _():
                self.zsend(st, b, 2 * CH, 4 * CH, True).wait_send()
                self.zsend(st, b, 0, CH, False).wait_send()

            @pl.when(self.p == 2)
            def _():
                self.zsend(st, b, 0, 2 * CH, False).wait_send()
                self.zsend(st, b, 3 * CH, 4 * CH, True).wait_send()

            rows = pl.ds(pl.multiple_of(self.p * CH + self.w[st] * SUB, SUB), SUB)
            self.fin[st, sl] = self.zbuf[st, zs, rows] + self.r3[st, sl]
            for c in self.fin_copies(st, b):
                c.start()

    def ag_copy(self, st, b, c, d):
        here = self.res_at(st, b, c, 0, CH, self.u[st])
        to, sem = ((self.up, self.zr), (self.dn, self.zr), (self.n1[st], self.xr))[d]
        return self.remote(here, here, self.ag_s.at[st, d, c, lax.rem(b, 4)], sem.at[st, b, c], to)

    def spread(self, st, b, c, up, down):
        if up:
            pl.when(self.p < 3)(lambda: self.ag_copy(st, b, c, 0).start())
        if down:
            pl.when(self.p > 0)(lambda: self.ag_copy(st, b, c, 1).start())
        self.ag_copy(st, b, c, 2).start()

    def s7(self, b):
        for st in (0, 1):
            far, near = self.fin_copies(st, b)
            far.wait()
            near.wait()
            self.spread(st, b, self.p, True, True)

    def hop(self, k, b):
        for st in (0, 1):
            @pl.when(self.p >= k)
            def _():
                self.ag_copy(st, b, self.p - k, 0).wait_recv()
                self.spread(st, b, self.p - k, True, False)

            @pl.when(self.p <= 3 - k)
            def _():
                self.ag_copy(st, b, self.p + k, 1).wait_recv()
                self.spread(st, b, self.p + k, False, True)

    def s8(self, b):
        self.hop(1, b)

    def s9(self, b):
        self.hop(2, b)

    def s10(self, b):
        self.hop(3, b)

    def s11(self, b):
        for st in (0, 1):
            for c in range(4):
                got = self.ag_copy(st, b, c, 2)
                got.wait_send()
                got.wait_recv()
                pl.when((self.p < 3) & (self.p >= c))(lambda: self.ag_copy(st, b, c, 0).wait_send())
                pl.when((self.p > 0) & (self.p <= c))(lambda: self.ag_copy(st, b, c, 1).wait_send())

    def tick(self, t):
        stages = (self.s0, self.s1, self.s2, self.s3, self.s4, self.s5, self.s6, self.s7, self.s8, self.s9, self.s10, self.s11)
        for k in reversed(range(NSTAGE)):
            b = t - k
            when((b >= 0) & (b < NB), lambda: stages[k](b))

    def vec_copy(self, k):
        s, z, y, x = coords()
        to = (self.core, dev(s, z, y, 1 - x), dev(s, z, 1 - y, x), dev(s, z + 1 - 2 * lax.rem(z, 2), y, x), dev(s, lax.rem(z + 2, 4), y, x))[k]
        src = self.vec.at[1 - s] if k == 0 else self.vcur.at[k - 1]
        return self.remote(src, self.vrecv.at[k], self.v_s.at[k], self.v_r.at[k], to)

    def vec_step(self, k):
        self.vec_copy(k).wait()
        s = self.s
        before = self.vec[s] if k == 0 else self.vcur[k - 1]
        self.vcur[k] = before + self.vrecv[k]
        if k < 4:
            self.vec_copy(k + 1).start()


def comm_scratch():
    bf = jnp.bfloat16
    dma = pltpu.SemaphoreType.DMA
    return dict(
        lda=pltpu.VMEM((2, 2, BLK, COL), bf), ldp=pltpu.VMEM((2, BLK, COL), bf),
        r1=pltpu.VMEM((2, 2, HALF, COL), bf), zbuf=pltpu.VMEM((2, 4, HALF, COL), bf),
        ru=pltpu.VMEM((2, 4, 3 * CH, COL), bf), rd=pltpu.VMEM((2, 4, 3 * CH, COL), bf),
        r3=pltpu.VMEM((2, 2, SUB, COL), bf), fin=pltpu.VMEM((2, 2, SUB, COL), bf),
        vcur=pltpu.VMEM((5, 16, BLK), jnp.float32), vrecv=pltpu.VMEM((5, 16, BLK), jnp.float32),
        prt_s=dma((NB,)), prt_r=dma((NB,)), ld_sem=dma((2, 2, 2)), r1_s=dma((2, 2)), r1_r=dma((2, 2)),
        ru_s=dma((2, 4)), ru_r=dma((2, 4)), rd_s=dma((2, 4)), rd_r=dma((2, 4)), r3_s=dma((2, 2)), r3_r=dma((2, 2)),
        ag_s=dma((2, 4, 4, 4)), wr=dma((2, NB)), zr=dma((2, NB, 4)), xr=dma((2, NB, 4)), v_s=dma((5,)), v_r=dma((5,)),
    )


class Program(Net):
    def __init__(self, refs, chips):
        super().__init__(refs)
        self.chips = chips
        self.s = lax.axis_index("section")
        self.core = (1 - self.s, lax.axis_index("batch"))
        self.comm = Comm(refs) if chips == 16 else None
        self.emitted = 0
        self.prev = None
        self.ready = [0, 0]
        self.ticks = [0, 0]
        self.plan = {}

    def here(self, l, yes, no):
        pl.when(self.s == l)(yes)
        pl.when(self.s != l)(no)

    def remote(self, src, dst, ss, rs):
        return pltpu.make_async_remote_copy(src_ref=src, dst_ref=dst, send_sem=ss, recv_sem=rs, device_id=self.core, device_id_type=MESH)

    def barrier(self):
        if self.comm:
            self.comm.barrier()
        else:
            bar = pltpu.get_barrier_semaphore()
            pl.semaphore_signal(bar, inc=1, device_id=self.core, device_id_type=MESH)
            pl.semaphore_wait(bar, 1)

    def swap(self, m):
        return self.remote(self.own[m], self.other[m], self.wx_s.at[m], self.wx_r.at[m])

    def swap_par(self):
        return self.remote(self.par.at[self.s], self.par.at[self.s], self.wx_s.at[6], self.wx_r.at[6])

    def held(self, m):
        return self.w4.at[m] if m < 4 else (self.we, self.ws)[m - 4]

    def load(self, l, m, first=True):
        def theirs():
            if first:
                self.swap(m).wait_recv()
            pltpu.make_async_copy(self.other[m], self.held(m), self.w_sem.at[m]).start()
        self.here(l, lambda: pltpu.make_async_copy(self.own[m], self.held(m), self.w_sem.at[m]).start(), theirs)

    def wait_load(self, m):
        pltpu.make_async_copy(self.own[m], self.held(m), self.w_sem.at[m]).wait()

    def aside(self, k, out):
        a, b = (self.probs, self.slope, self.act)[k], (self.sp_probs, self.sp_slope, self.sp_act)[k]
        return pltpu.make_async_copy(*((a, b) if out else (b, a)), self.sp_sem.at[k])

    def rows_near(self, k, l, src):
        return pltpu.make_async_copy(src, self.rows_at(k), self.ro_s.at[k, l])

    def rows_far(self, k, l, src):
        return self.remote(src, self.rows_at(k), self.ro_s.at[k, l], self.ro_r.at[k])

    def rows_at(self, k):
        return (self.lo, self.gi)[k].at[pl.ds(pl.multiple_of(self.s * T, T), T)]

    def put_rows(self, k, l, src):
        self.here(l, lambda: self.rows_near(k, l, src).start(), lambda: self.rows_far(k, l, src).start())

    def wait_rows(self, k, l, src):
        self.here(l, lambda: self.rows_near(k, l, src).wait(), lambda: self.rows_far(k, l, src).wait_send())

    def out_near(self, b, slot):
        return pltpu.make_async_copy(self.stage.at[slot], self.acc.at[b], self.st_sem.at[slot])

    def out_far(self, b, slot):
        return self.remote(self.stage.at[slot], self.prt.at[b], self.st_sem.at[slot], self.prt_r.at[b])

    def emit_out(self, l, b, slot):
        self.here(l, lambda: self.out_near(b, slot).start(), lambda: self.out_far(b, slot).start())
        self.flush()
        self.prev = (l, b, slot)

    def flush(self):
        if self.prev is not None:
            l, b, slot = self.prev
            self.here(l, lambda: self.out_near(b, slot).wait(), lambda: self.out_far(b, slot).wait_send())
            self.ready[l] = b + 1
            self.prev = None

    def point(self, name):
        if self.comm is None:
            return
        for l, n in self.plan.get((self.layer, name), ()):
            for _ in range(n):
                t = self.ticks[l]
                if t < NB and t >= self.ready[l]:
                    break
                pl.when(self.s == l)(functools.partial(self.comm.tick, t))
                self.ticks[l] = t + 1

    def forward(self, l, low):
        self.layer = l
        for m in range(3):
            self.wait_load(m)
        self.qkv(l)
        if l == 0:
            self.load(0, 3)
        else:
            self.aside(0, True).wait()
        self.attend(l)
        if l == 0:
            self.aside(0, True).start()
            self.load(0, 4)
        self.wait_load(3)
        self.mix(l)
        if l == 0:
            self.load(0, 5)
        else:
            self.aside(1, True).wait()
            self.aside(2, True).wait()
        self.wait_load(4)
        self.expand(l)
        if l == 0:
            for m in range(5):
                self.load(1, m)
            self.aside(1, True).start()
            self.aside(2, True).start()
        self.wait_load(5)
        self.shrink(l, low)
        if l == 0:
            self.load(1, 5)

    def backward(self, l):
        self.layer = l
        again = l == 1
        if not again:
            self.aside(2, False).wait()
        self.top_back(l, lambda rows: self.gin[rows].astype(F32))
        if again:
            self.aside(2, False).start()
        else:
            self.aside(1, False).wait()
            self.wait_load(5)
        self.inner_back(l, lambda: again and (self.load(0, 5, False), self.aside(1, False).start()), lambda: again or self.wait_load(4))
        if again:
            self.load(0, 4, False)
            self.wait_rows(0, 1, self.ag)
        else:
            self.wait_load(3)
        self.mid_back(l)
        if again:
            self.load(0, 3, False)
        else:
            self.aside(0, False).wait()
        self.attend_back(l)
        if again:
            self.aside(0, False).start()
        else:
            for m in range(3):
                self.wait_load(m)
            self.wait_rows(1, 1, self.gin)
        self.low_back(l, self.gin)
        if again:
            for m in range(3):
                self.load(0, m, False)
        self.put_rows(1, l, self.gin)

    def run(self):
        s = self.s
        self.barrier()
        for m in range(3):
            self.swap(m).start()
        for r, ref in enumerate(self.small[:8]):
            self.par[s, r:r + 1, :] = ref[...]
        for j in range(4):
            self.par[s, EB + j:EB + j + 1, :] = self.small[8][:, j * D:(j + 1) * D]
        self.swap_par().start()
        for m in range(3, 6):
            self.swap(m).start()
        rows = pl.ds(pl.multiple_of(s * T, T), T)
        first = (pltpu.make_async_copy(self.tokens.at[rows], self.h.at[0], self.in_sem.at[0]),
                 pltpu.make_async_copy(self.cotangent.at[rows], self.gin, self.in_sem.at[1]))
        for c in first:
            c.start()
        self.vec[...] = jnp.zeros_like(self.vec)
        self.labels(self.ids[pl.ds(s, 1), :])
        for m in range(3):
            self.load(0, m)
        for c in first:
            c.wait()
        self.swap_par().wait()
        self.forward(0, self.h.at[1])
        self.put_rows(0, 0, self.h.at[1])
        self.forward(1, self.ag)
        self.put_rows(0, 1, self.ag)
        self.backward(1)
        self.flush()
        self.point("flush")
        self.backward(0)
        self.flush()
        if self.comm:
            self.comm.vec_copy(0).start()

            def step(t, c):
                self.comm.tick(t)
                for k in range(5):
                    pl.when(t == NB + NSTAGE - 7 + k)(functools.partial(self.comm.vec_step, k))
                return c
            lax.fori_loop(jnp.where(s == 1, self.ticks[1], self.ticks[0]), NB + NSTAGE - 1, step, 0)
            self.vec_out[...] = self.comm.vcur[4]
        else:
            for b in range(NB):
                self.out_far(b, 0).wait_recv()
            self.vec_out[...] = self.vec[...]
        for m in range(6):
            self.swap(m).wait_send()
        self.wait_rows(0, 0, self.h.at[1])
        self.wait_rows(1, 0, self.gin)
        for k in (0, 1):
            self.rows_far(k, 0, self.gin).wait_recv()


def kernel(chips, names, plan, *refs):
    tokens, cotangent, ids = refs[0:3]
    weights = refs[3:9]
    small = refs[9:18]
    lo, gi, res, vec_out, acc, prt, o4, oe, os_, sp_probs, sp_slope, sp_act = refs[18:30]
    named = dict(zip(names, refs[30:]))
    named.update(tokens=tokens, cotangent=cotangent, ids=ids, own=[w.at[0] for w in weights], small=small, lo=lo, gi=gi, res=res,
                 vec_out=vec_out, acc=acc, prt=prt, other=[o4.at[0], o4.at[1], o4.at[2], o4.at[3], oe, os_],
                 sp_probs=sp_probs, sp_slope=sp_slope, sp_act=sp_act)
    p = Program(named, chips)
    p.plan = plan
    p.run()


PLAN = {
    (1, "shrink"): ((1, 1),), (1, "inner"): ((1, 1),), (1, "expand"): ((1, 1),), (1, "first"): ((1, 1),),
    (1, "mixer"): ((1, 1),), (1, "attend"): ((1, 1),), (1, "end"): ((1, 1),),
    (0, "shrink"): ((1, 1), (0, 1)), (0, "inner"): ((1, 1), (0, 1)), (0, "expand"): ((1, 1), (0, 1)), (0, "first"): ((1, 1), (0, 1)),
    (0, "mixer"): ((1, 1), (0, 1)), (0, "attend"): ((1, 1), (0, 1)), (0, "end"): ((1, 1), (0, 1)),
}


def both_layers(chips, tokens, cotangent, ids, weights, small):
    S = jax.ShapeDtypeStruct
    dma = pltpu.SemaphoreType.DMA
    sc = net_scratch()
    sc.update(comm_scratch())
    sc.update(wx_s=dma((7,)), wx_r=dma((7,)), w_sem=dma((6,)), sp_sem=dma((3,)), ro_s=dma((2, 2)), ro_r=dma((2,)), st_sem=dma((2,)),
              in_sem=dma((2,)))
    hbm, vm = pl.BlockSpec(memory_space=pl.ANY), pl.BlockSpec(memory_space=pltpu.VMEM)
    rows, blocks = S((2 * T, D), BF16), S((NB, D, D), BF16)
    out = pl.pallas_call(
        functools.partial(kernel, chips, tuple(sc), PLAN),
        out_shape=(rows, rows, blocks, S((16, D) if chips == 16 else (2, 16, D), F32), blocks, blocks, S((4, D, D), BF16), S((D, FF), BF16),
                   S((FF, D), BF16), S((HEADS, T, T), BF16), S((T, FF), BF16), S((T, FF), BF16)),
        in_specs=[hbm, hbm, vm] + [hbm] * 6 + [vm] * 9,
        out_specs=(hbm, hbm, hbm, vm) + (hbm,) * 8,
        scratch_shapes=list(sc.values()),
        compiler_params=pltpu.CompilerParams(collective_id=0, has_side_effects=True, vmem_limit_bytes=64 * 2**20 - 2**17),
    )(tokens, cotangent, ids, *weights, *small)
    return out[:6]


WROWS, WBUFS = 384, 4


def widen_kernel(res, vec, sh, ex, mi, q, k, v, *rest):
    small, (low, wide, in_sem, out_sem) = rest[:9], rest[9:]
    per = D // WROWS
    count = NB * per

    def take(i):
        rows = pl.ds((i % per) * WROWS, WROWS)
        return pltpu.make_async_copy(res.at[i // per, rows], low.at[i % WBUFS], in_sem.at[i % WBUFS])

    def put(i):
        b, r = i // per, (i % per) * WROWS
        if b < 4:
            to = sh.at[0, pl.ds(b * D + r, WROWS)]
        elif b < 8:
            to = ex.at[0, pl.ds(r, WROWS), pl.ds((b - 4) * D, D)]
        else:
            to = (mi, q, k, v)[b - 8].at[0, pl.ds(r, WROWS)]
        return pltpu.make_async_copy(wide.at[i % WBUFS], to, out_sem.at[i % WBUFS])

    for i in range(WBUFS):
        take(i).start()
    for r in range(8):
        small[r][...] = vec[r:r + 1, :]
    for j in range(4):
        small[8][:, j * D:(j + 1) * D] = vec[EB + j:EB + j + 1, :]
    for i in range(count):
        take(i).wait()
        if i >= WBUFS:
            put(i - WBUFS).wait()

        def convert(j, c):
            rows = tile(j, 32)
            wide[i % WBUFS, rows] = low[i % WBUFS, rows].astype(F32)
            return c
        lax.fori_loop(0, WROWS // 32, convert, 0, unroll=4)
        put(i).start()
        if i + WBUFS < count:
            take(i + WBUFS).start()
    for i in range(count - WBUFS, count):
        put(i).wait()


def widen(res, vec):
    S = jax.ShapeDtypeStruct
    hbm, vm = pl.BlockSpec(memory_space=pl.ANY), pl.BlockSpec(memory_space=pltpu.VMEM)
    square, row = S((1, D, D), F32), S((1, D), F32)
    return pl.pallas_call(
        widen_kernel,
        out_shape=(S((1, FF, D), F32), S((1, D, FF), F32), square, square, square, square) + (row,) * 8 + (S((1, FF), F32),),
        in_specs=[hbm, vm], out_specs=(hbm,) * 6 + (vm,) * 9,
        scratch_shapes=[pltpu.VMEM((WBUFS, WROWS, D), BF16), pltpu.VMEM((WBUFS, WROWS, D), F32),
                        pltpu.SemaphoreType.DMA((WBUFS,)), pltpu.SemaphoreType.DMA((WBUFS,))],
        compiler_params=pltpu.CompilerParams(vmem_limit_bytes=32 * 2**20),
    )(res, vec)


def body(tokens, cotangent, sentence_ids, *stored):
    (query_w, query_b, keys_w, value_w, value_b, mixer_w, mixer_b, gain_one, shift_one, expand_w, expand_b, shrink_w, shrink_b, gain_two,
     shift_two) = stored
    chips = lax.axis_size("batch")
    lo, gi, res, vec, acc, prt = both_layers(
        chips, tokens, cotangent, sentence_ids.reshape(2, T), (query_w, keys_w, value_w, mixer_w, expand_w, shrink_w),
        (query_b, value_b, mixer_b, gain_one, shift_one, shrink_b, gain_two, shift_two, expand_b))
    if chips != 16:
        vec = lax.psum(lax.dynamic_index_in_dim(lax.psum(vec, "section"), lax.axis_index("section"), 0, keepdims=False), "batch")
        res = lax.psum(acc.astype(F32) + prt.astype(F32), "batch").astype(BF16)
    sh, ex, mi, q, k, v, qb, vb, mb, g1, s1, sb, g2, s2, eb = widen(res, vec)
    return (lo[None], gi[None], q, qb, k, v, vb, mi, mb, g1, s1, ex, eb, sh, sb, g2, s2)


def solution(mesh):
    placed = (
        P("batch", None),
        P("batch", None),
        P("batch"),
        P("section", None, None),
        P("section", None),
        P("section", None, None),
        P("section", None, None),
        P("section", None),
        P("section", None, None),
        P("section", None),
        P("section", None),
        P("section", None),
        P("section", None, None),
        P("section", None),
        P("section", None, None),
        P("section", None),
        P("section", None),
        P("section", None),
    )
    return jax.shard_map(
        body,
        mesh=mesh,
        in_specs=placed,
        out_specs=(
            P("section", "batch", None),
            P("section", "batch", None),
            P("section", None, None),
            P("section", None),
            P("section", None, None),
            P("section", None, None),
            P("section", None),
            P("section", None, None),
            P("section", None),
            P("section", None),
            P("section", None),
            P("section", None, None),
            P("section", None),
            P("section", None, None),
            P("section", None),
            P("section", None),
            P("section", None),
        ),
        check_vma=False,
    )
```

```python
import functools

import jax
import jax.numpy as jnp
from jax import lax
from jax.experimental import pallas as pl
from jax.experimental.pallas import tpu as pltpu
from jax.sharding import PartitionSpec as P

T = 512
D = 768
FF = 3072
HEADS = 12
TILE = 256
PAIR = 128
EPS = 1e-06
SLOTS = 3
F32, BF16 = jnp.float32, jnp.bfloat16
QB, VB, MB, G1, S1, SB, G2, S2, EB = 0, 1, 2, 3, 4, 5, 6, 7, 8


def dot(a, b):
    return jnp.dot(a, b, preferred_element_type=F32)


def dot_nt(a, b):
    return lax.dot_general(a, b, (((1,), (1,)), ((), ())), preferred_element_type=F32)


def tile(j, n=TILE):
    return pl.ds(pl.multiple_of(j * n, n), n)


def loop(n, fn, unroll=1):
    def step(i, c):
        fn(i)
        return c
    lax.fori_loop(0, n, step, 0, unroll=unroll)


def gelu_parts(u):
    x = u * 0.7071067811865476
    cdf = 0.5 + 0.5 * lax.erf(x)
    return u * cdf, cdf + u * (0.3989422804014327 * jnp.exp2(x * (x * -1.4426950408889634)))


def fold(x):
    return jnp.sum(x.reshape(x.shape[0] // 8, 8, x.shape[1]), axis=0)


class Net:
    def __init__(self, refs):
        self.__dict__.update(refs)

    def row(self, l, r, cols=slice(None)):
        return self.par[l, r:r + 1, cols]

    def load(self, l, m):
        raise NotImplementedError

    def wait_load(self, l, m):
        raise NotImplementedError

    def point(self, name):
        pass

    def labels(self, ids):
        for a in range(4):
            self.mask[a:a + 1, :] = jnp.where(ids == ids[:, a * PAIR:a * PAIR + 1], 0.0, -1e9)

    def qkv(self, l, ready):
        for m, out, b in ((0, self.q, QB), (1, self.k, None), (2, self.v, VB)):
            ready(m)

            def body(j):
                cols = tile(j)
                r = dot(self.h[l], self.w4[m, :, cols])
                if b is not None:
                    r = r + self.par[l, b:b + 1, cols]
                r = r.astype(BF16)
                out[:, cols] = r * BF16(0.125) if m == 0 else r
            loop(3, body)

    def attend(self, l):
        lane = lax.broadcasted_iota(jnp.int32, (1, PAIR), 1)
        R = 256

        def body(hp):
            cols = tile(hp, PAIR)
            k2, v2 = self.k[:, cols], self.v[:, cols]
            kk = jnp.concatenate([jnp.where(lane < 64, k2, BF16(0)), jnp.where(lane >= 64, k2, BF16(0))], axis=0)
            for r in range(T // R):
                rows = pl.ds(r * R, R)
                both = dot_nt(self.q[rows, cols], kk)
                out = []
                for e in (0, 1):
                    s = both[:, e * T:(e + 1) * T].reshape(R // PAIR, PAIR, T)
                    s = (s + self.mask[r * R // PAIR:(r + 1) * R // PAIR, :][:, None, :]).reshape(R, T)
                    x = jnp.exp(s - jnp.max(s, axis=1, keepdims=True)).astype(BF16)
                    self.probs[2 * hp + e, rows] = x
                    out.append(dot(x, jnp.where(lane < 64 if e == 0 else lane >= 64, v2, BF16(1))))
                total = pltpu.roll(jnp.where(lane < 64, out[1], out[0]), 64, 1)
                self.att[l, rows, cols] = (jnp.where(lane < 64, out[0], out[1]) / total).astype(BF16)
        loop(HEADS // 2, body, 2)

    def norm(self, l, n_ref, k, g, b, low):
        def body(i):
            rows = tile(i, 128)
            x = self.tmp[rows]
            c = x - jnp.mean(x, axis=1, keepdims=True)
            inv = lax.rsqrt(jnp.mean(c * c, axis=1, keepdims=True) + EPS)
            n = c * inv
            n_ref[l, rows] = n.astype(n_ref.dtype)
            self.sc[rows, 2 * l + k:2 * l + k + 1] = inv
            y = n * self.row(l, g) + self.row(l, b)
            self.tmp[rows] = y
            low[rows] = y.astype(BF16)
        loop(T // 128, body, 2)

    def mix(self, l):
        def body(j):
            cols = tile(j)
            self.tmp[:, cols] = dot(self.att[l], self.w4[3, :, cols]) + self.par[l, MB:MB + 1, cols] + self.h[l, :, cols].astype(F32)
        loop(3, body)
        self.norm(l, self.n1, 0, G1, S1, self.fl.at[l])

    def expand(self, l):
        def body(j):
            for i in range(3):
                cols = pl.ds(pl.multiple_of(j * D + i * TILE, TILE), TILE)
                u = dot(self.fl[l], self.we[:, cols]) + self.par[l, pl.ds(EB + j, 1), i * TILE:(i + 1) * TILE]
                a, s = gelu_parts(u)
                self.act[:, cols] = a.astype(BF16)
                self.slope[:, cols] = s.astype(BF16)
        loop(4, body)

    def shrink(self, l, low):
        def body(j):
            cols = tile(j)
            self.tmp[:, cols] += dot(self.act[...], self.ws[:, cols]) + self.par[l, SB:SB + 1, cols]
        loop(3, body)
        self.norm(l, self.n2, 1, G2, S2, low)

    def norm_back(self, l, src, n_ref, k, g, b, low, low_row):
        def body(i, c):
            rows = tile(i, 128)
            dy = src(rows)
            n = n_ref[l, rows].astype(F32)
            gr = dy * self.row(l, g)
            m1 = jnp.mean(gr, axis=1, keepdims=True)
            m2 = jnp.mean(gr * n, axis=1, keepdims=True)
            dx = self.sc[rows, 2 * l + k:2 * l + k + 1] * (gr - m1 - n * m2)
            self.tmp[rows] = dx
            lw = dx.astype(BF16)
            low[rows] = lw
            return (c[0] + fold(dy * n), c[1] + fold(dy), c[2] + fold(lw.astype(F32)))
        z = jnp.zeros((8, D), F32)
        a, s, t = lax.fori_loop(0, T // 128, body, (z, z, z), unroll=2)
        for r, x in ((g, a), (b, s), (low_row, t)):
            self.vec[l, r:r + 1, :] = jnp.sum(x, axis=0, keepdims=True)

    def emit(self, l, b, rows_of):
        slot = self.free_slot()
        for i in range(3):
            self.stage[slot, i * TILE:(i + 1) * TILE] = rows_of(i).astype(BF16)
        self.emit_out(l, b, slot)
        self.point("e%d" % b)

    def top_back(self, l, src):
        self.norm_back(l, src, self.n2, 1, G2, S2, self.og, SB)
        self.point("norm2")
        for b in range(4):
            self.emit(l, b, lambda i: dot(self.act[:, b * D + i * TILE:b * D + (i + 1) * TILE].T, self.og[...]))
        self.point("shrink")

    def inner_back(self, l, done_inner, need_expand):
        def body(j):
            for i in range(3):
                cols = pl.ds(pl.multiple_of(j * D + i * TILE, TILE), TILE)
                g = (dot_nt(self.og[...], self.ws[cols, :]) * self.slope[:, cols].astype(F32)).astype(BF16)
                self.ig[:, cols] = g
                self.vec[l, pl.ds(EB + j, 1), i * TILE:(i + 1) * TILE] = jnp.sum(g.astype(F32), axis=0, keepdims=True)
        loop(4, body)
        done_inner()
        self.point("inner")
        self.xt[...] = self.fl[l].T
        for b in range(4):
            self.emit(l, 4 + b, lambda i: dot(self.xt[i * TILE:(i + 1) * TILE], self.ig[:, b * D:(b + 1) * D]))
        self.point("expand")
        need_expand()

        def back(j):
            cols = tile(j)
            self.tmp[:, cols] += dot_nt(self.ig[...], self.we[cols, :])
        loop(3, back)
        self.point("first")

    def mid_back(self, l):
        self.norm_back(l, lambda rows: self.tmp[rows], self.n1, 0, G1, S1, self.og, MB)
        self.emit(l, 8, lambda i: dot(self.att[l, :, i * TILE:(i + 1) * TILE].T, self.og[...]))

        def body(j):
            cols = tile(j)
            self.ag[:, cols] = dot_nt(self.og[...], self.w4[3, cols, :]).astype(BF16)
        loop(3, body)
        self.point("mixer")

    def attend_back(self, l):
        lane = lax.broadcasted_iota(jnp.int32, (1, PAIR), 1)

        def body(hp):
            cols = tile(hp, PAIR)
            q2, k2, v2 = self.q[:, cols], self.k[:, cols], self.v[:, cols]
            da = self.ag[:, cols]
            vv = jnp.concatenate([jnp.where(lane < 64, v2, BF16(0)), jnp.where(lane >= 64, v2, BF16(0))], axis=0)
            both = dot_nt(da, vv)
            ds, inv = [], []
            for e in (0, 1):
                x = self.probs[2 * hp + e].astype(F32)
                t = x * both[:, e * T:(e + 1) * T]
                i = 1.0 / jnp.sum(x, axis=1, keepdims=True)
                ds.append((t - x * (jnp.sum(t, axis=1, keepdims=True) * i)).astype(BF16))
                inv.append(i)
            inv = jnp.where(lane < 64, inv[0], inv[1])
            qt = (q2.astype(F32) * inv).astype(BF16).T
            dat = (da.astype(F32) * inv).astype(BF16).T
            dq = dot(ds[0], jnp.where(lane < 64, k2, BF16(0))) + dot(ds[1], jnp.where(lane >= 64, k2, BF16(0)))
            dq = (dq * (inv * 0.125)).astype(BF16)
            dk = jnp.concatenate([dot(qt[64 * e:64 * e + 64], ds[e]) for e in (0, 1)], axis=0).astype(BF16).T
            dv = jnp.concatenate([dot(dat[64 * e:64 * e + 64], self.probs[2 * hp + e]) for e in (0, 1)], axis=0).astype(BF16).T
            for m, r in ((0, dq), (1, dk), (2, dv)):
                self.ig[:, pl.ds(pl.multiple_of(m * D + hp * PAIR, PAIR), PAIR)] = r
            for r, x in ((QB, dq), (VB, dv)):
                self.vec[l, r:r + 1, cols] = jnp.sum(x.astype(F32), axis=0, keepdims=True)
        loop(3, body)
        self.point("heads")
        loop(3, lambda i: body(i + 3))
        self.point("attend")

    def low_back(self, l, out):
        self.xt[...] = self.h[l].T
        for m in range(3):
            self.emit(l, 9 + m, lambda i: dot(self.xt[i * TILE:(i + 1) * TILE], self.ig[:, m * D:(m + 1) * D]))
        self.point("qkv")

        def body(j):
            cols = tile(j)
            x = self.tmp[:, cols]
            for m in range(3):
                x = x + dot_nt(self.ig[:, m * D:(m + 1) * D], self.w4[m, cols, :])
            out[:, cols] = x.astype(BF16)
        loop(3, body)
        self.point("end")


def net_scratch():
    return dict(
        w4=pltpu.VMEM((4, D, D), BF16), we=pltpu.VMEM((D, FF), BF16), ws=pltpu.VMEM((FF, D), BF16),
        par=pltpu.VMEM((2, 16, D), F32), vec=pltpu.VMEM((2, 16, D), F32), mask=pltpu.VMEM((8, T), F32),
        h=pltpu.VMEM((2, T, D), BF16), q=pltpu.VMEM((T, D), BF16), k=pltpu.VMEM((T, D), BF16), v=pltpu.VMEM((T, D), BF16),
        att=pltpu.VMEM((2, T, D), BF16), n1=pltpu.VMEM((2, T, D), BF16), n2=pltpu.VMEM((2, T, D), BF16), fl=pltpu.VMEM((2, T, D), BF16),
        sc=pltpu.VMEM((T, 4), F32),
        probs=pltpu.VMEM((HEADS, T, T), BF16), slope=pltpu.VMEM((T, FF), BF16), act=pltpu.VMEM((T, FF), BF16),
        tmp=pltpu.VMEM((T, D), F32), og=pltpu.VMEM((T, D), BF16), ag=pltpu.VMEM((T, D), BF16), ig=pltpu.VMEM((T, FF), BF16),
        xt=pltpu.VMEM((D, T), BF16), gin=pltpu.VMEM((T, D), BF16), stage=pltpu.VMEM((SLOTS, D, D), BF16),
    )


MESH = pl.DeviceIdType.MESH
NB = 12
LEG = NB
NP = 2 * LEG
BLK = 768
PART = 384
COL = 384
HALF = 192
CH = 48
XS, RS, ZS, FS = 3, 4, 6, 6


def when(cond, fn):
    if isinstance(cond, bool):
        if cond:
            fn()
    else:
        pl.when(cond)(fn)


def coords():
    s = lax.axis_index("section")
    b = lax.axis_index("batch")
    return s, b // 4, (b // 2) % 2, b % 2


def dev(s, z, y, x):
    return (s, z * 4 + y * 2 + x)


def pair_place(l, b):
    return (1 - l) * (NB // 2) + b // 2


class Comm:
    def __init__(self, refs):
        self.__dict__.update(refs)
        s, z, y, x = coords()
        self.s, self.p = s, z
        self.core = dev(1 - s, z, y, x)
        xn, yn = dev(s, z, y, 1 - x), dev(s, z, 1 - y, x)
        self.u = (x, y)
        self.w = (y, x)
        self.n1 = (xn, yn)
        self.n3 = (yn, xn)
        self.up = dev(s, jnp.minimum(z + 1, 3), y, x)
        self.dn = dev(s, jnp.maximum(z - 1, 0), y, x)

    def barrier(self):
        bar = pltpu.get_barrier_semaphore()
        for d in (self.core, self.n1[0], self.n1[1]):
            pl.semaphore_signal(bar, inc=1, device_id=d, device_id_type=MESH)

        @pl.when(self.p < 3)
        def _():
            pl.semaphore_signal(bar, inc=1, device_id=self.up, device_id_type=MESH)

        @pl.when(self.p > 0)
        def _():
            pl.semaphore_signal(bar, inc=1, device_id=self.dn, device_id_type=MESH)
        pl.semaphore_wait(bar, 4 + self.p * (3 - self.p) // 2)

    def slot_of(self, b):
        l = 1 - b // LEG
        mine = l * self.s + (1 - l) * (1 - self.s)
        pair = lax.rem(b, LEG) // 2
        return mine * (2 * pair + self.s) + (1 - mine) * (NB + pair)

    def remote(self, src, dst, ss, rs, d):
        return pltpu.make_async_remote_copy(src_ref=src, dst_ref=dst, send_sem=ss, recv_sem=rs, device_id=d, device_id_type=MESH)

    def prt_copy(self, src, i):
        return self.remote(src, self.prt.at[i], self.prt_s.at[i], self.prt_r.at[i], self.core)

    def loads(self, st, b):
        rows, cols = pl.ds(pl.multiple_of(lax.rem(b, 2) * PART, PART), PART), pl.ds(st * COL, COL)
        return (
            pltpu.make_async_copy(self.acc.at[b // 2, rows, cols], self.lda.at[st], self.ld_sem.at[st, 0]),
            pltpu.make_async_copy(self.prt.at[b // 2, rows, cols], self.ldp.at[st], self.ld_sem.at[st, 1]),
        )

    def s0(self, b):
        when(lax.rem(b, 2) == 0 if not isinstance(b, int) else b % 2 == 0, lambda: self.prt_copy(self.prt.at[b // 2], b // 2).wait_recv())
        for st in (0, 1):
            for c in self.loads(st, b):
                c.start()

    def r1_copy(self, st, b):
        sl = lax.rem(b, RS)
        return self.remote(self.x1.at[st, lax.rem(b, XS)], self.r1.at[st, sl], self.r1_s.at[st, sl], self.r1_r.at[st, sl], self.n1[st])

    def s1(self, b):
        for st in (0, 1):
            for c in self.loads(st, b):
                c.wait()
            oth = pl.ds(pl.multiple_of((1 - self.u[st]) * HALF, HALF), HALF)
            own = pl.ds(pl.multiple_of(self.u[st] * HALF, HALF), HALF)
            self.x1[st, lax.rem(b, XS)] = self.lda[st, oth] + self.ldp[st, oth]
            self.r1_copy(st, b).start()
            self.zbuf[st, lax.rem(b, ZS)] = self.lda[st, own] + self.ldp[st, own]

    def zsend(self, st, b, lo, hi, up):
        zs, zb = lax.rem(b, 4), lax.rem(b, ZS)
        if up:
            return self.remote(self.zbuf.at[st, zb, pl.ds(lo, hi - lo)], self.ru.at[st, lax.rem(b, 3), pl.ds(lo - CH, hi - lo)],
                               self.ru_s.at[st, zs], self.ru_r.at[st, zs], self.up)
        return self.remote(self.zbuf.at[st, zb, pl.ds(lo, hi - lo)], self.rd.at[st, lax.rem(b, 3), pl.ds(lo, hi - lo)],
                           self.rd_s.at[st, zs], self.rd_r.at[st, zs], self.dn)

    def zadd(self, st, b, lo, hi, up):
        zs = lax.rem(b, ZS)
        self.zsend(st, b, lo, hi, up).wait_recv()
        if up:
            self.zbuf[st, zs, lo:hi] += self.ru[st, lax.rem(b, 3), lo - CH:hi - CH]
        else:
            self.zbuf[st, zs, lo:hi] += self.rd[st, lax.rem(b, 3), lo:hi]

    def s2(self, b):
        for st in (0, 1):
            self.r1_copy(st, b).wait()
            self.zbuf[st, lax.rem(b, ZS)] += self.r1[st, lax.rem(b, RS)]
            pl.when(self.p == 0)(lambda: self.zsend(st, b, CH, 4 * CH, True).start())
            pl.when(self.p == 3)(lambda: self.zsend(st, b, 0, 3 * CH, False).start())

    def s3(self, b):
        for st in (0, 1):
            @pl.when(self.p == 1)
            def _():
                self.zadd(st, b, CH, 4 * CH, True)
                self.zsend(st, b, 2 * CH, 4 * CH, True).start()

            @pl.when(self.p == 2)
            def _():
                self.zadd(st, b, 0, 3 * CH, False)
                self.zsend(st, b, 0, 2 * CH, False).start()

    def s4(self, b):
        for st in (0, 1):
            @pl.when(self.p == 2)
            def _():
                self.zadd(st, b, 2 * CH, 4 * CH, True)
                self.zsend(st, b, 3 * CH, 4 * CH, True).start()

            @pl.when(self.p == 1)
            def _():
                self.zadd(st, b, 0, 2 * CH, False)
                self.zsend(st, b, 0, CH, False).start()

    def r3_copy(self, st, b):
        sl = lax.rem(b, 2)
        rows = pl.ds(pl.multiple_of(self.p * CH, CH), CH)
        return self.remote(self.zbuf.at[st, lax.rem(b, ZS), rows], self.r3.at[st, sl], self.r3_s.at[st, sl], self.r3_r.at[st, sl], self.n3[st])

    def s5(self, b):
        for st in (0, 1):
            pl.when(self.p == 0)(lambda: self.zadd(st, b, 0, CH, False))
            pl.when(self.p == 3)(lambda: self.zadd(st, b, 3 * CH, 4 * CH, True))
            self.r3_copy(st, b).start()

    def res_at(self, st, b, c):
        rows = pl.ds(pl.multiple_of(lax.rem(b, 2) * PART + self.u[st] * HALF + c * CH, CH), CH)
        return self.pool.at[self.slot_of(b), rows, pl.ds(st * COL, COL)]

    def ag_copy(self, st, b, c, d, src=None):
        here = self.res_at(st, b, c)
        to, sem = ((self.up, self.zr), (self.dn, self.zr), (self.n1[st], self.xr))[d]
        return self.remote(here if src is None else src, here, self.ag_s.at[st, d, c, lax.rem(b, 4)], sem.at[st, b, c], to)

    def own_copy(self, st, b):
        return pltpu.make_async_copy(self.fin.at[st, lax.rem(b, FS)], self.res_at(st, b, self.p), self.fin_s.at[st, lax.rem(b, 4)])

    def spread(self, st, b, c, up, down, src=None):
        if up:
            pl.when(self.p < 3)(lambda: self.ag_copy(st, b, c, 0, src).start())
        if down:
            pl.when(self.p > 0)(lambda: self.ag_copy(st, b, c, 1, src).start())
        self.ag_copy(st, b, c, 2, src).start()

    def s6(self, b):
        for st in (0, 1):
            self.r3_copy(st, b).wait()
            rows = pl.ds(pl.multiple_of(self.p * CH, CH), CH)
            fin = self.fin.at[st, lax.rem(b, FS)]
            fin[...] = self.zbuf[st, lax.rem(b, ZS), rows] + self.r3[st, lax.rem(b, 2)]
            self.spread(st, b, self.p, True, True, fin)
            self.own_copy(st, b).start()
            pl.when(self.p == 0)(lambda: self.zsend(st, b, CH, 4 * CH, True).wait_send())
            pl.when(self.p == 3)(lambda: self.zsend(st, b, 0, 3 * CH, False).wait_send())

            @pl.when(self.p == 1)
            def _():
                self.zsend(st, b, 2 * CH, 4 * CH, True).wait_send()
                self.zsend(st, b, 0, CH, False).wait_send()

            @pl.when(self.p == 2)
            def _():
                self.zsend(st, b, 0, 2 * CH, False).wait_send()
                self.zsend(st, b, 3 * CH, 4 * CH, True).wait_send()

    def hop(self, k, b):
        for st in (0, 1):
            @pl.when(self.p >= k)
            def _():
                self.ag_copy(st, b, self.p - k, 0).wait_recv()
                self.spread(st, b, self.p - k, True, False)

            @pl.when(self.p <= 3 - k)
            def _():
                self.ag_copy(st, b, self.p + k, 1).wait_recv()
                self.spread(st, b, self.p + k, False, True)

    def s7(self, b):
        self.hop(1, b)

    def s8(self, b):
        self.hop(2, b)

    def s9(self, b):
        self.hop(3, b)

    def s10(self, b):
        for st in (0, 1):
            self.own_copy(st, b).wait()
            for c in range(4):
                got = self.ag_copy(st, b, c, 2)
                got.wait_send()
                got.wait_recv()
                pl.when((self.p < 3) & (self.p >= c))(lambda: self.ag_copy(st, b, c, 0).wait_send())
                pl.when((self.p > 0) & (self.p <= c))(lambda: self.ag_copy(st, b, c, 1).wait_send())
        pair = lax.rem(b, LEG) // 2
        pl.when((1 - b // LEG != self.s) & (lax.rem(b, 2) == 1))(lambda: self.home(pair).start())

    stages = ("s0", "s1", None, "s2", "s3", "s4", "s5", "s6", "s7", "s8", "s9", "s10")

    def home(self, pair):
        return self.remote(self.pool.at[NB + pair], self.pool.at[2 * pair + self.s], self.h_s.at[pair], self.h_r.at[pair], self.core)

    def finish(self):
        for pair in range(NB // 2):
            self.home(pair).wait()

    def tick(self, t):
        for k in reversed(range(len(self.stages))):
            b = t - k
            if self.stages[k]:
                when(0 <= b < NP if isinstance(b, int) else (b >= 0) & (b < NP), lambda: getattr(self, self.stages[k])(b))

    def vec_copy(self, k):
        s, z, y, x = coords()
        odd = lax.rem(z, 2)
        to = (self.core, dev(s, z, y, 1 - x), dev(s, z, 1 - y, x), dev(s, z + 1 - 2 * odd, y, x), dev(s, jnp.clip(3 - z, 1, 2), y, x),
              dev(s, jnp.where(z == 1, 0, 3), y, x))[k]
        src = self.vec.at[1 - s] if k == 0 else self.vcur.at[(k - 1) % 2]
        return self.remote(src, self.vrecv.at[k], self.v_s.at[k], self.v_r.at[k], to)

    def vec_step(self, k):
        inner = (self.p == 1) | (self.p == 2)
        if k < 4:
            self.vec_copy(k).wait()
            before = self.vec[self.s] if k == 0 else self.vcur[(k - 1) % 2]
            self.vcur[k % 2] = before + self.vrecv[k]
            if k < 3:
                self.vec_copy(k + 1).start()
            else:
                pl.when(inner)(lambda: self.vec_copy(4).start())
        elif k == 4:
            @pl.when(inner)
            def _():
                self.vec_copy(4).wait()
                self.vcur[0] = self.vcur[1] + self.vrecv[4]
                self.vec_copy(5).start()
        else:
            pl.when(inner)(lambda: self.vec_copy(5).wait_send())

            @pl.when((self.p == 0) | (self.p == 3))
            def _():
                self.vec_copy(5).wait_recv()
                self.vcur[0] = self.vrecv[5]


def comm_scratch():
    bf = jnp.bfloat16
    dma = pltpu.SemaphoreType.DMA
    return dict(
        lda=pltpu.VMEM((2, PART, COL), bf), x1=pltpu.VMEM((2, XS, HALF, COL), bf), ldp=pltpu.VMEM((2, PART, COL), bf),
        r1=pltpu.VMEM((2, RS, HALF, COL), bf), zbuf=pltpu.VMEM((2, ZS, HALF, COL), bf),
        ru=pltpu.VMEM((2, 3, 3 * CH, COL), bf), rd=pltpu.VMEM((2, 3, 3 * CH, COL), bf),
        r3=pltpu.VMEM((2, 2, CH, COL), bf), fin=pltpu.VMEM((2, FS, CH, COL), bf),
        vcur=pltpu.VMEM((2, 16, BLK), jnp.float32), vrecv=pltpu.VMEM((6, 16, BLK), jnp.float32),
        prt_s=dma((NB,)), prt_r=dma((NB,)), h_s=dma((NB // 2,)), h_r=dma((NB // 2,)), ld_sem=dma((2, 2)), r1_s=dma((2, RS)), r1_r=dma((2, RS)),
        ru_s=dma((2, 4)), ru_r=dma((2, 4)), rd_s=dma((2, 4)), rd_r=dma((2, 4)), r3_s=dma((2, 2)), r3_r=dma((2, 2)),
        ag_s=dma((2, 3, 4, 4)), fin_s=dma((2, 4)), zr=dma((2, NP, 4)), xr=dma((2, NP, 4)), v_s=dma((6,)), v_r=dma((6,)),
    )


def scoped(name, fn, *args):
    with jax.named_scope(name):
        fn(*args)


class Program(Net):
    def __init__(self, refs, chips):
        super().__init__(refs)
        self.chips = chips
        self.s = lax.axis_index("section")
        self.core = (1 - self.s, lax.axis_index("batch"))
        self.comm = Comm(refs) if chips == 16 else None
        self.sent = []
        self.ticks = 0
        self.plan = {}

    def here(self, l, yes, no):
        pl.when(self.s == l)(yes)
        pl.when(self.s != l)(no)

    def remote(self, src, dst, ss, rs):
        return pltpu.make_async_remote_copy(src_ref=src, dst_ref=dst, send_sem=ss, recv_sem=rs, device_id=self.core, device_id_type=MESH)

    def barrier(self):
        if self.comm:
            self.comm.barrier()
        else:
            bar = pltpu.get_barrier_semaphore()
            pl.semaphore_signal(bar, inc=1, device_id=self.core, device_id_type=MESH)
            pl.semaphore_wait(bar, 1)

    def swap(self, m):
        return self.remote(self.own[m], self.other[m], self.wx_s.at[m], self.wx_r.at[m])

    def swap_par(self):
        return self.remote(self.par.at[self.s], self.par.at[self.s], self.wx_s.at[6], self.wx_r.at[6])

    def held(self, m):
        return self.w4.at[m] if m < 4 else (self.we, self.ws)[m - 4]

    def direct(self, m):
        return self.remote(self.own[m], self.held(m), self.dx_s.at[m], self.dx_r.at[m])

    def near(self, m):
        return pltpu.make_async_copy(self.own[m], self.held(m), self.w_sem.at[m])

    def wait_first(self, m):
        self.here(0, lambda: self.near(m).wait(), lambda: self.direct(m).wait_recv())

    def load(self, l, m):
        def theirs():
            self.swap(m).wait_recv()
            pltpu.make_async_copy(self.other[m], self.held(m), self.w_sem.at[m]).start()
        self.here(l, lambda: self.near(m).start(), theirs)

    def wait_load(self, m):
        self.near(m).wait()

    def aside(self, k, out):
        a, b = (self.probs, self.slope, self.act, self.q, self.k, self.v)[k], self.sp[k]
        return pltpu.make_async_copy(*((a, b) if out else (b, a)), self.sp_sem.at[k])

    def rows_near(self, k, l, src):
        return pltpu.make_async_copy(src, self.rows_at(k), self.ro_s.at[k, l])

    def rows_far(self, k, l, src):
        return self.remote(src, self.rows_at(k), self.ro_s.at[k, l], self.ro_r.at[k])

    def rows_at(self, k):
        return (self.lo, self.gi)[k].at[pl.ds(pl.multiple_of(self.s * T, T), T)]

    def put_rows(self, k, l, src):
        self.here(l, lambda: self.rows_near(k, l, src).start(), lambda: self.rows_far(k, l, src).start())

    def wait_rows(self, k, l, src):
        self.here(l, lambda: self.rows_near(k, l, src).wait(), lambda: self.rows_far(k, l, src).wait_send())

    def out_near(self, i, slot):
        return pltpu.make_async_copy(self.stage.at[slot], self.acc.at[i], self.st_sem.at[slot])

    def out_far(self, i, slot):
        return self.remote(self.stage.at[slot], self.prt.at[i], self.st_sem.at[slot], self.prt_r.at[i])

    def free_slot(self):
        if len(self.sent) < SLOTS:
            return len(self.sent)
        i, has, slot, done = self.sent[-SLOTS]
        if not done:
            self.settle(i)
        pl.when(self.s != has)(lambda: self.out_far(i, slot).wait_send())
        return slot

    def emit_out(self, l, b, slot):
        i = pair_place(l, b)
        self.here(b % 2, lambda: self.out_near(i, slot).start(), lambda: self.out_far(i, slot).start())
        self.sent.append([i, b % 2, slot, False])

    def settle(self, upto):
        for entry in self.sent:
            if entry[0] <= upto and not entry[3]:
                entry[3] = True
                pl.when(self.s == entry[1])(lambda: self.out_near(entry[0], entry[2]).wait())

    def point(self, name):
        if self.comm is None:
            return
        for _ in range(self.plan.get((self.layer, name), 0)):
            self.settle(self.ticks // 2)
            scoped("tick", self.comm.tick, self.ticks)
            self.ticks += 1

    def forward(self, l, low):
        self.layer = l
        ready = self.wait_first if l == 0 else self.wait_load
        if l == 1:
            for k in (3, 4, 5):
                self.aside(k, True).wait()
        scoped("qkv", self.qkv, l, ready)
        if l == 1:
            self.aside(0, True).wait()
        scoped("attend", self.attend, l)
        if l == 0:
            for k in (3, 4, 5, 0):
                self.aside(k, True).start()
        ready(3)
        scoped("mix", self.mix, l)
        if l == 1:
            self.aside(1, True).wait()
            self.aside(2, True).wait()
        ready(4)
        scoped("expand", self.expand, l)
        if l == 0:
            for m in range(5):
                self.load(1, m)
            self.aside(1, True).start()
            self.aside(2, True).start()
        ready(5)
        scoped("shrink", self.shrink, l, low)
        if l == 0:
            self.load(1, 5)

    def backward(self, l):
        self.layer = l
        again = l == 1
        if not again:
            self.aside(2, False).wait()
        scoped("top_back", self.top_back, l, lambda rows: self.gin[rows].astype(F32))
        if again:
            self.aside(2, False).start()
        else:
            self.aside(1, False).wait()
            self.wait_load(5)
        scoped("inner_back", self.inner_back, l, lambda: again and (self.load(0, 5), self.aside(1, False).start()), lambda: again or self.wait_load(4))
        if again:
            self.load(0, 4)
            self.wait_rows(0, 1, self.ag)
        else:
            self.wait_load(3)
        scoped("mid_back", self.mid_back, l)
        if again:
            self.load(0, 3)
        else:
            for k in (0, 3, 4, 5):
                self.aside(k, False).wait()
        scoped("attend_back", self.attend_back, l)
        if again:
            for k in (0, 3, 4, 5):
                self.aside(k, False).start()
        else:
            for m in range(3):
                self.wait_load(m)
            self.wait_rows(1, 1, self.gin)
        scoped("low_back", self.low_back, l, self.gin)
        if again:
            for m in range(3):
                self.load(0, m)
        self.put_rows(1, l, self.gin)

    def run(self):
        s = self.s
        rows = pl.ds(pl.multiple_of(s * T, T), T)
        first = (pltpu.make_async_copy(self.tokens.at[rows], self.h.at[0], self.in_sem.at[0]),
                 pltpu.make_async_copy(self.cotangent.at[rows], self.gin, self.in_sem.at[1]))
        first[0].start()
        for m in range(6):
            pl.when(s == 0)(lambda: self.near(m).start())
        first[1].start()
        for r, ref in enumerate(self.small[:8]):
            self.par[s, r:r + 1, :] = ref[...]
        for j in range(4):
            self.par[s, EB + j:EB + j + 1, :] = self.small[8][:, j * D:(j + 1) * D]
        self.barrier()

        @pl.when(s == 0)
        def _():
            self.direct(0).start()
            self.swap_par().start()
            for m in range(1, 6):
                self.direct(m).start()

        @pl.when(s == 1)
        def _():
            self.swap_par().start()
            for m in range(6):
                self.swap(m).start()
        self.vec[...] = jnp.zeros_like(self.vec)
        self.labels(self.ids[pl.ds(s, 1), :])
        for c in first:
            c.wait()
        pl.when(s == 1)(lambda: self.swap_par().wait_recv())
        self.forward(0, self.h.at[1])

        @pl.when(s == 0)
        def _():
            for m in range(6):
                self.swap(m).start()
        self.put_rows(0, 0, self.h.at[1])
        pl.when(s == 0)(lambda: self.swap_par().wait_recv())
        self.forward(1, self.ag)
        self.put_rows(0, 1, self.ag)
        self.backward(1)
        self.point("done")
        self.backward(0)
        self.settle(NB)
        for i, has, slot, _ in self.sent[-SLOTS:]:
            pl.when(s != has)(lambda: self.out_far(i, slot).wait_send())
        if self.comm:
            self.comm.vec_copy(0).start()

            def step(t, c):
                scoped("tick", self.comm.tick, t)
                for k in range(6):
                    pl.when(t == VEC_TICK + k)(functools.partial(self.comm.vec_step, k))
                return c
            lax.fori_loop(self.ticks, TICKS, step, 0)
            self.vec_out[...] = self.comm.vcur[0]
            self.comm.finish()
        else:
            for i in range(NB):
                self.out_far(i, 0).wait_recv()
            self.vec_out[...] = self.vec[...]
        for m in range(6):
            self.swap(m).wait_send()
            pl.when(s == 0)(lambda: self.direct(m).wait_send())
        self.swap_par().wait_send()
        self.wait_rows(0, 0, self.h.at[1])
        self.wait_rows(1, 0, self.gin)
        for k in (0, 1):
            self.rows_far(k, 0, self.gin).wait_recv()


def kernel(chips, names, plan, *refs):
    tokens, cotangent, ids = refs[0:3]
    weights = refs[3:9]
    small = refs[9:18]
    lo, gi, pool, vec_out, acc, prt, o4, oe, os_ = refs[18:27]
    named = dict(zip(names, refs[33:]))
    named.update(tokens=tokens, cotangent=cotangent, ids=ids, own=[w.at[0] for w in weights], small=small, lo=lo, gi=gi, pool=pool,
                 vec_out=vec_out, acc=acc, prt=prt, other=[o4.at[0], o4.at[1], o4.at[2], o4.at[3], oe, os_],
                 sp=refs[27:33])
    p = Program(named, chips)
    p.plan = plan
    p.run()


TICKS = NP + len(Comm.stages) - 1
VEC_TICK = TICKS - 7
PLAN = {(1, name): 1 for name in ("e1", "e3", "inner", "e7", "first", "mixer", "heads", "attend", "e9", "end")}
PLAN.update({(0, name): 1 for name in ("e1", "e3", "inner", "e7", "first", "mixer", "heads", "attend", "e9", "end")})


def both_layers(chips, tokens, cotangent, ids, weights, small):
    S = jax.ShapeDtypeStruct
    dma = pltpu.SemaphoreType.DMA
    sc = net_scratch()
    sc.update(comm_scratch())
    sc.update(wx_s=dma((7,)), wx_r=dma((7,)), dx_s=dma((6,)), dx_r=dma((6,)), w_sem=dma((6,)), sp_sem=dma((6,)), ro_s=dma((2, 2)), ro_r=dma((2,)), st_sem=dma((SLOTS,)),
              in_sem=dma((2,)))
    hbm, vm = pl.BlockSpec(memory_space=pl.ANY), pl.BlockSpec(memory_space=pltpu.VMEM)
    rows = S((2 * T, D), BF16)
    out = pl.pallas_call(
        functools.partial(kernel, chips, tuple(sc), PLAN),
        out_shape=(rows, rows, S((NB + NB // 2, D, D), BF16), S((16, D) if chips == 16 else (2, 16, D), F32), S((NB, D, D), BF16), S((NB, D, D), BF16), S((4, D, D), BF16), S((D, FF), BF16),
                   S((FF, D), BF16), S((HEADS, T, T), BF16), S((T, FF), BF16), S((T, FF), BF16)) + (S((T, D), BF16),) * 3,
        in_specs=[hbm, hbm, vm] + [hbm] * 6 + [vm] * 9,
        out_specs=(hbm, hbm, hbm, vm) + (hbm,) * 11,
        scratch_shapes=list(sc.values()),
        compiler_params=pltpu.CompilerParams(collective_id=0, has_side_effects=True, vmem_limit_bytes=64 * 2**20 - 2**17),
    )(tokens, cotangent, ids, *weights, *small)
    return out[:6]


WROWS, WBUFS = 768, 4


def widen_kernel(res, vec, sh, ex, mi, q, k, v, *rest):
    small, (low, wide, in_sem, out_sem) = rest[:9], rest[9:]
    per = D // WROWS
    count = NB * per

    def take(i):
        rows = pl.ds((i % per) * WROWS, WROWS)
        return pltpu.make_async_copy(res.at[i // per, rows], low.at[i % WBUFS], in_sem.at[i % WBUFS])

    def put(i):
        b, r = i // per, (i % per) * WROWS
        if b < 4:
            to = sh.at[0, pl.ds(b * D + r, WROWS)]
        elif b < 8:
            to = ex.at[0, pl.ds(r, WROWS), pl.ds((b - 4) * D, D)]
        else:
            to = (mi, q, k, v)[b - 8].at[0, pl.ds(r, WROWS)]
        return pltpu.make_async_copy(wide.at[i % WBUFS], to, out_sem.at[i % WBUFS])

    for i in range(WBUFS):
        take(i).start()
    for r in range(8):
        small[r][...] = vec[r:r + 1, :]
    for j in range(4):
        small[8][:, j * D:(j + 1) * D] = vec[EB + j:EB + j + 1, :]
    for i in range(count):
        take(i).wait()
        if i >= WBUFS:
            put(i - WBUFS).wait()

        def convert(j, c):
            rows = tile(j, 32)
            wide[i % WBUFS, rows] = low[i % WBUFS, rows].astype(F32)
            return c
        lax.fori_loop(0, WROWS // 32, convert, 0, unroll=4)
        put(i).start()
        if i + WBUFS < count:
            take(i + WBUFS).start()
    for i in range(count - WBUFS, count):
        put(i).wait()


def widen(res, vec):
    S = jax.ShapeDtypeStruct
    hbm, vm = pl.BlockSpec(memory_space=pl.ANY), pl.BlockSpec(memory_space=pltpu.VMEM)
    square, row = S((1, D, D), F32), S((1, D), F32)
    return pl.pallas_call(
        widen_kernel,
        out_shape=(S((1, FF, D), F32), S((1, D, FF), F32), square, square, square, square) + (row,) * 8 + (S((1, FF), F32),),
        in_specs=[hbm, vm], out_specs=(hbm,) * 6 + (vm,) * 9,
        scratch_shapes=[pltpu.VMEM((WBUFS, WROWS, D), BF16), pltpu.VMEM((WBUFS, WROWS, D), F32),
                        pltpu.SemaphoreType.DMA((WBUFS,)), pltpu.SemaphoreType.DMA((WBUFS,))],
        compiler_params=pltpu.CompilerParams(vmem_limit_bytes=62 * 2**20),
    )(res, vec)


def body(tokens, cotangent, sentence_ids, *stored):
    (query_w, query_b, keys_w, value_w, value_b, mixer_w, mixer_b, gain_one, shift_one, expand_w, expand_b, shrink_w, shrink_b, gain_two,
     shift_two) = stored
    chips = lax.axis_size("batch")
    lo, gi, pool, vec, acc, prt = both_layers(
        chips, tokens, cotangent, sentence_ids.reshape(2, T), (query_w, keys_w, value_w, mixer_w, expand_w, shrink_w),
        (query_b, value_b, mixer_b, gain_one, shift_one, shrink_b, gain_two, shift_two, expand_b))
    if chips != 16:
        s = lax.axis_index("section")
        part = acc.astype(F32) + prt.astype(F32)
        part = part.reshape(2, NB // 2, 1, D, D)
        pairs = jnp.where(lax.broadcasted_iota(jnp.int32, (1, 1, 2, 1, 1), 2) == s, part, 0.0)
        both = lax.psum(pairs, ("section", "batch")).reshape(2, NB, D, D)
        pool = lax.dynamic_index_in_dim(both, 1 - s, 0, keepdims=False).astype(BF16)
        vec = lax.dynamic_index_in_dim(lax.psum(vec, ("section", "batch")), s, 0, keepdims=False)
    sh, ex, mi, q, k, v, qb, vb, mb, g1, s1, sb, g2, s2, eb = widen(pool, vec)
    return (lo[None], gi[None], q, qb, k, v, vb, mi, mb, g1, s1, ex, eb, sh, sb, g2, s2)


def solution(mesh):
    placed = (
        P("batch", None),
        P("batch", None),
        P("batch"),
        P("section", None, None),
        P("section", None),
        P("section", None, None),
        P("section", None, None),
        P("section", None),
        P("section", None, None),
        P("section", None),
        P("section", None),
        P("section", None),
        P("section", None, None),
        P("section", None),
        P("section", None, None),
        P("section", None),
        P("section", None),
        P("section", None),
    )
    return jax.shard_map(
        body,
        mesh=mesh,
        in_specs=placed,
        out_specs=(
            P("section", "batch", None),
            P("section", "batch", None),
            P("section", None, None),
            P("section", None),
            P("section", None, None),
            P("section", None, None),
            P("section", None),
            P("section", None, None),
            P("section", None),
            P("section", None),
            P("section", None),
            P("section", None, None),
            P("section", None),
            P("section", None, None),
            P("section", None),
            P("section", None),
            P("section", None),
        ),
        check_vma=False,
    )
```

```python
import functools

import jax
import jax.numpy as jnp
from jax import lax
from jax.experimental import pallas as pl
from jax.experimental.pallas import tpu as pltpu
from jax.sharding import PartitionSpec as P

T = 512
D = 768
FF = 3072
HEADS = 12
TILE = 256
PAIR = 128
EPS = 1e-06
SLOTS = 3
F32, BF16 = jnp.float32, jnp.bfloat16
QB, VB, MB, G1, S1, SB, G2, S2, EB = 0, 1, 2, 3, 4, 5, 6, 7, 8


def dot(a, b):
    return jnp.dot(a, b, preferred_element_type=F32)


def dot_nt(a, b):
    return lax.dot_general(a, b, (((1,), (1,)), ((), ())), preferred_element_type=F32)


def tile(j, n=TILE):
    return pl.ds(pl.multiple_of(j * n, n), n)


def loop(n, fn, unroll=1):
    def step(i, c):
        fn(i)
        return c
    lax.fori_loop(0, n, step, 0, unroll=unroll)


def cdf_of(u):
    return 0.5 + 0.5 * lax.erf(u * 0.7071067811865476)


def gelu_slope(u):
    return cdf_of(u) + u * (0.3989422804014327 * jnp.exp2(u * (u * -0.7213475204444817)))


def fold(x):
    return jnp.sum(x.reshape(x.shape[0] // 8, 8, x.shape[1]), axis=0)


class Net:
    def __init__(self, refs):
        self.__dict__.update(refs)

    def row(self, l, r, cols=slice(None)):
        return self.par[l, r:r + 1, cols]

    def load(self, l, m):
        raise NotImplementedError

    def wait_load(self, l, m):
        raise NotImplementedError

    def point(self, name):
        pass

    def labels(self, ids):
        for a in range(4):
            for c in range(4):
                self.mask[a:a + 1, c * PAIR:(c + 1) * PAIR] = jnp.where(ids[c:c + 1, :] == ids[a:a + 1, 0:1], 0.0, -1e9)

    def qkv(self, l, ready):
        for m, out, b in ((0, self.q, QB), (1, self.k, None), (2, self.v, VB)):
            ready(m)
            r = dot(self.h[l], self.w4[m])
            if b is not None:
                r = r + self.row(l, b)
            r = r.astype(BF16)
            out[...] = r * BF16(0.125) if m == 0 else r

    def attend(self, l):
        lane = lax.broadcasted_iota(jnp.int32, (1, PAIR), 1)
        R = 256

        def body(hp):
            cols = tile(hp, PAIR)
            k2, v2 = self.k[:, cols], self.v[:, cols]
            kk = jnp.concatenate([jnp.where(lane < 64, k2, BF16(0)), jnp.where(lane >= 64, k2, BF16(0))], axis=0)
            for r in range(T // R):
                rows = pl.ds(r * R, R)
                both = dot_nt(self.q[rows, cols], kk)
                out = []
                for e in (0, 1):
                    s = both[:, e * T:(e + 1) * T].reshape(R // PAIR, PAIR, T)
                    s = (s + self.mask[r * R // PAIR:(r + 1) * R // PAIR, :][:, None, :]).reshape(R, T)
                    x = jnp.exp(s - jnp.max(s, axis=1, keepdims=True)).astype(BF16)
                    self.probs[2 * hp + e, rows] = x
                    out.append(dot(x, jnp.where(lane < 64 if e == 0 else lane >= 64, v2, BF16(1))))
                total = pltpu.roll(jnp.where(lane < 64, out[1], out[0]), 64, 1)
                self.att[l, rows, cols] = (jnp.where(lane < 64, out[0], out[1]) / total).astype(BF16)
        loop(HEADS // 2, body, 2)

    def norm(self, l, n_ref, k, g, b, low):
        def body(i):
            rows = tile(i, 128)
            x = self.tmp[rows]
            c = x - jnp.mean(x, axis=1, keepdims=True)
            inv = lax.rsqrt(jnp.mean(c * c, axis=1, keepdims=True) + EPS)
            n = c * inv
            n_ref[l, rows] = n.astype(n_ref.dtype)
            self.sc[rows, 2 * l + k:2 * l + k + 1] = inv
            y = n * self.row(l, g) + self.row(l, b)
            self.tmp[rows] = y
            low[rows] = y.astype(BF16)
        loop(T // 128, body, 4)

    def mix(self, l):
        self.tmp[...] = dot(self.att[l], self.w4[3]) + self.row(l, MB) + self.h[l].astype(F32)
        self.norm(l, self.n1, 0, G1, S1, self.fl.at[l])

    def expand(self, l):
        def body(j):
            cols = tile(j, D)
            u = dot(self.fl[l], self.we[:, cols]) + self.par[l, pl.ds(EB + j, 1), :]
            self.act[:, cols] = (u * cdf_of(u)).astype(BF16)
            self.inner[:, cols] = u.astype(BF16)
        loop(4, body)

    def shrink(self, l, low, ready):
        n = FF // 2
        if l == 0:
            ready(5)
            self.tmp[...] += dot(self.act[:, :n], self.ws[:n]) + self.row(l, SB)
            ready(6)
            self.tmp[...] += dot(self.act[:, n:], self.ws[n:])
        else:
            ready(5)
            self.tmp[...] += dot(self.act[...], self.ws[...]) + self.row(l, SB)
        self.norm(l, self.n2, 1, G2, S2, low)

    def norm_back(self, l, src, n_ref, k, g, b, low, low_row):
        def body(i, c):
            rows = tile(i, 128)
            dy = src(rows)
            n = n_ref[l, rows].astype(F32)
            gr = dy * self.row(l, g)
            m1 = jnp.mean(gr, axis=1, keepdims=True)
            m2 = jnp.mean(gr * n, axis=1, keepdims=True)
            dx = self.sc[rows, 2 * l + k:2 * l + k + 1] * (gr - m1 - n * m2)
            self.tmp[rows] = dx
            lw = dx.astype(BF16)
            low[rows] = lw
            return (c[0] + fold(dy * n), c[1] + fold(dy), c[2] + fold(lw.astype(F32)))
        z = jnp.zeros((8, D), F32)
        a, s, t = lax.fori_loop(0, T // 128, body, (z, z, z), unroll=4)
        for r, x in ((g, a), (b, s), (low_row, t)):
            self.vec[l, r:r + 1, :] = jnp.sum(x, axis=0, keepdims=True)

    def emit(self, l, b, left, right):
        slot = self.free_slot()
        self.stage[slot] = dot(left, right).astype(BF16)
        self.emit_out(l, b, slot)
        self.point("e%d" % b)

    def top_back(self, l, src):
        self.norm_back(l, src, self.n2, 1, G2, S2, self.og, SB)
        for b in range(4):
            self.emit(l, b, self.act[:, b * D:(b + 1) * D].T, self.og[...])

    def inner_back(self, l, done_inner, need_expand):
        def body(j):
            cols = tile(j, D)
            g = (dot_nt(self.og[...], self.ws[cols, :]) * gelu_slope(self.inner[:, cols].astype(F32))).astype(BF16)
            self.ig[:, cols] = g
            self.vec[l, pl.ds(EB + j, 1), :] = jnp.sum(g.astype(F32), axis=0, keepdims=True)
        loop(4, body)
        done_inner()
        self.point("inner")
        self.xt[...] = self.fl[l].T
        for b in range(4):
            self.emit(l, 4 + b, self.xt[...], self.ig[:, b * D:(b + 1) * D])
        need_expand()
        self.tmp[...] += dot_nt(self.ig[...], self.we[...])
        self.point("first")

    def mid_back(self, l):
        self.norm_back(l, lambda rows: self.tmp[rows], self.n1, 0, G1, S1, self.og, MB)
        self.emit(l, 8, self.att[l].T, self.og[...])
        self.ag[...] = dot_nt(self.og[...], self.w4[3]).astype(BF16)
        self.point("mixer")

    def attend_back(self, l):
        lane = lax.broadcasted_iota(jnp.int32, (1, PAIR), 1)

        def body(hp):
            cols = tile(hp, PAIR)
            q2, k2, v2 = self.q[:, cols], self.k[:, cols], self.v[:, cols]
            da = self.ag[:, cols]
            vv = jnp.concatenate([jnp.where(lane < 64, v2, BF16(0)), jnp.where(lane >= 64, v2, BF16(0))], axis=0)
            both = dot_nt(da, vv)
            ds, inv = [], []
            for e in (0, 1):
                x = self.probs[2 * hp + e].astype(F32)
                t = x * both[:, e * T:(e + 1) * T]
                i = 1.0 / jnp.sum(x, axis=1, keepdims=True)
                ds.append((t - x * (jnp.sum(t, axis=1, keepdims=True) * i)).astype(BF16))
                inv.append(i)
            inv = jnp.where(lane < 64, inv[0], inv[1])
            qt = (q2.astype(F32) * inv).astype(BF16).T
            dat = (da.astype(F32) * inv).astype(BF16).T
            dq = dot(ds[0], jnp.where(lane < 64, k2, BF16(0))) + dot(ds[1], jnp.where(lane >= 64, k2, BF16(0)))
            dq = (dq * (inv * 0.125)).astype(BF16)
            dk = jnp.concatenate([dot(qt[64 * e:64 * e + 64], ds[e]) for e in (0, 1)], axis=0).astype(BF16).T
            dv = jnp.concatenate([dot(dat[64 * e:64 * e + 64], self.probs[2 * hp + e]) for e in (0, 1)], axis=0).astype(BF16).T
            for m, r in ((0, dq), (1, dk), (2, dv)):
                self.ig[:, pl.ds(pl.multiple_of(m * D + hp * PAIR, PAIR), PAIR)] = r
            for r, x in ((QB, dq), (VB, dv)):
                self.vec[l, r:r + 1, cols] = jnp.sum(x.astype(F32), axis=0, keepdims=True)
        loop(3, body)
        self.point("heads")
        loop(3, lambda i: body(i + 3))
        self.point("attend")

    def low_back(self, l, out):
        self.xt[...] = self.h[l].T
        for m in range(3):
            self.emit(l, 9 + m, self.xt[...], self.ig[:, m * D:(m + 1) * D])
        x = self.tmp[...]
        for m in range(3):
            x = x + dot_nt(self.ig[:, m * D:(m + 1) * D], self.w4[m])
        out[...] = x.astype(BF16)
        self.point("end")


def net_scratch():
    return dict(
        w4=pltpu.VMEM((4, D, D), BF16), we=pltpu.VMEM((D, FF), BF16), ws=pltpu.VMEM((FF, D), BF16),
        par=pltpu.VMEM((2, 16, D), F32), vec=pltpu.VMEM((2, 16, D), F32), mask=pltpu.VMEM((8, T), F32),
        h=pltpu.VMEM((2, T, D), BF16), q=pltpu.VMEM((T, D), BF16), k=pltpu.VMEM((T, D), BF16), v=pltpu.VMEM((T, D), BF16),
        att=pltpu.VMEM((2, T, D), BF16), n1=pltpu.VMEM((2, T, D), BF16), n2=pltpu.VMEM((2, T, D), BF16), fl=pltpu.VMEM((2, T, D), BF16),
        sc=pltpu.VMEM((T, 4), F32),
        probs=pltpu.VMEM((HEADS, T, T), BF16), inner=pltpu.VMEM((T, FF), BF16), act=pltpu.VMEM((T, FF), BF16),
        tmp=pltpu.VMEM((T, D), F32), og=pltpu.VMEM((T, D), BF16), ag=pltpu.VMEM((T, D), BF16), ig=pltpu.VMEM((T, FF), BF16),
        xt=pltpu.VMEM((D, T), BF16), gin=pltpu.VMEM((T, D), BF16), stage=pltpu.VMEM((SLOTS, D, D), BF16),
    )


MESH = pl.DeviceIdType.MESH
NB = 12
LEG = NB
NP = 2 * LEG
BLK = 768
PART = 384
COL = 384
HALF = 192
CH = 48
XS, RS, ZS, FS = 2, 2, 5, 6


def when(cond, fn):
    if isinstance(cond, bool):
        if cond:
            fn()
    else:
        pl.when(cond)(fn)


def coords():
    s = lax.axis_index("section")
    b = lax.axis_index("batch")
    return s, b // 4, (b // 2) % 2, b % 2


def dev(s, z, y, x):
    return (s, z * 4 + y * 2 + x)


def pair_place(l, b):
    return (1 - l) * (NB // 2) + b // 2


class Comm:
    def __init__(self, refs):
        self.__dict__.update(refs)
        s, z, y, x = coords()
        self.s, self.p = s, z
        self.core = dev(1 - s, z, y, x)
        xn, yn = dev(s, z, y, 1 - x), dev(s, z, 1 - y, x)
        self.u = (x, y)
        self.w = (y, x)
        self.n1 = (xn, yn)
        self.n3 = (yn, xn)
        self.up = dev(s, jnp.minimum(z + 1, 3), y, x)
        self.dn = dev(s, jnp.maximum(z - 1, 0), y, x)

    def barrier(self):
        bar = pltpu.get_barrier_semaphore()
        for d in (self.core, self.n1[0], self.n1[1]):
            pl.semaphore_signal(bar, inc=1, device_id=d, device_id_type=MESH)

        @pl.when(self.p < 3)
        def _():
            pl.semaphore_signal(bar, inc=1, device_id=self.up, device_id_type=MESH)

        @pl.when(self.p > 0)
        def _():
            pl.semaphore_signal(bar, inc=1, device_id=self.dn, device_id_type=MESH)
        pl.semaphore_wait(bar, 4 + self.p * (3 - self.p) // 2)

    def slot_of(self, b):
        l = 1 - b // LEG
        mine = l * self.s + (1 - l) * (1 - self.s)
        pair = lax.rem(b, LEG) // 2
        return mine * (2 * pair + self.s) + (1 - mine) * (NB + pair)

    def remote(self, src, dst, ss, rs, d):
        return pltpu.make_async_remote_copy(src_ref=src, dst_ref=dst, send_sem=ss, recv_sem=rs, device_id=d, device_id_type=MESH)

    def prt_copy(self, src, i):
        return self.remote(src, self.prt.at[i], self.prt_s.at[i], self.prt_r.at[i], self.core)

    def loads(self, st, b):
        rows, cols = pl.ds(pl.multiple_of(lax.rem(b, 2) * PART, PART), PART), pl.ds(st * COL, COL)
        return (
            pltpu.make_async_copy(self.acc.at[b // 2, rows, cols], self.lda.at[st], self.ld_sem.at[st, 0]),
            pltpu.make_async_copy(self.prt.at[b // 2, rows, cols], self.ldp.at[st], self.ld_sem.at[st, 1]),
        )

    def s0(self, b):
        when(lax.rem(b, 2) == 0 if not isinstance(b, int) else b % 2 == 0, lambda: self.prt_copy(self.prt.at[b // 2], b // 2).wait_recv())
        for st in (0, 1):
            for c in self.loads(st, b):
                c.start()

    def r1_copy(self, st, b):
        sl = lax.rem(b, RS)
        return self.remote(self.x1.at[st, lax.rem(b, XS)], self.r1.at[st, sl], self.r1_s.at[st, sl], self.r1_r.at[st, sl], self.n1[st])

    def s1(self, b):
        for st in (0, 1):
            for c in self.loads(st, b):
                c.wait()
            oth = pl.ds(pl.multiple_of((1 - self.u[st]) * HALF, HALF), HALF)
            own = pl.ds(pl.multiple_of(self.u[st] * HALF, HALF), HALF)
            self.x1[st, lax.rem(b, XS)] = self.lda[st, oth] + self.ldp[st, oth]
            self.r1_copy(st, b).start()
            self.zbuf[st, lax.rem(b, ZS)] = self.lda[st, own] + self.ldp[st, own]

    def zsend(self, st, b, lo, hi, up):
        zs, zb = lax.rem(b, 4), lax.rem(b, ZS)
        if up:
            return self.remote(self.zbuf.at[st, zb, pl.ds(lo, hi - lo)], self.ru.at[st, lax.rem(b, 3), pl.ds(lo - CH, hi - lo)],
                               self.ru_s.at[st, zs], self.ru_r.at[st, zs], self.up)
        return self.remote(self.zbuf.at[st, zb, pl.ds(lo, hi - lo)], self.rd.at[st, lax.rem(b, 3), pl.ds(lo, hi - lo)],
                           self.rd_s.at[st, zs], self.rd_r.at[st, zs], self.dn)

    def zadd(self, st, b, lo, hi, up):
        zs = lax.rem(b, ZS)
        self.zsend(st, b, lo, hi, up).wait_recv()
        if up:
            self.zbuf[st, zs, lo:hi] += self.ru[st, lax.rem(b, 3), lo - CH:hi - CH]
        else:
            self.zbuf[st, zs, lo:hi] += self.rd[st, lax.rem(b, 3), lo:hi]

    def s2(self, b):
        for st in (0, 1):
            self.r1_copy(st, b).wait()
            self.zbuf[st, lax.rem(b, ZS)] += self.r1[st, lax.rem(b, RS)]
            pl.when(self.p == 0)(lambda: self.zsend(st, b, CH, 4 * CH, True).start())
            pl.when(self.p == 3)(lambda: self.zsend(st, b, 0, 3 * CH, False).start())

    def s3(self, b):
        for st in (0, 1):
            @pl.when(self.p == 1)
            def _():
                self.zadd(st, b, CH, 4 * CH, True)
                self.zsend(st, b, 2 * CH, 4 * CH, True).start()

            @pl.when(self.p == 2)
            def _():
                self.zadd(st, b, 0, 3 * CH, False)
                self.zsend(st, b, 0, 2 * CH, False).start()

    def s4(self, b):
        for st in (0, 1):
            @pl.when(self.p == 2)
            def _():
                self.zadd(st, b, 2 * CH, 4 * CH, True)
                self.zsend(st, b, 3 * CH, 4 * CH, True).start()

            @pl.when(self.p == 1)
            def _():
                self.zadd(st, b, 0, 2 * CH, False)
                self.zsend(st, b, 0, CH, False).start()

    def r3_copy(self, st, b):
        sl = lax.rem(b, 2)
        rows = pl.ds(pl.multiple_of(self.p * CH, CH), CH)
        return self.remote(self.zbuf.at[st, lax.rem(b, ZS), rows], self.r3.at[st, sl], self.r3_s.at[st, sl], self.r3_r.at[st, sl], self.n3[st])

    def s5(self, b):
        for st in (0, 1):
            pl.when(self.p == 0)(lambda: self.zadd(st, b, 0, CH, False))
            pl.when(self.p == 3)(lambda: self.zadd(st, b, 3 * CH, 4 * CH, True))
            self.r3_copy(st, b).start()

    def res_at(self, st, b, c):
        rows = pl.ds(pl.multiple_of(lax.rem(b, 2) * PART + self.u[st] * HALF + c * CH, CH), CH)
        return self.pool.at[self.slot_of(b), rows, pl.ds(st * COL, COL)]

    def ag_copy(self, st, b, c, d, src=None):
        here = self.res_at(st, b, c)
        to, sem = ((self.up, self.zr), (self.dn, self.zr), (self.n1[st], self.xr))[d]
        return self.remote(here if src is None else src, here, self.ag_s.at[st, d, c, lax.rem(b, 4)], sem.at[st, b, c], to)

    def own_copy(self, st, b):
        return pltpu.make_async_copy(self.fin.at[st, lax.rem(b, FS)], self.res_at(st, b, self.p), self.fin_s.at[st, lax.rem(b, 4)])

    def spread(self, st, b, c, up, down, src=None):
        if up:
            pl.when(self.p < 3)(lambda: self.ag_copy(st, b, c, 0, src).start())
        if down:
            pl.when(self.p > 0)(lambda: self.ag_copy(st, b, c, 1, src).start())
        self.ag_copy(st, b, c, 2, src).start()

    def s6(self, b):
        for st in (0, 1):
            self.r3_copy(st, b).wait()
            rows = pl.ds(pl.multiple_of(self.p * CH, CH), CH)
            fin = self.fin.at[st, lax.rem(b, FS)]
            fin[...] = self.zbuf[st, lax.rem(b, ZS), rows] + self.r3[st, lax.rem(b, 2)]
            self.spread(st, b, self.p, True, True, fin)
            self.own_copy(st, b).start()
            pl.when(self.p == 0)(lambda: self.zsend(st, b, CH, 4 * CH, True).wait_send())
            pl.when(self.p == 3)(lambda: self.zsend(st, b, 0, 3 * CH, False).wait_send())

            @pl.when(self.p == 1)
            def _():
                self.zsend(st, b, 2 * CH, 4 * CH, True).wait_send()
                self.zsend(st, b, 0, CH, False).wait_send()

            @pl.when(self.p == 2)
            def _():
                self.zsend(st, b, 0, 2 * CH, False).wait_send()
                self.zsend(st, b, 3 * CH, 4 * CH, True).wait_send()

    def hop(self, k, b):
        for st in (0, 1):
            @pl.when(self.p >= k)
            def _():
                self.ag_copy(st, b, self.p - k, 0).wait_recv()
                self.spread(st, b, self.p - k, True, False)

            @pl.when(self.p <= 3 - k)
            def _():
                self.ag_copy(st, b, self.p + k, 1).wait_recv()
                self.spread(st, b, self.p + k, False, True)

    def s7(self, b):
        self.hop(1, b)

    def s8(self, b):
        self.hop(2, b)

    def s9(self, b):
        self.hop(3, b)

    def s10(self, b):
        for st in (0, 1):
            self.own_copy(st, b).wait()
            for c in range(4):
                got = self.ag_copy(st, b, c, 2)
                got.wait_send()
                got.wait_recv()
                pl.when((self.p < 3) & (self.p >= c))(lambda: self.ag_copy(st, b, c, 0).wait_send())
                pl.when((self.p > 0) & (self.p <= c))(lambda: self.ag_copy(st, b, c, 1).wait_send())
        pair = lax.rem(b, LEG) // 2
        pl.when((1 - b // LEG != self.s) & (lax.rem(b, 2) == 1))(lambda: self.home(pair).start())

    stages = ("s0", "s1", "s2", "s3", "s4", "s5", "s6", "s7", "s8", "s9", "s10")

    def home(self, pair):
        return self.remote(self.pool.at[NB + pair], self.pool.at[2 * pair + self.s], self.h_s.at[pair], self.h_r.at[pair], self.core)

    def finish(self):
        for pair in range(NB // 2):
            self.home(pair).wait()

    def tick(self, t):
        for k in reversed(range(len(self.stages))):
            b = t - k
            when(0 <= b < NP if isinstance(b, int) else (b >= 0) & (b < NP), lambda: getattr(self, self.stages[k])(b))

    def vec_copy(self, k):
        s, z, y, x = coords()
        odd = lax.rem(z, 2)
        to = (self.core, dev(s, z, y, 1 - x), dev(s, z, 1 - y, x), dev(s, z + 1 - 2 * odd, y, x), dev(s, jnp.clip(3 - z, 1, 2), y, x),
              dev(s, jnp.where(z == 1, 0, 3), y, x))[k]
        src = self.vec.at[1 - s] if k == 0 else self.vcur.at[(k - 1) % 2]
        return self.remote(src, self.vrecv.at[k], self.v_s.at[k], self.v_r.at[k], to)

    def vec_step(self, k):
        inner = (self.p == 1) | (self.p == 2)
        if k < 4:
            self.vec_copy(k).wait()
            before = self.vec[self.s] if k == 0 else self.vcur[(k - 1) % 2]
            self.vcur[k % 2] = before + self.vrecv[k]
            if k < 3:
                self.vec_copy(k + 1).start()
            else:
                pl.when(inner)(lambda: self.vec_copy(4).start())
        elif k == 4:
            @pl.when(inner)
            def _():
                self.vec_copy(4).wait()
                self.vcur[0] = self.vcur[1] + self.vrecv[4]
                self.vec_copy(5).start()
        else:
            pl.when(inner)(lambda: self.vec_copy(5).wait_send())

            @pl.when((self.p == 0) | (self.p == 3))
            def _():
                self.vec_copy(5).wait_recv()
                self.vcur[0] = self.vrecv[5]


def comm_scratch():
    bf = jnp.bfloat16
    dma = pltpu.SemaphoreType.DMA
    return dict(
        lda=pltpu.VMEM((2, PART, COL), bf), x1=pltpu.VMEM((2, XS, HALF, COL), bf), ldp=pltpu.VMEM((2, PART, COL), bf),
        r1=pltpu.VMEM((2, RS, HALF, COL), bf), zbuf=pltpu.VMEM((2, ZS, HALF, COL), bf),
        ru=pltpu.VMEM((2, 3, 3 * CH, COL), bf), rd=pltpu.VMEM((2, 3, 3 * CH, COL), bf),
        r3=pltpu.VMEM((2, 2, CH, COL), bf), fin=pltpu.VMEM((2, FS, CH, COL), bf),
        vcur=pltpu.VMEM((2, 16, BLK), jnp.float32), vrecv=pltpu.VMEM((6, 16, BLK), jnp.float32),
        prt_s=dma((NB,)), prt_r=dma((NB,)), h_s=dma((NB // 2,)), h_r=dma((NB // 2,)), ld_sem=dma((2, 2)), r1_s=dma((2, RS)), r1_r=dma((2, RS)),
        ru_s=dma((2, 4)), ru_r=dma((2, 4)), rd_s=dma((2, 4)), rd_r=dma((2, 4)), r3_s=dma((2, 2)), r3_r=dma((2, 2)),
        ag_s=dma((2, 3, 4, 4)), fin_s=dma((2, 4)), zr=dma((2, NP, 4)), xr=dma((2, NP, 4)), v_s=dma((6,)), v_r=dma((6,)),
    )


def scoped(name, fn, *args):
    with jax.named_scope(name):
        fn(*args)


class Program(Net):
    def __init__(self, refs, chips):
        super().__init__(refs)
        self.chips = chips
        self.s = lax.axis_index("section")
        self.core = (1 - self.s, lax.axis_index("batch"))
        self.comm = Comm(refs) if chips == 16 else None
        self.sent = []
        self.ticks = 0
        self.plan = {}

    def here(self, l, yes, no):
        pl.when(self.s == l)(yes)
        pl.when(self.s != l)(no)

    def remote(self, src, dst, ss, rs):
        return pltpu.make_async_remote_copy(src_ref=src, dst_ref=dst, send_sem=ss, recv_sem=rs, device_id=self.core, device_id_type=MESH)

    def barrier(self):
        if self.comm:
            self.comm.barrier()
        else:
            bar = pltpu.get_barrier_semaphore()
            pl.semaphore_signal(bar, inc=1, device_id=self.core, device_id_type=MESH)
            pl.semaphore_wait(bar, 1)

    def swap(self, m):
        return self.remote(self.own[m], self.other[m], self.wx_s.at[m], self.wx_r.at[m])

    def swap_par(self):
        return self.remote(self.par.at[self.s], self.par.at[self.s], self.wx_s.at[6], self.wx_r.at[6])

    def held(self, m):
        return self.w4.at[m] if m < 4 else (self.we, self.ws)[m - 4]

    def first_refs(self, m):
        if m < 5:
            return self.own[m], self.held(m)
        half = pl.ds((m - 5) * (FF // 2), FF // 2)
        return self.own[5].at[half], self.ws.at[half]

    def direct(self, m):
        return self.remote(*self.first_refs(m), self.dx_s.at[m], self.dx_r.at[m])

    def first_near(self, m):
        return pltpu.make_async_copy(*self.first_refs(m), self.w_sem.at[m])

    def near(self, m):
        return pltpu.make_async_copy(self.own[m], self.held(m), self.w_sem.at[m])

    def wait_first(self, m):
        self.here(0, lambda: self.first_near(m).wait(), lambda: self.direct(m).wait_recv())

    def load(self, l, m):
        def theirs():
            self.swap(m).wait_recv()
            pltpu.make_async_copy(self.other[m], self.held(m), self.w_sem.at[m]).start()
        self.here(l, lambda: self.near(m).start(), theirs)

    def wait_load(self, m):
        self.near(m).wait()

    def aside(self, k, out):
        a, b = (self.probs, self.inner, self.act, self.q, self.k, self.v)[k], self.sp[k]
        return pltpu.make_async_copy(*((a, b) if out else (b, a)), self.sp_sem.at[k])

    def rows_near(self, k, l, src):
        return pltpu.make_async_copy(src, self.rows_at(k), self.ro_s.at[k, l])

    def rows_far(self, k, l, src):
        return self.remote(src, self.rows_at(k), self.ro_s.at[k, l], self.ro_r.at[k])

    def rows_at(self, k):
        return (self.lo, self.gi)[k].at[pl.ds(pl.multiple_of(self.s * T, T), T)]

    def put_rows(self, k, l, src):
        self.here(l, lambda: self.rows_near(k, l, src).start(), lambda: self.rows_far(k, l, src).start())

    def wait_rows(self, k, l, src):
        self.here(l, lambda: self.rows_near(k, l, src).wait(), lambda: self.rows_far(k, l, src).wait_send())

    def out_near(self, i, slot):
        return pltpu.make_async_copy(self.stage.at[slot], self.acc.at[i], self.st_sem.at[slot])

    def out_far(self, i, slot):
        return self.remote(self.stage.at[slot], self.prt.at[i], self.st_sem.at[slot], self.prt_r.at[i])

    def free_slot(self):
        if len(self.sent) < SLOTS:
            return len(self.sent)
        i, has, slot, done = self.sent[-SLOTS]
        if not done:
            self.settle(i)
        pl.when(self.s != has)(lambda: self.out_far(i, slot).wait_send())
        return slot

    def emit_out(self, l, b, slot):
        i = pair_place(l, b)
        self.here(b % 2, lambda: self.out_near(i, slot).start(), lambda: self.out_far(i, slot).start())
        self.sent.append([i, b % 2, slot, False])

    def settle(self, upto):
        for entry in self.sent:
            if entry[0] <= upto and not entry[3]:
                entry[3] = True
                pl.when(self.s == entry[1])(lambda: self.out_near(entry[0], entry[2]).wait())

    def point(self, name):
        if self.comm is None:
            return
        for _ in range(self.plan.get((self.layer, name), 0)):
            assert self.ticks >= NP or len(self.sent) >= 2 * (self.ticks // 2 + 1)
            self.settle(self.ticks // 2)
            scoped("tick", self.comm.tick, self.ticks)
            self.ticks += 1

    def forward(self, l, low):
        self.layer = l
        ready = self.wait_first if l == 0 else self.wait_load
        if l == 1:
            for k in (3, 4, 5):
                self.aside(k, True).wait()
        scoped("qkv", self.qkv, l, ready)
        if l == 1:
            self.aside(0, True).wait()
        scoped("attend", self.attend, l)
        if l == 0:
            for m in range(3):
                self.load(1, m)
            for k in (3, 4, 5, 0):
                self.aside(k, True).start()
        ready(3)
        scoped("mix", self.mix, l)
        if l == 0:
            self.load(1, 3)
        else:
            self.aside(1, True).wait()
            self.aside(2, True).wait()
        ready(4)
        scoped("expand", self.expand, l)
        if l == 0:
            self.load(1, 4)
            self.aside(1, True).start()
            self.aside(2, True).start()
        scoped("shrink", self.shrink, l, low, ready)
        if l == 0:
            self.load(1, 5)

    def backward(self, l):
        self.layer = l
        again = l == 1
        if not again:
            self.aside(2, False).wait()
        scoped("top_back", self.top_back, l, lambda rows: self.gin[rows].astype(F32))
        if again:
            self.aside(2, False).start()
        else:
            self.aside(1, False).wait()
            self.wait_load(5)
        scoped("inner_back", self.inner_back, l, lambda: again and (self.load(0, 5), self.aside(1, False).start()), lambda: again or self.wait_load(4))
        if again:
            self.load(0, 4)
            self.wait_rows(0, 1, self.ag)
        else:
            self.wait_load(3)
        scoped("mid_back", self.mid_back, l)
        if again:
            self.load(0, 3)
        else:
            for k in (0, 3, 4, 5):
                self.aside(k, False).wait()
        scoped("attend_back", self.attend_back, l)
        if again:
            for k in (0, 3, 4, 5):
                self.aside(k, False).start()
        else:
            for m in range(3):
                self.wait_load(m)
            self.wait_rows(1, 1, self.gin)
        scoped("low_back", self.low_back, l, self.gin)
        if again:
            for m in range(3):
                self.load(0, m)
        self.put_rows(1, l, self.gin)

    def run(self):
        s = self.s
        rows = pl.ds(pl.multiple_of(s * T, T), T)
        first = (pltpu.make_async_copy(self.tokens.at[rows], self.h.at[0], self.in_sem.at[0]),
                 pltpu.make_async_copy(self.cotangent.at[rows], self.gin, self.in_sem.at[1]))
        first[0].start()
        for m in range(7):
            pl.when(s == 0)(lambda: self.first_near(m).start())
        first[1].start()
        for r, ref in enumerate(self.small[:8]):
            self.par[s, r:r + 1, :] = ref[...]
        for j in range(4):
            self.par[s, EB + j:EB + j + 1, :] = self.small[8][:, j * D:(j + 1) * D]
        self.barrier()

        @pl.when(s == 0)
        def _():
            self.direct(0).start()
            self.swap_par().start()
            for m in range(1, 7):
                self.direct(m).start()

        @pl.when(s == 1)
        def _():
            self.swap_par().start()
            for m in range(6):
                self.swap(m).start()
        self.vec[...] = jnp.zeros_like(self.vec)
        self.labels(jnp.where(s == 0, self.ids[0:4, :], self.ids[4:8, :]))
        for c in first:
            c.wait()
        pl.when(s == 1)(lambda: self.swap_par().wait_recv())
        self.forward(0, self.h.at[1])

        @pl.when(s == 0)
        def _():
            for m in range(6):
                self.swap(m).start()
        self.put_rows(0, 0, self.h.at[1])
        pl.when(s == 0)(lambda: self.swap_par().wait_recv())
        self.forward(1, self.ag)
        self.put_rows(0, 1, self.ag)
        self.backward(1)
        self.point("done")
        self.backward(0)
        self.settle(NB)
        for i, has, slot, _ in self.sent[-SLOTS:]:
            pl.when(s != has)(lambda: self.out_far(i, slot).wait_send())
        if self.comm:
            self.comm.vec_copy(0).start()

            def step(t, c):
                scoped("tick", self.comm.tick, t)
                for k in range(6):
                    pl.when(t == VEC_TICK + k)(functools.partial(self.comm.vec_step, k))
                return c
            lax.fori_loop(self.ticks, TICKS, step, 0)
            self.vec_out[...] = self.comm.vcur[0]
            self.comm.finish()
        else:
            for i in range(NB):
                self.out_far(i, 0).wait_recv()
            self.vec_out[...] = self.vec[...]
        for m in range(6):
            self.swap(m).wait_send()
        for m in range(7):
            pl.when(s == 0)(lambda: self.direct(m).wait_send())
        self.swap_par().wait_send()
        self.wait_rows(0, 0, self.h.at[1])
        self.wait_rows(1, 0, self.gin)
        for k in (0, 1):
            self.rows_far(k, 0, self.gin).wait_recv()


def kernel(chips, names, plan, *refs):
    tokens, cotangent, ids = refs[0:3]
    weights = refs[3:9]
    small = refs[9:18]
    lo, gi, pool, vec_out, acc, prt, o4, oe, os_ = refs[18:27]
    named = dict(zip(names, refs[33:]))
    named.update(tokens=tokens, cotangent=cotangent, ids=ids, own=[w.at[0] for w in weights], small=small, lo=lo, gi=gi, pool=pool,
                 vec_out=vec_out, acc=acc, prt=prt, other=[o4.at[0], o4.at[1], o4.at[2], o4.at[3], oe, os_],
                 sp=refs[27:33])
    p = Program(named, chips)
    p.plan = plan
    p.run()


TICKS = NP + len(Comm.stages) - 1
VEC_TICK = TICKS - 7
PLAN = {(1, name): 1 for name in ("e1", "e2", "e3", "inner", "e7", "first", "mixer", "heads", "e9", "end")}
PLAN.update({(0, name): 1 for name in ("e1", "e3", "inner", "e7", "first", "mixer", "heads", "attend", "e9", "end")})


def both_layers(chips, tokens, cotangent, ids, weights, small):
    S = jax.ShapeDtypeStruct
    dma = pltpu.SemaphoreType.DMA
    sc = net_scratch()
    sc.update(comm_scratch())
    sc.update(wx_s=dma((7,)), wx_r=dma((7,)), dx_s=dma((7,)), dx_r=dma((7,)), w_sem=dma((7,)), sp_sem=dma((6,)), ro_s=dma((2, 2)), ro_r=dma((2,)), st_sem=dma((SLOTS,)),
              in_sem=dma((2,)))
    hbm, vm = pl.BlockSpec(memory_space=pl.ANY), pl.BlockSpec(memory_space=pltpu.VMEM)
    rows = S((2 * T, D), BF16)
    out = pl.pallas_call(
        functools.partial(kernel, chips, tuple(sc), PLAN),
        out_shape=(rows, rows, S((NB + NB // 2, D, D), BF16), S((16, D) if chips == 16 else (2, 16, D), F32), S((NB, D, D), BF16), S((NB, D, D), BF16), S((4, D, D), BF16), S((D, FF), BF16),
                   S((FF, D), BF16), S((HEADS, T, T), BF16), S((T, FF), BF16), S((T, FF), BF16)) + (S((T, D), BF16),) * 3,
        in_specs=[hbm, hbm, vm] + [hbm] * 6 + [vm] * 9,
        out_specs=(hbm, hbm, hbm, vm) + (hbm,) * 11,
        scratch_shapes=list(sc.values()),
        compiler_params=pltpu.CompilerParams(collective_id=0, has_side_effects=True, vmem_limit_bytes=64 * 2**20 - 2**17),
    )(tokens, cotangent, ids, *weights, *small)
    return out[:6]


WROWS, WBUFS = 768, 4


def widen_kernel(res, vec, lo, gi, sh, ex, mi, q, k, v, lo_out, gi_out, *rest):
    small, (low, wide, in_sem, out_sem, row_buf, row_sem) = rest[:9], rest[9:]
    rows_in = [pltpu.make_async_copy(a, row_buf.at[i], row_sem.at[i]) for i, a in enumerate((lo, gi))]
    rows_out = [pltpu.make_async_copy(row_buf.at[i], a.at[0], row_sem.at[i]) for i, a in enumerate((lo_out, gi_out))]
    per = D // WROWS
    count = NB * per

    def take(i):
        rows = pl.ds((i % per) * WROWS, WROWS)
        return pltpu.make_async_copy(res.at[i // per, rows], low.at[i % WBUFS], in_sem.at[i % WBUFS])

    def put(i):
        b, r = i // per, (i % per) * WROWS
        if b < 4:
            to = sh.at[0, pl.ds(b * D + r, WROWS)]
        elif b < 8:
            to = ex.at[0, pl.ds(r, WROWS), pl.ds((b - 4) * D, D)]
        else:
            to = (mi, q, k, v)[b - 8].at[0, pl.ds(r, WROWS)]
        return pltpu.make_async_copy(wide.at[i % WBUFS], to, out_sem.at[i % WBUFS])

    for i in range(WBUFS):
        take(i).start()
    for c in rows_in:
        c.start()
    for r in range(8):
        small[r][...] = vec[r:r + 1, :]
    for j in range(4):
        small[8][:, j * D:(j + 1) * D] = vec[EB + j:EB + j + 1, :]
    for i in range(count):
        take(i).wait()
        if i >= WBUFS:
            put(i - WBUFS).wait()

        def convert(j, c):
            rows = tile(j, 32)
            wide[i % WBUFS, rows] = low[i % WBUFS, rows].astype(F32)
            return c
        lax.fori_loop(0, WROWS // 32, convert, 0, unroll=4)
        put(i).start()
        if i == 1:
            for a, b in zip(rows_in, rows_out):
                a.wait()
                b.start()
        if i + WBUFS < count:
            take(i + WBUFS).start()
    for i in range(count - WBUFS, count):
        put(i).wait()
    for c in rows_out:
        c.wait()


def widen(res, vec, lo, gi):
    S = jax.ShapeDtypeStruct
    hbm, vm = pl.BlockSpec(memory_space=pl.ANY), pl.BlockSpec(memory_space=pltpu.VMEM)
    square, row = S((1, D, D), F32), S((1, D), F32)
    return pl.pallas_call(
        widen_kernel,
        out_shape=(S((1, FF, D), F32), S((1, D, FF), F32), square, square, square, square, S((1, 2 * T, D), BF16), S((1, 2 * T, D), BF16)) + (row,) * 8 + (S((1, FF), F32),),
        in_specs=[hbm, vm, hbm, hbm], out_specs=(hbm,) * 8 + (vm,) * 9,
        scratch_shapes=[pltpu.VMEM((WBUFS, WROWS, D), BF16), pltpu.VMEM((WBUFS, WROWS, D), F32),
                        pltpu.SemaphoreType.DMA((WBUFS,)), pltpu.SemaphoreType.DMA((WBUFS,)), pltpu.VMEM((2, 2 * T, D), BF16), pltpu.SemaphoreType.DMA((2,))],
        compiler_params=pltpu.CompilerParams(vmem_limit_bytes=62 * 2**20),
    )(res, vec, lo, gi)


def body(tokens, cotangent, sentence_ids, *stored):
    (query_w, query_b, keys_w, value_w, value_b, mixer_w, mixer_b, gain_one, shift_one, expand_w, expand_b, shrink_w, shrink_b, gain_two,
     shift_two) = stored
    chips = lax.axis_size("batch")
    lo, gi, pool, vec, acc, prt = both_layers(
        chips, tokens, cotangent, sentence_ids.reshape(8, PAIR), (query_w, keys_w, value_w, mixer_w, expand_w, shrink_w),
        (query_b, value_b, mixer_b, gain_one, shift_one, shrink_b, gain_two, shift_two, expand_b))
    if chips != 16:
        s = lax.axis_index("section")
        part = acc.astype(F32) + prt.astype(F32)
        part = part.reshape(2, NB // 2, 1, D, D)
        pairs = jnp.where(lax.broadcasted_iota(jnp.int32, (1, 1, 2, 1, 1), 2) == s, part, 0.0)
        both = lax.psum(pairs, ("section", "batch")).reshape(2, NB, D, D)
        pool = lax.dynamic_index_in_dim(both, 1 - s, 0, keepdims=False).astype(BF16)
        vec = lax.dynamic_index_in_dim(lax.psum(vec, ("section", "batch")), s, 0, keepdims=False)
    sh, ex, mi, q, k, v, lo, gi, qb, vb, mb, g1, s1, sb, g2, s2, eb = widen(pool, vec, lo, gi)
    return (lo, gi, q, qb, k, v, vb, mi, mb, g1, s1, ex, eb, sh, sb, g2, s2)


def solution(mesh):
    placed = (
        P("batch", None),
        P("batch", None),
        P("batch"),
        P("section", None, None),
        P("section", None),
        P("section", None, None),
        P("section", None, None),
        P("section", None),
        P("section", None, None),
        P("section", None),
        P("section", None),
        P("section", None),
        P("section", None, None),
        P("section", None),
        P("section", None, None),
        P("section", None),
        P("section", None),
        P("section", None),
    )
    return jax.shard_map(
        body,
        mesh=mesh,
        in_specs=placed,
        out_specs=(
            P("section", "batch", None),
            P("section", "batch", None),
            P("section", None, None),
            P("section", None),
            P("section", None, None),
            P("section", None, None),
            P("section", None),
            P("section", None, None),
            P("section", None),
            P("section", None),
            P("section", None),
            P("section", None, None),
            P("section", None),
            P("section", None, None),
            P("section", None),
            P("section", None),
            P("section", None),
        ),
        check_vma=False,
    )
```

```python
import functools

import jax
import jax.numpy as jnp
from jax import lax
from jax.experimental import pallas as pl
from jax.experimental.pallas import tpu as pltpu
from jax.sharding import PartitionSpec as P

T = 512
D = 768
FF = 3072
HEADS = 12
TILE = 256
PAIR = 128
EPS = 1e-06
SLOTS = 3
F32, BF16 = jnp.float32, jnp.bfloat16
QB, VB, MB, G1, S1, SB, G2, S2, EB = 0, 1, 2, 3, 4, 5, 6, 7, 8


def dot(a, b):
    return jnp.dot(a, b, preferred_element_type=F32)


def dot_nt(a, b):
    return lax.dot_general(a, b, (((1,), (1,)), ((), ())), preferred_element_type=F32)


def tile(j, n=TILE):
    return pl.ds(pl.multiple_of(j * n, n), n)


def loop(n, fn, unroll=1):
    def step(i, c):
        fn(i)
        return c
    lax.fori_loop(0, n, step, 0, unroll=unroll)


def cdf_of(u):
    return 0.5 + 0.5 * lax.erf(u * 0.7071067811865476)


def gelu_slope(u):
    return cdf_of(u) + u * (0.3989422804014327 * jnp.exp2(u * (u * -0.7213475204444817)))


def fold(x):
    return jnp.sum(x.reshape(x.shape[0] // 8, 8, x.shape[1]), axis=0)


class Net:
    def __init__(self, refs):
        self.__dict__.update(refs)

    def row(self, l, r, cols=slice(None)):
        return self.par[l, r:r + 1, cols]

    def load(self, l, m):
        raise NotImplementedError

    def wait_load(self, l, m):
        raise NotImplementedError

    def point(self, name):
        pass

    def labels(self, ids):
        for a in range(4):
            for c in range(4):
                self.mask[a:a + 1, c * PAIR:(c + 1) * PAIR] = jnp.where(ids[c:c + 1, :] == ids[a:a + 1, 0:1], 0.0, -1e9)

    def qkv(self, l, ready):
        for m, out, b in ((0, self.q, QB), (1, self.k, None), (2, self.v, VB)):
            ready(m)
            r = dot(self.h[l], self.w4[m])
            if b is not None:
                r = r + self.row(l, b)
            r = r.astype(BF16)
            out[...] = r * BF16(0.125) if m == 0 else r

    def attend(self, l):
        lane = lax.broadcasted_iota(jnp.int32, (1, PAIR), 1)
        R = 256

        def body(hp):
            cols = tile(hp, PAIR)
            k2, v2 = self.k[:, cols], self.v[:, cols]
            kk = jnp.concatenate([jnp.where(lane < 64, k2, BF16(0)), jnp.where(lane >= 64, k2, BF16(0))], axis=0)
            for r in range(T // R):
                rows = pl.ds(r * R, R)
                both = dot_nt(self.q[rows, cols], kk)
                out = []
                for e in (0, 1):
                    s = both[:, e * T:(e + 1) * T].reshape(R // PAIR, PAIR, T)
                    s = (s + self.mask[r * R // PAIR:(r + 1) * R // PAIR, :][:, None, :]).reshape(R, T)
                    x = jnp.exp(s - jnp.max(s, axis=1, keepdims=True)).astype(BF16)
                    self.probs[2 * hp + e, rows] = x
                    out.append(dot(x, jnp.where(lane < 64 if e == 0 else lane >= 64, v2, BF16(1))))
                total = pltpu.roll(jnp.where(lane < 64, out[1], out[0]), 64, 1)
                self.att[l, rows, cols] = (jnp.where(lane < 64, out[0], out[1]) / total).astype(BF16)
        loop(HEADS // 2, body, 2)

    def norm(self, l, n_ref, k, g, b, low):
        def body(i):
            rows = tile(i, 128)
            x = self.tmp[rows]
            c = x - jnp.mean(x, axis=1, keepdims=True)
            inv = lax.rsqrt(jnp.mean(c * c, axis=1, keepdims=True) + EPS)
            n = c * inv
            n_ref[l, rows] = n.astype(n_ref.dtype)
            self.sc[rows, 2 * l + k:2 * l + k + 1] = inv
            y = n * self.row(l, g) + self.row(l, b)
            self.tmp[rows] = y
            low[rows] = y.astype(BF16)
        loop(T // 128, body, 4)

    def mix(self, l):
        self.tmp[...] = dot(self.att[l], self.w4[3]) + self.row(l, MB) + self.h[l].astype(F32)
        self.norm(l, self.n1, 0, G1, S1, self.fl.at[l])

    def expand(self, l):
        def body(j):
            cols = tile(j, D)
            u = dot(self.fl[l], self.we[:, cols]) + self.par[l, pl.ds(EB + j, 1), :]
            self.act[:, cols] = (u * cdf_of(u)).astype(BF16)
            self.inner[:, cols] = u.astype(BF16)
        loop(4, body)

    def shrink(self, l, low, ready):
        n = FF // 2
        if l == 0:
            ready(5)
            self.tmp[...] += dot(self.act[:, :n], self.ws[:n]) + self.row(l, SB)
            ready(6)
            self.tmp[...] += dot(self.act[:, n:], self.ws[n:])
        else:
            ready(5)
            self.tmp[...] += dot(self.act[...], self.ws[...]) + self.row(l, SB)
        self.norm(l, self.n2, 1, G2, S2, low)

    def norm_back(self, l, src, n_ref, k, g, b, low, low_row):
        def body(i, c):
            rows = tile(i, 128)
            dy = src(rows)
            n = n_ref[l, rows].astype(F32)
            gr = dy * self.row(l, g)
            m1 = jnp.mean(gr, axis=1, keepdims=True)
            m2 = jnp.mean(gr * n, axis=1, keepdims=True)
            dx = self.sc[rows, 2 * l + k:2 * l + k + 1] * (gr - m1 - n * m2)
            self.tmp[rows] = dx
            lw = dx.astype(BF16)
            low[rows] = lw
            return (c[0] + fold(dy * n), c[1] + fold(dy), c[2] + fold(lw.astype(F32)))
        z = jnp.zeros((8, D), F32)
        a, s, t = lax.fori_loop(0, T // 128, body, (z, z, z), unroll=4)
        for r, x in ((g, a), (b, s), (low_row, t)):
            self.vec[l, r:r + 1, :] = jnp.sum(x, axis=0, keepdims=True)

    def emit(self, l, b, left, right):
        slot = self.free_slot()
        self.stage[slot] = dot(left, right).astype(BF16)
        self.emit_out(l, b, slot)
        self.point("e%d" % b)

    def top_back(self, l, src):
        self.norm_back(l, src, self.n2, 1, G2, S2, self.og, SB)
        for b in range(4):
            self.emit(l, b, self.act[:, b * D:(b + 1) * D].T, self.og[...])

    def inner_back(self, l, done_inner, need_expand):
        def body(j):
            cols = tile(j, D)
            g = (dot_nt(self.og[...], self.ws[cols, :]) * gelu_slope(self.inner[:, cols].astype(F32))).astype(BF16)
            self.ig[:, cols] = g
            self.vec[l, pl.ds(EB + j, 1), :] = jnp.sum(g.astype(F32), axis=0, keepdims=True)
        loop(4, body)
        done_inner()
        self.point("inner")
        self.xt[...] = self.fl[l].T
        for b in range(4):
            self.emit(l, 4 + b, self.xt[...], self.ig[:, b * D:(b + 1) * D])
        need_expand()
        self.tmp[...] += dot_nt(self.ig[...], self.we[...])
        self.point("first")

    def mid_back(self, l):
        self.norm_back(l, lambda rows: self.tmp[rows], self.n1, 0, G1, S1, self.og, MB)
        self.emit(l, 8, self.att[l].T, self.og[...])
        self.ag[...] = dot_nt(self.og[...], self.w4[3]).astype(BF16)
        self.point("mixer")

    def attend_back(self, l):
        lane = lax.broadcasted_iota(jnp.int32, (1, PAIR), 1)

        def body(hp):
            cols = tile(hp, PAIR)
            q2, k2, v2 = self.q[:, cols], self.k[:, cols], self.v[:, cols]
            da = self.ag[:, cols]
            vv = jnp.concatenate([jnp.where(lane < 64, v2, BF16(0)), jnp.where(lane >= 64, v2, BF16(0))], axis=0)
            both = dot_nt(da, vv)
            ds, inv = [], []
            for e in (0, 1):
                x = self.probs[2 * hp + e].astype(F32)
                t = x * both[:, e * T:(e + 1) * T]
                i = 1.0 / jnp.sum(x, axis=1, keepdims=True)
                ds.append((t - x * (jnp.sum(t, axis=1, keepdims=True) * i)).astype(BF16))
                inv.append(i)
            inv = jnp.where(lane < 64, inv[0], inv[1])
            qt = (q2.astype(F32) * inv).astype(BF16).T
            dat = (da.astype(F32) * inv).astype(BF16).T
            dq = dot(ds[0], jnp.where(lane < 64, k2, BF16(0))) + dot(ds[1], jnp.where(lane >= 64, k2, BF16(0)))
            dq = (dq * (inv * 0.125)).astype(BF16)
            dk = jnp.concatenate([dot(qt[64 * e:64 * e + 64], ds[e]) for e in (0, 1)], axis=0).astype(BF16).T
            dv = jnp.concatenate([dot(dat[64 * e:64 * e + 64], self.probs[2 * hp + e]) for e in (0, 1)], axis=0).astype(BF16).T
            for m, r in ((0, dq), (1, dk), (2, dv)):
                self.ig[:, pl.ds(pl.multiple_of(m * D + hp * PAIR, PAIR), PAIR)] = r
            for r, x in ((QB, dq), (VB, dv)):
                self.vec[l, r:r + 1, cols] = jnp.sum(x.astype(F32), axis=0, keepdims=True)
        loop(3, body)
        self.point("heads")
        loop(3, lambda i: body(i + 3))
        self.point("attend")

    def low_back(self, l, out):
        self.xt[...] = self.h[l].T
        for m in range(3):
            self.emit(l, 9 + m, self.xt[...], self.ig[:, m * D:(m + 1) * D])
        x = self.tmp[...]
        for m in range(3):
            x = x + dot_nt(self.ig[:, m * D:(m + 1) * D], self.w4[m])
        out[...] = x.astype(BF16)
        self.point("end")


def net_scratch():
    return dict(
        par=pltpu.VMEM((2, 16, D), F32), vec=pltpu.VMEM((2, 16, D), F32), mask=pltpu.VMEM((8, T), F32),
        h=pltpu.VMEM((2, T, D), BF16), q=pltpu.VMEM((T, D), BF16), k=pltpu.VMEM((T, D), BF16), v=pltpu.VMEM((T, D), BF16),
        att=pltpu.VMEM((2, T, D), BF16), n1=pltpu.VMEM((2, T, D), BF16), n2=pltpu.VMEM((2, T, D), BF16), fl=pltpu.VMEM((2, T, D), BF16),
        sc=pltpu.VMEM((T, 4), F32),
        probs=pltpu.VMEM((HEADS, T, T), BF16), inner=pltpu.VMEM((T, FF), BF16), act=pltpu.VMEM((T, FF), BF16),
        tmp=pltpu.VMEM((T, D), F32), og=pltpu.VMEM((T, D), BF16), ag=pltpu.VMEM((T, D), BF16), ig=pltpu.VMEM((T, FF), BF16),
        xt=pltpu.VMEM((D, T), BF16), gin=pltpu.VMEM((T, D), BF16), stage=pltpu.VMEM((SLOTS, D, D), BF16),
    )


MESH = pl.DeviceIdType.MESH
NB = 12
LEG = NB
NP = 2 * LEG
BLK = 768
PART = 384
COL = 384
HALF = 192
CH = 48
XS, RS, ZS, FS = 2, 2, 5, 6


def when(cond, fn):
    if isinstance(cond, bool):
        if cond:
            fn()
    else:
        pl.when(cond)(fn)


def coords():
    s = lax.axis_index("section")
    b = lax.axis_index("batch")
    return s, b // 4, (b // 2) % 2, b % 2


def dev(s, z, y, x):
    return (s, z * 4 + y * 2 + x)


def pair_place(l, b):
    return (1 - l) * (NB // 2) + b // 2


class Comm:
    def __init__(self, refs):
        self.__dict__.update(refs)
        s, z, y, x = coords()
        self.s, self.p = s, z
        self.core = dev(1 - s, z, y, x)
        xn, yn = dev(s, z, y, 1 - x), dev(s, z, 1 - y, x)
        self.cross = (dev(1 - s, z, y, 1 - x), dev(1 - s, z, 1 - y, x))
        self.u = (x, y)
        self.w = (y, x)
        self.n1 = (xn, yn)
        self.n3 = (yn, xn)
        self.up = dev(s, jnp.minimum(z + 1, 3), y, x)
        self.dn = dev(s, jnp.maximum(z - 1, 0), y, x)

    def barrier(self):
        bar = pltpu.get_barrier_semaphore()
        for d in (self.core, *self.n1, *self.cross):
            pl.semaphore_signal(bar, inc=1, device_id=d, device_id_type=MESH)

        @pl.when(self.p < 3)
        def _():
            pl.semaphore_signal(bar, inc=1, device_id=self.up, device_id_type=MESH)

        @pl.when(self.p > 0)
        def _():
            pl.semaphore_signal(bar, inc=1, device_id=self.dn, device_id_type=MESH)
        pl.semaphore_wait(bar, 6 + self.p * (3 - self.p) // 2)

    def slot_of(self, b):
        l = 1 - b // LEG
        mine = l * self.s + (1 - l) * (1 - self.s)
        pair = lax.rem(b, LEG) // 2
        return mine * (2 * pair + self.s) + (1 - mine) * (NB + pair)

    def remote(self, src, dst, ss, rs, d):
        return pltpu.make_async_remote_copy(src_ref=src, dst_ref=dst, send_sem=ss, recv_sem=rs, device_id=d, device_id_type=MESH)

    def prt_copy(self, src, i):
        return self.remote(src, self.prt.at[i], self.prt_s.at[i], self.prt_r.at[i], self.core)

    def loads(self, st, b):
        rows, cols = pl.ds(pl.multiple_of(lax.rem(b, 2) * PART, PART), PART), pl.ds(st * COL, COL)
        return (
            pltpu.make_async_copy(self.acc.at[b // 2, rows, cols], self.lda.at[st], self.ld_sem.at[st, 0]),
            pltpu.make_async_copy(self.prt.at[b // 2, rows, cols], self.ldp.at[st], self.ld_sem.at[st, 1]),
        )

    def s0(self, b):
        when(lax.rem(b, 2) == 0 if not isinstance(b, int) else b % 2 == 0, lambda: self.prt_copy(self.prt.at[b // 2], b // 2).wait_recv())
        for st in (0, 1):
            for c in self.loads(st, b):
                c.start()

    def r1_copy(self, st, b):
        sl = lax.rem(b, RS)
        return self.remote(self.x1.at[st, lax.rem(b, XS)], self.r1.at[st, sl], self.r1_s.at[st, sl], self.r1_r.at[st, sl], self.n1[st])

    def s1(self, b):
        for st in (0, 1):
            for c in self.loads(st, b):
                c.wait()
            oth = pl.ds(pl.multiple_of((1 - self.u[st]) * HALF, HALF), HALF)
            own = pl.ds(pl.multiple_of(self.u[st] * HALF, HALF), HALF)
            self.x1[st, lax.rem(b, XS)] = self.lda[st, oth] + self.ldp[st, oth]
            self.r1_copy(st, b).start()
            self.zbuf[st, lax.rem(b, ZS)] = self.lda[st, own] + self.ldp[st, own]

    def zsend(self, st, b, lo, hi, up):
        zs, zb = lax.rem(b, 4), lax.rem(b, ZS)
        if up:
            return self.remote(self.zbuf.at[st, zb, pl.ds(lo, hi - lo)], self.ru.at[st, lax.rem(b, 3), pl.ds(lo - CH, hi - lo)],
                               self.ru_s.at[st, zs], self.ru_r.at[st, zs], self.up)
        return self.remote(self.zbuf.at[st, zb, pl.ds(lo, hi - lo)], self.rd.at[st, lax.rem(b, 3), pl.ds(lo, hi - lo)],
                           self.rd_s.at[st, zs], self.rd_r.at[st, zs], self.dn)

    def zadd(self, st, b, lo, hi, up):
        zs = lax.rem(b, ZS)
        self.zsend(st, b, lo, hi, up).wait_recv()
        if up:
            self.zbuf[st, zs, lo:hi] += self.ru[st, lax.rem(b, 3), lo - CH:hi - CH]
        else:
            self.zbuf[st, zs, lo:hi] += self.rd[st, lax.rem(b, 3), lo:hi]

    def s2(self, b):
        for st in (0, 1):
            self.r1_copy(st, b).wait()
            self.zbuf[st, lax.rem(b, ZS)] += self.r1[st, lax.rem(b, RS)]
            pl.when(self.p == 0)(lambda: self.zsend(st, b, CH, 4 * CH, True).start())
            pl.when(self.p == 3)(lambda: self.zsend(st, b, 0, 3 * CH, False).start())

    def s3(self, b):
        for st in (0, 1):
            @pl.when(self.p == 1)
            def _():
                self.zadd(st, b, CH, 4 * CH, True)
                self.zsend(st, b, 2 * CH, 4 * CH, True).start()

            @pl.when(self.p == 2)
            def _():
                self.zadd(st, b, 0, 3 * CH, False)
                self.zsend(st, b, 0, 2 * CH, False).start()

    def s4(self, b):
        for st in (0, 1):
            @pl.when(self.p == 2)
            def _():
                self.zadd(st, b, 2 * CH, 4 * CH, True)
                self.zsend(st, b, 3 * CH, 4 * CH, True).start()

            @pl.when(self.p == 1)
            def _():
                self.zadd(st, b, 0, 2 * CH, False)
                self.zsend(st, b, 0, CH, False).start()

    def r3_copy(self, st, b):
        sl = lax.rem(b, 2)
        rows = pl.ds(pl.multiple_of(self.p * CH, CH), CH)
        return self.remote(self.zbuf.at[st, lax.rem(b, ZS), rows], self.r3.at[st, sl], self.r3_s.at[st, sl], self.r3_r.at[st, sl], self.n3[st])

    def s5(self, b):
        for st in (0, 1):
            pl.when(self.p == 0)(lambda: self.zadd(st, b, 0, CH, False))
            pl.when(self.p == 3)(lambda: self.zadd(st, b, 3 * CH, 4 * CH, True))
            self.r3_copy(st, b).start()

    def res_at(self, st, b, c):
        rows = pl.ds(pl.multiple_of(lax.rem(b, 2) * PART + self.u[st] * HALF + c * CH, CH), CH)
        return self.pool.at[self.slot_of(b), rows, pl.ds(st * COL, COL)]

    def ag_copy(self, st, b, c, d, src=None):
        here = self.res_at(st, b, c)
        to, sem = ((self.up, self.zr), (self.dn, self.zr), (self.n1[st], self.xr))[d]
        return self.remote(here if src is None else src, here, self.ag_s.at[st, d, c, lax.rem(b, 4)], sem.at[st, b, c], to)

    def own_copy(self, st, b):
        return pltpu.make_async_copy(self.fin.at[st, lax.rem(b, FS)], self.res_at(st, b, self.p), self.fin_s.at[st, lax.rem(b, 4)])

    def spread(self, st, b, c, up, down, src=None):
        if up:
            pl.when(self.p < 3)(lambda: self.ag_copy(st, b, c, 0, src).start())
        if down:
            pl.when(self.p > 0)(lambda: self.ag_copy(st, b, c, 1, src).start())
        self.ag_copy(st, b, c, 2, src).start()

    def s6(self, b):
        for st in (0, 1):
            self.r3_copy(st, b).wait()
            rows = pl.ds(pl.multiple_of(self.p * CH, CH), CH)
            fin = self.fin.at[st, lax.rem(b, FS)]
            fin[...] = self.zbuf[st, lax.rem(b, ZS), rows] + self.r3[st, lax.rem(b, 2)]
            self.spread(st, b, self.p, True, True, fin)
            self.own_copy(st, b).start()
            pl.when(self.p == 0)(lambda: self.zsend(st, b, CH, 4 * CH, True).wait_send())
            pl.when(self.p == 3)(lambda: self.zsend(st, b, 0, 3 * CH, False).wait_send())

            @pl.when(self.p == 1)
            def _():
                self.zsend(st, b, 2 * CH, 4 * CH, True).wait_send()
                self.zsend(st, b, 0, CH, False).wait_send()

            @pl.when(self.p == 2)
            def _():
                self.zsend(st, b, 0, 2 * CH, False).wait_send()
                self.zsend(st, b, 3 * CH, 4 * CH, True).wait_send()

    def hop(self, k, b):
        for st in (0, 1):
            @pl.when(self.p >= k)
            def _():
                self.ag_copy(st, b, self.p - k, 0).wait_recv()
                self.spread(st, b, self.p - k, True, False)

            @pl.when(self.p <= 3 - k)
            def _():
                self.ag_copy(st, b, self.p + k, 1).wait_recv()
                self.spread(st, b, self.p + k, False, True)

    def s7(self, b):
        self.hop(1, b)

    def s8(self, b):
        self.hop(2, b)

    def s9(self, b):
        self.hop(3, b)

    def s10(self, b):
        for st in (0, 1):
            self.own_copy(st, b).wait()
            for c in range(4):
                got = self.ag_copy(st, b, c, 2)
                got.wait_send()
                got.wait_recv()
                pl.when((self.p < 3) & (self.p >= c))(lambda: self.ag_copy(st, b, c, 0).wait_send())
                pl.when((self.p > 0) & (self.p <= c))(lambda: self.ag_copy(st, b, c, 1).wait_send())
        pair = lax.rem(b, LEG) // 2
        pl.when((1 - b // LEG != self.s) & (lax.rem(b, 2) == 1))(lambda: self.home(pair).start())

    stages = ("s0", "s1", "s2", "s3", "s4", "s5", "s6", "s7", "s8", "s9", "s10")

    def home(self, pair):
        return self.remote(self.pool.at[NB + pair], self.pool.at[2 * pair + self.s], self.h_s.at[pair], self.h_r.at[pair], self.core)

    def keep_copy(self, b):
        if b < 4:
            to = self.ws.at[pl.ds(b * BLK, BLK)]
        elif b < 8:
            to = self.we.at[:, pl.ds((b - 4) * BLK, BLK)]
        else:
            to = self.w4.at[b - 8]
        return pltpu.make_async_copy(self.pool.at[b], to, self.k_s.at[b])

    def keep(self, pair):
        self.home(pair).wait_recv()
        for b in (2 * pair, 2 * pair + 1):
            self.keep_copy(b).start()

    def finish(self):
        for pair in range(NB // 2):
            self.home(pair).wait_send()
        for b in range(NB):
            self.keep_copy(b).wait()

    def tick(self, t):
        for k in reversed(range(len(self.stages))):
            b = t - k
            when(0 <= b < NP if isinstance(b, int) else (b >= 0) & (b < NP), lambda: getattr(self, self.stages[k])(b))

    def vec_copy(self, k):
        s, z, y, x = coords()
        odd = lax.rem(z, 2)
        to = (self.core, dev(s, z, y, 1 - x), dev(s, z, 1 - y, x), dev(s, z + 1 - 2 * odd, y, x), dev(s, jnp.clip(3 - z, 1, 2), y, x),
              dev(s, jnp.where(z == 1, 0, 3), y, x))[k]
        src = self.vec.at[1 - s] if k == 0 else self.vcur.at[(k - 1) % 2]
        return self.remote(src, self.vrecv.at[k], self.v_s.at[k], self.v_r.at[k], to)

    def vec_step(self, k):
        inner = (self.p == 1) | (self.p == 2)
        if k < 4:
            self.vec_copy(k).wait()
            before = self.vec[self.s] if k == 0 else self.vcur[(k - 1) % 2]
            self.vcur[k % 2] = before + self.vrecv[k]
            if k < 3:
                self.vec_copy(k + 1).start()
            else:
                pl.when(inner)(lambda: self.vec_copy(4).start())
        elif k == 4:
            @pl.when(inner)
            def _():
                self.vec_copy(4).wait()
                self.vcur[0] = self.vcur[1] + self.vrecv[4]
                self.vec_copy(5).start()
        else:
            pl.when(inner)(lambda: self.vec_copy(5).wait_send())

            @pl.when((self.p == 0) | (self.p == 3))
            def _():
                self.vec_copy(5).wait_recv()
                self.vcur[0] = self.vrecv[5]


def comm_scratch():
    bf = jnp.bfloat16
    dma = pltpu.SemaphoreType.DMA
    return dict(
        lda=pltpu.VMEM((2, PART, COL), bf), x1=pltpu.VMEM((2, XS, HALF, COL), bf), ldp=pltpu.VMEM((2, PART, COL), bf),
        r1=pltpu.VMEM((2, RS, HALF, COL), bf), zbuf=pltpu.VMEM((2, ZS, HALF, COL), bf),
        ru=pltpu.VMEM((2, 3, 3 * CH, COL), bf), rd=pltpu.VMEM((2, 3, 3 * CH, COL), bf),
        r3=pltpu.VMEM((2, 2, CH, COL), bf), fin=pltpu.VMEM((2, FS, CH, COL), bf),
        vcur=pltpu.VMEM((2, 16, BLK), jnp.float32), vrecv=pltpu.VMEM((6, 16, BLK), jnp.float32),
        prt_s=dma((NB,)), prt_r=dma((NB,)), h_s=dma((NB // 2,)), h_r=dma((NB // 2,)), k_s=dma((NB,)), ld_sem=dma((2, 2)), r1_s=dma((2, RS)), r1_r=dma((2, RS)),
        ru_s=dma((2, 4)), ru_r=dma((2, 4)), rd_s=dma((2, 4)), rd_r=dma((2, 4)), r3_s=dma((2, 2)), r3_r=dma((2, 2)),
        ag_s=dma((2, 3, 4, 4)), fin_s=dma((2, 4)), zr=dma((2, NP, 4)), xr=dma((2, NP, 4)), v_s=dma((6,)), v_r=dma((6,)),
    )


def scoped(name, fn, *args):
    with jax.named_scope(name):
        fn(*args)


class Program(Net):
    def __init__(self, refs, chips):
        super().__init__(refs)
        self.chips = chips
        self.s = lax.axis_index("section")
        self.core = (1 - self.s, lax.axis_index("batch"))
        self.comm = Comm(refs) if chips == 16 else None
        self.sent = []
        self.ticks = 0
        self.plan = {}

    def here(self, l, yes, no):
        pl.when(self.s == l)(yes)
        pl.when(self.s != l)(no)

    def remote(self, src, dst, ss, rs):
        return pltpu.make_async_remote_copy(src_ref=src, dst_ref=dst, send_sem=ss, recv_sem=rs, device_id=self.core, device_id_type=MESH)

    def barrier(self):
        if self.comm:
            self.comm.barrier()
        else:
            bar = pltpu.get_barrier_semaphore()
            pl.semaphore_signal(bar, inc=1, device_id=self.core, device_id_type=MESH)
            pl.semaphore_wait(bar, 1)

    def swap(self, m):
        return self.remote(self.own[m], self.other[m], self.wx_s.at[m], self.wx_r.at[m])

    def swap_par(self):
        return self.remote(self.par.at[self.s], self.par.at[self.s], self.wx_s.at[6], self.wx_r.at[6])

    def held(self, m):
        return self.w4.at[m] if m < 4 else (self.we, self.ws)[m - 4]

    def first_refs(self, m):
        if m < 5:
            return self.own[m], self.held(m)
        rows = (pl.ds(0, FF // 2), pl.ds(FF // 2, FF // 4), pl.ds(3 * FF // 4, FF // 4))[m - 5]
        return self.own[5].at[rows], self.ws.at[rows]

    def direct(self, m):
        to = self.comm.cross[m - 6] if self.comm and m > 5 else self.core
        src, dst = self.first_refs(m)
        return pltpu.make_async_remote_copy(src_ref=src, dst_ref=dst, send_sem=self.dx_s.at[m], recv_sem=self.dx_r.at[m], device_id=to,
                                            device_id_type=MESH)

    def first_near(self, m):
        return pltpu.make_async_copy(*self.first_refs(m), self.w_sem.at[m])

    def near(self, m):
        return pltpu.make_async_copy(self.own[m], self.held(m), self.w_sem.at[m])

    def wait_first(self, m):
        for i in (m,) if m < 6 else (6, 7):
            self.here(0, lambda: self.first_near(i).wait(), lambda: self.direct(i).wait_recv())

    def load(self, l, m):
        def theirs():
            self.swap(m).wait_recv()
            pltpu.make_async_copy(self.other[m], self.held(m), self.w_sem.at[m]).start()
        self.here(l, lambda: self.near(m).start(), theirs)

    def wait_load(self, m):
        self.near(m).wait()

    def aside(self, k, out):
        a, b = (self.probs, self.inner, self.act, self.q, self.k, self.v)[k], self.sp[k]
        return pltpu.make_async_copy(*((a, b) if out else (b, a)), self.sp_sem.at[k])

    def rows_near(self, k, l, src):
        return pltpu.make_async_copy(src, self.rows_at(k), self.ro_s.at[k, l])

    def rows_far(self, k, l, src):
        return self.remote(src, self.rows_at(k), self.ro_s.at[k, l], self.ro_r.at[k])

    def rows_at(self, k):
        return (self.lo, self.gi)[k].at[pl.ds(pl.multiple_of(self.s * T, T), T)]

    def put_rows(self, k, l, src):
        self.here(l, lambda: self.rows_near(k, l, src).start(), lambda: self.rows_far(k, l, src).start())

    def wait_rows(self, k, l, src):
        self.here(l, lambda: self.rows_near(k, l, src).wait(), lambda: self.rows_far(k, l, src).wait_send())

    def out_near(self, i, slot):
        return pltpu.make_async_copy(self.stage.at[slot], self.acc.at[i], self.st_sem.at[slot])

    def out_far(self, i, slot):
        return self.remote(self.stage.at[slot], self.prt.at[i], self.st_sem.at[slot], self.prt_r.at[i])

    def free_slot(self):
        if len(self.sent) < SLOTS:
            return len(self.sent)
        i, has, slot, done = self.sent[-SLOTS]
        if not done:
            self.settle(i)
        pl.when(self.s != has)(lambda: self.out_far(i, slot).wait_send())
        return slot

    def emit_out(self, l, b, slot):
        i = pair_place(l, b)
        self.here(b % 2, lambda: self.out_near(i, slot).start(), lambda: self.out_far(i, slot).start())
        self.sent.append([i, b % 2, slot, False])

    def settle(self, upto):
        for entry in self.sent:
            if entry[0] <= upto and not entry[3]:
                entry[3] = True
                pl.when(self.s == entry[1])(lambda: self.out_near(entry[0], entry[2]).wait())

    def point(self, name):
        if self.comm is None:
            return
        for _ in range(self.plan.get((self.layer, name), 0)):
            assert self.ticks >= NP or len(self.sent) >= 2 * (self.ticks // 2 + 1)
            self.settle(self.ticks // 2)
            scoped("tick", self.comm.tick, self.ticks)
            self.ticks += 1

    def forward(self, l, low):
        self.layer = l
        ready = self.wait_first if l == 0 else self.wait_load
        if l == 1:
            for k in (3, 4, 5):
                self.aside(k, True).wait()
        scoped("qkv", self.qkv, l, ready)
        if l == 1:
            self.aside(0, True).wait()
        scoped("attend", self.attend, l)
        if l == 1:
            self.load(1, 5)
        if l == 0:
            for m in range(3):
                self.load(1, m)
            for k in (3, 4, 5, 0):
                self.aside(k, True).start()
        ready(3)
        scoped("mix", self.mix, l)
        if l == 0:
            self.load(1, 3)
        else:
            self.aside(1, True).wait()
            self.aside(2, True).wait()
        ready(4)
        scoped("expand", self.expand, l)
        if l == 0:
            self.load(1, 4)
            self.aside(1, True).start()
            self.aside(2, True).start()
        scoped("shrink", self.shrink, l, low, ready)

    def push(self, *ms):
        @pl.when(self.s == 0)
        def _():
            for m in ms:
                self.swap(m).start()

    def backward(self, l):
        self.layer = l
        again = l == 1
        if not again:
            self.aside(2, False).wait()
        scoped("top_back", self.top_back, l, lambda rows: self.gin[rows].astype(F32))
        if again:
            self.aside(2, False).start()
        else:
            self.load(0, 3)
            for m in range(3):
                self.load(0, m)
            self.aside(1, False).wait()
            self.wait_load(5)
        scoped("inner_back", self.inner_back, l, lambda: again and self.aside(1, False).start(), lambda: again or self.wait_load(4))
        if again:
            self.push(5, 4)
            self.wait_rows(0, 1, self.ag)
        else:
            self.wait_load(3)
        scoped("mid_back", self.mid_back, l)
        if not again:
            for k in (0, 3, 4, 5):
                self.aside(k, False).wait()
        scoped("attend_back", self.attend_back, l)
        if again:
            self.push(3, 0, 1, 2)
            for k in (0, 3, 4, 5):
                self.aside(k, False).start()
        else:
            for m in range(3):
                self.wait_load(m)
            self.wait_rows(1, 1, self.gin)
        scoped("low_back", self.low_back, l, self.gin)
        if again:
            self.load(0, 5)
            self.load(0, 4)
        self.put_rows(1, l, self.gin)

    def run(self):
        s = self.s
        rows = pl.ds(pl.multiple_of(s * T, T), T)
        first = (pltpu.make_async_copy(self.tokens.at[rows], self.h.at[0], self.in_sem.at[0]),
                 pltpu.make_async_copy(self.cotangent.at[rows], self.gin, self.in_sem.at[1]))
        first[0].start()
        for m in range(8):
            pl.when(s == 0)(lambda: self.first_near(m).start())
        first[1].start()
        for r, ref in enumerate(self.small[:8]):
            self.par[s, r:r + 1, :] = ref[...]
        for j in range(4):
            self.par[s, EB + j:EB + j + 1, :] = self.small[8][:, j * D:(j + 1) * D]
        self.barrier()

        @pl.when(s == 0)
        def _():
            self.direct(0).start()
            self.swap_par().start()
            for m in (6, 7, 1, 2, 3, 4, 5):
                self.direct(m).start()

        @pl.when(s == 1)
        def _():
            self.swap_par().start()
            for m in range(6):
                self.swap(m).start()
        self.vec[...] = jnp.zeros_like(self.vec)
        self.labels(jnp.where(s == 0, self.ids[0:4, :], self.ids[4:8, :]))
        for c in first:
            c.wait()
        pl.when(s == 1)(lambda: self.swap_par().wait_recv())
        self.forward(0, self.h.at[1])
        self.put_rows(0, 0, self.h.at[1])
        pl.when(s == 0)(lambda: self.swap_par().wait_recv())
        self.forward(1, self.ag)
        self.put_rows(0, 1, self.ag)
        self.backward(1)
        self.point("done")
        self.backward(0)
        self.settle(NB)
        for i, has, slot, _ in self.sent[-SLOTS:]:
            pl.when(s != has)(lambda: self.out_far(i, slot).wait_send())
        if self.comm:
            self.comm.vec_copy(0).start()

            def step(t, c):
                scoped("tick", self.comm.tick, t)
                for k in range(6):
                    pl.when(t == VEC_TICK + k)(functools.partial(self.comm.vec_step, k))
                for k in range(NB // 2 - 1):
                    pl.when(t == LEG + len(Comm.stages) + 2 * k + 1)(functools.partial(self.comm.keep, k))
                return c
            lax.fori_loop(self.ticks, TICKS, step, 0)
            self.vec_out[...] = self.comm.vcur[0]
            self.comm.keep(NB // 2 - 1)
            self.comm.finish()
        else:
            for i in range(NB):
                self.out_far(i, 0).wait_recv()
            self.vec_out[...] = self.vec[...]
        for m in range(6):
            self.swap(m).wait_send()
        for m in range(8):
            pl.when(s == 0)(lambda: self.direct(m).wait_send())
        self.swap_par().wait_send()
        self.wait_rows(0, 0, self.h.at[1])
        self.wait_rows(1, 0, self.gin)
        for k in (0, 1):
            self.rows_far(k, 0, self.gin).wait_recv()


def kernel(chips, names, plan, *refs):
    tokens, cotangent, ids = refs[0:3]
    weights = refs[3:9]
    small = refs[9:18]
    lo, gi, pool, vec_out, acc, prt, o4, oe, os_ = refs[18:27]
    named = dict(zip(names, refs[33:]))
    named.update(tokens=tokens, cotangent=cotangent, ids=ids, own=[w.at[0] for w in weights], small=small, lo=lo, gi=gi, pool=pool,
                 vec_out=vec_out, acc=acc, prt=prt, other=[o4.at[0], o4.at[1], o4.at[2], o4.at[3], oe, os_],
                 sp=refs[27:33])
    p = Program(named, chips)
    p.plan = plan
    p.run()


TICKS = NP + len(Comm.stages) - 1
VEC_TICK = TICKS - 7
PLAN = {(1, name): 1 for name in ("e1", "e2", "e3", "inner", "e7", "first", "mixer", "heads", "e9", "e11")}
PLAN.update({(0, name): 1 for name in ("e0", "e2", "inner", "e6", "first", "mixer", "heads", "attend", "e9", "e11")})


def both_layers(chips, tokens, cotangent, ids, weights, small):
    S = jax.ShapeDtypeStruct
    dma = pltpu.SemaphoreType.DMA
    sc = net_scratch()
    sc.update(comm_scratch())
    sc.update(wx_s=dma((7,)), wx_r=dma((7,)), dx_s=dma((8,)), dx_r=dma((8,)), w_sem=dma((8,)), sp_sem=dma((6,)), ro_s=dma((2, 2)), ro_r=dma((2,)), st_sem=dma((SLOTS,)),
              in_sem=dma((2,)))
    hbm, vm = pl.BlockSpec(memory_space=pl.ANY), pl.BlockSpec(memory_space=pltpu.VMEM)
    kept = dict(w4=pltpu.VMEM((4, D, D), BF16), we=pltpu.VMEM((D, FF), BF16), ws=pltpu.VMEM((FF, D), BF16))
    here = chips == 16
    if not here:
        sc.update(kept)
    mem, rows_spec = (pltpu.VMEM, vm) if here else (S, hbm)
    rows = mem((2 * T, D), BF16)
    out = pl.pallas_call(
        functools.partial(kernel, chips, (tuple(kept) if here else ()) + tuple(sc), PLAN),
        out_shape=(rows, rows, S((NB + NB // 2, D, D), BF16), mem((16, D) if here else (2, 16, D), F32), S((NB, D, D), BF16),
                   S((NB, D, D), BF16), S((4, D, D), BF16), S((D, FF), BF16), S((FF, D), BF16), S((HEADS, T, T), BF16), S((T, FF), BF16),
                   S((T, FF), BF16)) + (S((T, D), BF16),) * 3 + (tuple(kept.values()) if here else ()),
        in_specs=[hbm, hbm, vm] + [hbm] * 6 + [vm] * 9,
        out_specs=(rows_spec, rows_spec, hbm, vm) + (hbm,) * 11 + ((vm,) * 3 if here else ()),
        scratch_shapes=list(sc.values()),
        compiler_params=pltpu.CompilerParams(collective_id=0, has_side_effects=True, vmem_limit_bytes=(47 if here else 63) * 2**20),
    )(tokens, cotangent, ids, *weights, *small)
    return out[:6] + (out[-3:] if here else (None,) * 3)


WROWS, WBUFS = 768, 4


def widen_kernel(rest_in, ex_in, sh_in, vec, lo, gi, sh, ex, mi, q, k, v, lo_out, gi_out, *rest):
    small, (low, wide, in_sem, out_sem, row_buf, row_sem, vec_buf, vec_sem) = rest[:9], rest[9:]
    vec_in = pltpu.make_async_copy(vec, vec_buf, vec_sem)
    rows_in = [pltpu.make_async_copy(a, row_buf.at[i], row_sem.at[i]) for i, a in enumerate((lo, gi))]
    rows_out = [pltpu.make_async_copy(row_buf.at[i], a.at[0], row_sem.at[i]) for i, a in enumerate((lo_out, gi_out))]
    per = D // WROWS
    count = NB * per

    def take(i):
        b, r = i // per, (i % per) * WROWS
        if b < 4:
            src = sh_in.at[pl.ds(b * D + r, WROWS)]
        elif b < 8:
            src = ex_in.at[pl.ds(r, WROWS), pl.ds((b - 4) * D, D)]
        else:
            src = rest_in.at[b - 8, pl.ds(r, WROWS)]
        return pltpu.make_async_copy(src, low.at[i % WBUFS], in_sem.at[i % WBUFS])

    def put(i):
        b, r = i // per, (i % per) * WROWS
        if b < 4:
            to = sh.at[0, pl.ds(b * D + r, WROWS)]
        elif b < 8:
            to = ex.at[0, pl.ds(r, WROWS), pl.ds((b - 4) * D, D)]
        else:
            to = (mi, q, k, v)[b - 8].at[0, pl.ds(r, WROWS)]
        return pltpu.make_async_copy(wide.at[i % WBUFS], to, out_sem.at[i % WBUFS])

    for i in range(WBUFS):
        take(i).start()
    vec_in.start()
    for c in rows_in:
        c.start()
    vec_in.wait()
    for r in range(8):
        small[r][...] = vec_buf[r:r + 1, :]
    for j in range(4):
        small[8][:, j * D:(j + 1) * D] = vec_buf[EB + j:EB + j + 1, :]
    for i in range(count):
        take(i).wait()
        if i >= WBUFS:
            put(i - WBUFS).wait()

        def convert(j, c):
            rows = tile(j, 32)
            wide[i % WBUFS, rows] = low[i % WBUFS, rows].astype(F32)
            return c
        lax.fori_loop(0, WROWS // 32, convert, 0, unroll=4)
        put(i).start()
        if i == 1:
            for a, b in zip(rows_in, rows_out):
                a.wait()
                b.start()
        if i + WBUFS < count:
            take(i + WBUFS).start()
    for i in range(count - WBUFS, count):
        put(i).wait()
    for c in rows_out:
        c.wait()


def widen(rest_in, ex_in, sh_in, vec, lo, gi):
    S = jax.ShapeDtypeStruct
    hbm, vm = pl.BlockSpec(memory_space=pl.ANY), pl.BlockSpec(memory_space=pltpu.VMEM)
    square, row = S((1, D, D), F32), S((1, D), F32)
    return pl.pallas_call(
        widen_kernel,
        out_shape=(S((1, FF, D), F32), S((1, D, FF), F32), square, square, square, square, S((1, 2 * T, D), BF16), S((1, 2 * T, D), BF16)) + (row,) * 8 + (S((1, FF), F32),),
        in_specs=[hbm] * 6, out_specs=(hbm,) * 8 + (vm,) * 9,
        scratch_shapes=[pltpu.VMEM((WBUFS, WROWS, D), BF16), pltpu.VMEM((WBUFS, WROWS, D), F32),
                        pltpu.SemaphoreType.DMA((WBUFS,)), pltpu.SemaphoreType.DMA((WBUFS,)), pltpu.VMEM((2, 2 * T, D), BF16), pltpu.SemaphoreType.DMA((2,)), pltpu.VMEM((16, D), F32), pltpu.SemaphoreType.DMA],
        compiler_params=pltpu.CompilerParams(vmem_limit_bytes=24 * 2**20),
    )(rest_in, ex_in, sh_in, vec, lo, gi)


def body(tokens, cotangent, sentence_ids, *stored):
    (query_w, query_b, keys_w, value_w, value_b, mixer_w, mixer_b, gain_one, shift_one, expand_w, expand_b, shrink_w, shrink_b, gain_two,
     shift_two) = stored
    chips = lax.axis_size("batch")
    lo, gi, pool, vec, acc, prt, rest, ex, sh = both_layers(
        chips, tokens, cotangent, sentence_ids.reshape(8, PAIR), (query_w, keys_w, value_w, mixer_w, expand_w, shrink_w),
        (query_b, value_b, mixer_b, gain_one, shift_one, shrink_b, gain_two, shift_two, expand_b))
    if chips != 16:
        s = lax.axis_index("section")
        part = acc.astype(F32) + prt.astype(F32)
        part = part.reshape(2, NB // 2, 1, D, D)
        pairs = jnp.where(lax.broadcasted_iota(jnp.int32, (1, 1, 2, 1, 1), 2) == s, part, 0.0)
        both = lax.psum(pairs, ("section", "batch")).reshape(2, NB, D, D)
        pool = lax.dynamic_index_in_dim(both, 1 - s, 0, keepdims=False).astype(BF16)
        sh, ex, rest = pool[:4].reshape(FF, D), pool[4:8].transpose(1, 0, 2).reshape(D, FF), pool[8:]
        vec = lax.dynamic_index_in_dim(lax.psum(vec, ("section", "batch")), s, 0, keepdims=False)
    sh, ex, mi, q, k, v, lo, gi, qb, vb, mb, g1, s1, sb, g2, s2, eb = widen(rest, ex, sh, vec, lo, gi)
    return (lo, gi, q, qb, k, v, vb, mi, mb, g1, s1, ex, eb, sh, sb, g2, s2)


def solution(mesh):
    placed = (
        P("batch", None),
        P("batch", None),
        P("batch"),
        P("section", None, None),
        P("section", None),
        P("section", None, None),
        P("section", None, None),
        P("section", None),
        P("section", None, None),
        P("section", None),
        P("section", None),
        P("section", None),
        P("section", None, None),
        P("section", None),
        P("section", None, None),
        P("section", None),
        P("section", None),
        P("section", None),
    )
    return jax.shard_map(
        body,
        mesh=mesh,
        in_specs=placed,
        out_specs=(
            P("section", "batch", None),
            P("section", "batch", None),
            P("section", None, None),
            P("section", None),
            P("section", None, None),
            P("section", None, None),
            P("section", None),
            P("section", None, None),
            P("section", None),
            P("section", None),
            P("section", None),
            P("section", None, None),
            P("section", None),
            P("section", None, None),
            P("section", None),
            P("section", None),
            P("section", None),
        ),
        check_vma=False,
    )
```

```python
import functools

import jax
import jax.numpy as jnp
from jax import lax
from jax.experimental import pallas as pl
from jax.experimental.pallas import tpu as pltpu
from jax.sharding import PartitionSpec as P

T = 512
D = 768
FF = 3072
HEADS = 12
TILE = 256
PAIR = 128
EPS = 1e-06
SLOTS = 3
F32, BF16 = jnp.float32, jnp.bfloat16
QB, VB, MB, G1, S1, SB, G2, S2, EB = 0, 1, 2, 3, 4, 5, 6, 7, 8


def dot(a, b):
    return jnp.dot(a, b, preferred_element_type=F32)


def dot_nt(a, b):
    return lax.dot_general(a, b, (((1,), (1,)), ((), ())), preferred_element_type=F32)


def tile(j, n=TILE):
    return pl.ds(pl.multiple_of(j * n, n), n)


def loop(n, fn, unroll=1):
    def step(i, c):
        fn(i)
        return c
    lax.fori_loop(0, n, step, 0, unroll=unroll)


def cdf_of(u):
    return 0.5 + 0.5 * lax.erf(u * 0.7071067811865476)


def gelu_slope(u):
    return cdf_of(u) + u * (0.3989422804014327 * jnp.exp2(u * (u * -0.7213475204444817)))


def fold(x):
    return jnp.sum(x.reshape(x.shape[0] // 8, 8, x.shape[1]), axis=0)


class Net:
    def __init__(self, refs):
        self.__dict__.update(refs)

    def row(self, l, r, cols=slice(None)):
        return self.par[l, r:r + 1, cols]

    def load(self, l, m):
        raise NotImplementedError

    def wait_load(self, l, m):
        raise NotImplementedError

    def point(self, name):
        pass

    def labels(self, ids):
        for a in range(4):
            for c in range(4):
                self.mask[a:a + 1, c * PAIR:(c + 1) * PAIR] = jnp.where(ids[c:c + 1, :] == ids[a:a + 1, 0:1], 0.0, -1e9)

    def qkv(self, l, ready):
        for m, out, b in ((0, self.q, QB), (1, self.k, None), (2, self.v, VB)):
            ready(m)
            r = dot(self.h[l], self.w4[m])
            if b is not None:
                r = r + self.row(l, b)
            r = r.astype(BF16)
            out[...] = r * BF16(0.125) if m == 0 else r

    def attend(self, l):
        lane = lax.broadcasted_iota(jnp.int32, (1, PAIR), 1)
        R = 256

        def body(hp):
            cols = tile(hp, PAIR)
            k2, v2 = self.k[:, cols], self.v[:, cols]
            kk = jnp.concatenate([jnp.where(lane < 64, k2, BF16(0)), jnp.where(lane >= 64, k2, BF16(0))], axis=0)
            for r in range(T // R):
                rows = pl.ds(r * R, R)
                both = dot_nt(self.q[rows, cols], kk)
                out = []
                for e in (0, 1):
                    s = both[:, e * T:(e + 1) * T].reshape(R // PAIR, PAIR, T)
                    s = (s + self.mask[r * R // PAIR:(r + 1) * R // PAIR, :][:, None, :]).reshape(R, T)
                    x = jnp.exp(s - jnp.max(s, axis=1, keepdims=True)).astype(BF16)
                    self.probs[2 * hp + e, rows] = x
                    out.append(dot(x, jnp.where(lane < 64 if e == 0 else lane >= 64, v2, BF16(1))))
                total = pltpu.roll(jnp.where(lane < 64, out[1], out[0]), 64, 1)
                self.att[l, rows, cols] = (jnp.where(lane < 64, out[0], out[1]) / total).astype(BF16)
        loop(HEADS // 2, body, 2)

    def norm(self, l, n_ref, k, g, b, low):
        def body(i):
            rows = tile(i, 128)
            x = self.tmp[rows]
            c = x - jnp.mean(x, axis=1, keepdims=True)
            inv = lax.rsqrt(jnp.mean(c * c, axis=1, keepdims=True) + EPS)
            n = c * inv
            n_ref[l, rows] = n.astype(n_ref.dtype)
            self.sc[rows, 2 * l + k:2 * l + k + 1] = inv
            y = n * self.row(l, g) + self.row(l, b)
            self.tmp[rows] = y
            low[rows] = y.astype(BF16)
        loop(T // 128, body, 4)

    def mix(self, l):
        self.tmp[...] = dot(self.att[l], self.w4[3]) + self.row(l, MB) + self.h[l].astype(F32)
        self.norm(l, self.n1, 0, G1, S1, self.fl.at[l])

    def expand(self, l):
        def body(j):
            cols = tile(j, D)
            u = dot(self.fl[l], self.we[:, cols]) + self.par[l, pl.ds(EB + j, 1), :]
            self.act[:, cols] = (u * cdf_of(u)).astype(BF16)
            self.inner[:, cols] = u.astype(BF16)
        loop(4, body)

    def shrink(self, l, low, ready):
        n = FF // 2
        if l == 0:
            ready(5)
            self.tmp[...] += dot(self.act[:, :n], self.ws[:n]) + self.row(l, SB)
            ready(6)
            self.tmp[...] += dot(self.act[:, n:], self.ws[n:])
        else:
            ready(5)
            self.tmp[...] += dot(self.act[...], self.ws[...]) + self.row(l, SB)
        self.norm(l, self.n2, 1, G2, S2, low)

    def norm_back(self, l, src, n_ref, k, g, b, low, low_row):
        def body(i, c):
            rows = tile(i, 128)
            dy = src(rows)
            n = n_ref[l, rows].astype(F32)
            gr = dy * self.row(l, g)
            m1 = jnp.mean(gr, axis=1, keepdims=True)
            m2 = jnp.mean(gr * n, axis=1, keepdims=True)
            dx = self.sc[rows, 2 * l + k:2 * l + k + 1] * (gr - m1 - n * m2)
            self.tmp[rows] = dx
            lw = dx.astype(BF16)
            low[rows] = lw
            return (c[0] + fold(dy * n), c[1] + fold(dy), c[2] + fold(lw.astype(F32)))
        z = jnp.zeros((8, D), F32)
        a, s, t = lax.fori_loop(0, T // 128, body, (z, z, z), unroll=4)
        for r, x in ((g, a), (b, s), (low_row, t)):
            self.vec[l, r:r + 1, :] = jnp.sum(x, axis=0, keepdims=True)

    def emit(self, l, b, left, right):
        slot = self.free_slot()
        self.stage[slot] = dot(left, right).astype(BF16)
        self.emit_out(l, b, slot)
        self.point("e%d" % b)

    def top_back(self, l, src):
        self.norm_back(l, src, self.n2, 1, G2, S2, self.og, SB)
        for b in range(4):
            self.emit(l, b, self.act[:, b * D:(b + 1) * D].T, self.og[...])

    def inner_back(self, l, done_inner, need_expand):
        def body(j):
            cols = tile(j, D)
            g = (dot_nt(self.og[...], self.ws[cols, :]) * gelu_slope(self.inner[:, cols].astype(F32))).astype(BF16)
            self.ig[:, cols] = g
            self.vec[l, pl.ds(EB + j, 1), :] = jnp.sum(g.astype(F32), axis=0, keepdims=True)
        loop(4, body)
        done_inner()
        self.point("inner")
        self.xt[...] = self.fl[l].T
        for b in range(4):
            self.emit(l, 4 + b, self.xt[...], self.ig[:, b * D:(b + 1) * D])
        need_expand()
        self.tmp[...] += dot_nt(self.ig[...], self.we[...])
        self.point("first")

    def mid_back(self, l):
        self.norm_back(l, lambda rows: self.tmp[rows], self.n1, 0, G1, S1, self.og, MB)
        self.emit(l, 8, self.att[l].T, self.og[...])
        self.ag[...] = dot_nt(self.og[...], self.w4[3]).astype(BF16)
        self.point("mixer")

    def attend_back(self, l):
        lane = lax.broadcasted_iota(jnp.int32, (1, PAIR), 1)

        def body(hp):
            cols = tile(hp, PAIR)
            q2, k2, v2 = self.q[:, cols], self.k[:, cols], self.v[:, cols]
            da = self.ag[:, cols]
            vv = jnp.concatenate([jnp.where(lane < 64, v2, BF16(0)), jnp.where(lane >= 64, v2, BF16(0))], axis=0)
            both = dot_nt(da, vv)
            ds, inv = [], []
            for e in (0, 1):
                x = self.probs[2 * hp + e].astype(F32)
                t = x * both[:, e * T:(e + 1) * T]
                i = 1.0 / jnp.sum(x, axis=1, keepdims=True)
                ds.append((t - x * (jnp.sum(t, axis=1, keepdims=True) * i)).astype(BF16))
                inv.append(i)
            inv = jnp.where(lane < 64, inv[0], inv[1])
            qt = (q2.astype(F32) * inv).astype(BF16).T
            dat = (da.astype(F32) * inv).astype(BF16).T
            dq = dot(ds[0], jnp.where(lane < 64, k2, BF16(0))) + dot(ds[1], jnp.where(lane >= 64, k2, BF16(0)))
            dq = (dq * (inv * 0.125)).astype(BF16)
            dk = jnp.concatenate([dot(qt[64 * e:64 * e + 64], ds[e]) for e in (0, 1)], axis=0).astype(BF16).T
            dv = jnp.concatenate([dot(dat[64 * e:64 * e + 64], self.probs[2 * hp + e]) for e in (0, 1)], axis=0).astype(BF16).T
            for m, r in ((0, dq), (1, dk), (2, dv)):
                self.ig[:, pl.ds(pl.multiple_of(m * D + hp * PAIR, PAIR), PAIR)] = r
            for r, x in ((QB, dq), (VB, dv)):
                self.vec[l, r:r + 1, cols] = jnp.sum(x.astype(F32), axis=0, keepdims=True)
        loop(3, body)
        self.point("heads")
        loop(3, lambda i: body(i + 3))
        self.point("attend")

    def low_back(self, l, out):
        self.xt[...] = self.h[l].T
        for m in range(3):
            self.emit(l, 9 + m, self.xt[...], self.ig[:, m * D:(m + 1) * D])
        x = self.tmp[...]
        for m in range(3):
            x = x + dot_nt(self.ig[:, m * D:(m + 1) * D], self.w4[m])
        out[...] = x.astype(BF16)
        self.point("end")


def net_scratch():
    return dict(
        par=pltpu.VMEM((2, 16, D), F32), vec=pltpu.VMEM((2, 16, D), F32), mask=pltpu.VMEM((8, T), F32),
        h=pltpu.VMEM((2, T, D), BF16), q=pltpu.VMEM((T, D), BF16), k=pltpu.VMEM((T, D), BF16), v=pltpu.VMEM((T, D), BF16),
        att=pltpu.VMEM((2, T, D), BF16), n1=pltpu.VMEM((2, T, D), BF16), n2=pltpu.VMEM((2, T, D), BF16), fl=pltpu.VMEM((2, T, D), BF16),
        sc=pltpu.VMEM((T, 4), F32),
        probs=pltpu.VMEM((HEADS, T, T), BF16), inner=pltpu.VMEM((T, FF), BF16), act=pltpu.VMEM((T, FF), BF16),
        tmp=pltpu.VMEM((T, D), F32), og=pltpu.VMEM((T, D), BF16), ag=pltpu.VMEM((T, D), BF16), ig=pltpu.VMEM((T, FF), BF16),
        xt=pltpu.VMEM((D, T), BF16), gin=pltpu.VMEM((T, D), BF16), stage=pltpu.VMEM((SLOTS, D, D), BF16),
    )


MESH = pl.DeviceIdType.MESH
NB = 12
LEG = NB
NP = 2 * LEG
BLK = 768
PART = 384
COL = 384
HALF = 192
CH = 48
XS, RS, ZS, FS = 2, 2, 5, 6


def when(cond, fn):
    if isinstance(cond, bool):
        if cond:
            fn()
    else:
        pl.when(cond)(fn)


def coords():
    s = lax.axis_index("section")
    b = lax.axis_index("batch")
    return s, b // 4, (b // 2) % 2, b % 2


def dev(s, z, y, x):
    return (s, z * 4 + y * 2 + x)


def pair_place(l, b):
    return (1 - l) * (NB // 2) + b // 2


class Comm:
    def __init__(self, refs):
        self.__dict__.update(refs)
        s, z, y, x = coords()
        self.s, self.p = s, z
        self.core = dev(1 - s, z, y, x)
        xn, yn = dev(s, z, y, 1 - x), dev(s, z, 1 - y, x)
        self.cross = (dev(1 - s, z, y, 1 - x), dev(1 - s, z, 1 - y, x))
        self.u = (x, y)
        self.w = (y, x)
        self.n1 = (xn, yn)
        self.n3 = (yn, xn)
        self.up = dev(s, jnp.minimum(z + 1, 3), y, x)
        self.dn = dev(s, jnp.maximum(z - 1, 0), y, x)

    def barrier(self):
        bar = pltpu.get_barrier_semaphore()
        for d in (self.core, *self.n1, *self.cross):
            pl.semaphore_signal(bar, inc=1, device_id=d, device_id_type=MESH)

        @pl.when(self.p < 3)
        def _():
            pl.semaphore_signal(bar, inc=1, device_id=self.up, device_id_type=MESH)

        @pl.when(self.p > 0)
        def _():
            pl.semaphore_signal(bar, inc=1, device_id=self.dn, device_id_type=MESH)
        pl.semaphore_wait(bar, 6 + self.p * (3 - self.p) // 2)

    def slot_of(self, b):
        l = 1 - b // LEG
        mine = l * self.s + (1 - l) * (1 - self.s)
        pair = lax.rem(b, LEG) // 2
        return mine * (2 * pair + self.s) + (1 - mine) * (NB + pair)

    def remote(self, src, dst, ss, rs, d):
        return pltpu.make_async_remote_copy(src_ref=src, dst_ref=dst, send_sem=ss, recv_sem=rs, device_id=d, device_id_type=MESH)

    def prt_copy(self, src, i):
        return self.remote(src, self.prt.at[i], self.prt_s.at[i], self.prt_r.at[i], self.core)

    def loads(self, st, b):
        rows, cols = pl.ds(pl.multiple_of(lax.rem(b, 2) * PART, PART), PART), pl.ds(st * COL, COL)
        return (
            pltpu.make_async_copy(self.acc.at[b // 2, rows, cols], self.lda.at[st], self.ld_sem.at[st, 0]),
            pltpu.make_async_copy(self.prt.at[b // 2, rows, cols], self.ldp.at[st], self.ld_sem.at[st, 1]),
        )

    def s0(self, b):
        when(lax.rem(b, 2) == 0 if not isinstance(b, int) else b % 2 == 0, lambda: self.prt_copy(self.prt.at[b // 2], b // 2).wait_recv())
        for st in (0, 1):
            for c in self.loads(st, b):
                c.start()

    def r1_copy(self, st, b):
        sl = lax.rem(b, RS)
        return self.remote(self.x1.at[st, lax.rem(b, XS)], self.r1.at[st, sl], self.r1_s.at[st, sl], self.r1_r.at[st, sl], self.n1[st])

    def s1(self, b):
        for st in (0, 1):
            for c in self.loads(st, b):
                c.wait()
            oth = pl.ds(pl.multiple_of((1 - self.u[st]) * HALF, HALF), HALF)
            own = pl.ds(pl.multiple_of(self.u[st] * HALF, HALF), HALF)
            self.x1[st, lax.rem(b, XS)] = self.lda[st, oth] + self.ldp[st, oth]
            self.r1_copy(st, b).start()
            self.zbuf[st, lax.rem(b, ZS)] = self.lda[st, own] + self.ldp[st, own]

    def zsend(self, st, b, lo, hi, up):
        zs, zb = lax.rem(b, 4), lax.rem(b, ZS)
        if up:
            return self.remote(self.zbuf.at[st, zb, pl.ds(lo, hi - lo)], self.ru.at[st, lax.rem(b, 3), pl.ds(lo - CH, hi - lo)],
                               self.ru_s.at[st, zs], self.ru_r.at[st, zs], self.up)
        return self.remote(self.zbuf.at[st, zb, pl.ds(lo, hi - lo)], self.rd.at[st, lax.rem(b, 3), pl.ds(lo, hi - lo)],
                           self.rd_s.at[st, zs], self.rd_r.at[st, zs], self.dn)

    def zadd(self, st, b, lo, hi, up):
        zs = lax.rem(b, ZS)
        self.zsend(st, b, lo, hi, up).wait_recv()
        if up:
            self.zbuf[st, zs, lo:hi] += self.ru[st, lax.rem(b, 3), lo - CH:hi - CH]
        else:
            self.zbuf[st, zs, lo:hi] += self.rd[st, lax.rem(b, 3), lo:hi]

    def s2(self, b):
        for st in (0, 1):
            self.r1_copy(st, b).wait()
            self.zbuf[st, lax.rem(b, ZS)] += self.r1[st, lax.rem(b, RS)]
            pl.when(self.p == 0)(lambda: self.zsend(st, b, CH, 4 * CH, True).start())
            pl.when(self.p == 3)(lambda: self.zsend(st, b, 0, 3 * CH, False).start())

    def s3(self, b):
        for st in (0, 1):
            @pl.when(self.p == 1)
            def _():
                self.zadd(st, b, CH, 4 * CH, True)
                self.zsend(st, b, 2 * CH, 4 * CH, True).start()

            @pl.when(self.p == 2)
            def _():
                self.zadd(st, b, 0, 3 * CH, False)
                self.zsend(st, b, 0, 2 * CH, False).start()

    def s4(self, b):
        for st in (0, 1):
            @pl.when(self.p == 2)
            def _():
                self.zadd(st, b, 2 * CH, 4 * CH, True)
                self.zsend(st, b, 3 * CH, 4 * CH, True).start()

            @pl.when(self.p == 1)
            def _():
                self.zadd(st, b, 0, 2 * CH, False)
                self.zsend(st, b, 0, CH, False).start()

    def r3_copy(self, st, b):
        sl = lax.rem(b, 2)
        rows = pl.ds(pl.multiple_of(self.p * CH, CH), CH)
        return self.remote(self.zbuf.at[st, lax.rem(b, ZS), rows], self.r3.at[st, sl], self.r3_s.at[st, sl], self.r3_r.at[st, sl], self.n3[st])

    def s5(self, b):
        for st in (0, 1):
            pl.when(self.p == 0)(lambda: self.zadd(st, b, 0, CH, False))
            pl.when(self.p == 3)(lambda: self.zadd(st, b, 3 * CH, 4 * CH, True))
            self.r3_copy(st, b).start()

    def res_at(self, st, b, c):
        rows = pl.ds(pl.multiple_of(lax.rem(b, 2) * PART + self.u[st] * HALF + c * CH, CH), CH)
        return self.pool.at[self.slot_of(b), rows, pl.ds(st * COL, COL)]

    def ag_copy(self, st, b, c, d, src=None):
        here = self.res_at(st, b, c)
        to, sem = ((self.up, self.zr), (self.dn, self.zr), (self.n1[st], self.xr))[d]
        return self.remote(here if src is None else src, here, self.ag_s.at[st, d, c, lax.rem(b, 4)], sem.at[st, b, c], to)

    def own_copy(self, st, b):
        return pltpu.make_async_copy(self.fin.at[st, lax.rem(b, FS)], self.res_at(st, b, self.p), self.fin_s.at[st, lax.rem(b, 4)])

    def spread(self, st, b, c, up, down, src=None):
        if up:
            pl.when(self.p < 3)(lambda: self.ag_copy(st, b, c, 0, src).start())
        if down:
            pl.when(self.p > 0)(lambda: self.ag_copy(st, b, c, 1, src).start())
        self.ag_copy(st, b, c, 2, src).start()

    def s6(self, b):
        for st in (0, 1):
            self.r3_copy(st, b).wait()
            rows = pl.ds(pl.multiple_of(self.p * CH, CH), CH)
            fin = self.fin.at[st, lax.rem(b, FS)]
            fin[...] = self.zbuf[st, lax.rem(b, ZS), rows] + self.r3[st, lax.rem(b, 2)]
            self.spread(st, b, self.p, True, True, fin)
            self.own_copy(st, b).start()
            pl.when(self.p == 0)(lambda: self.zsend(st, b, CH, 4 * CH, True).wait_send())
            pl.when(self.p == 3)(lambda: self.zsend(st, b, 0, 3 * CH, False).wait_send())

            @pl.when(self.p == 1)
            def _():
                self.zsend(st, b, 2 * CH, 4 * CH, True).wait_send()
                self.zsend(st, b, 0, CH, False).wait_send()

            @pl.when(self.p == 2)
            def _():
                self.zsend(st, b, 0, 2 * CH, False).wait_send()
                self.zsend(st, b, 3 * CH, 4 * CH, True).wait_send()

    def hop(self, k, b):
        for st in (0, 1):
            @pl.when(self.p >= k)
            def _():
                self.ag_copy(st, b, self.p - k, 0).wait_recv()
                self.spread(st, b, self.p - k, True, False)

            @pl.when(self.p <= 3 - k)
            def _():
                self.ag_copy(st, b, self.p + k, 1).wait_recv()
                self.spread(st, b, self.p + k, False, True)

    def s7(self, b):
        self.hop(1, b)

    def s8(self, b):
        self.hop(2, b)

    def s9(self, b):
        self.hop(3, b)

    def s10(self, b):
        for st in (0, 1):
            self.own_copy(st, b).wait()
            for c in range(4):
                got = self.ag_copy(st, b, c, 2)
                got.wait_send()
                got.wait_recv()
                pl.when((self.p < 3) & (self.p >= c))(lambda: self.ag_copy(st, b, c, 0).wait_send())
                pl.when((self.p > 0) & (self.p <= c))(lambda: self.ag_copy(st, b, c, 1).wait_send())
        pair = lax.rem(b, LEG) // 2
        pl.when((1 - b // LEG != self.s) & (lax.rem(b, 2) == 1))(lambda: self.home(pair).start())

    stages = ("s0", "s1", "s2", "s3", "s4", "s5", "s6", "s7", "s8", "s9", "s10")

    def home(self, pair):
        return self.remote(self.pool.at[NB + pair], self.pool.at[2 * pair + self.s], self.h_s.at[pair], self.h_r.at[pair], self.core)

    def keep_copy(self, b):
        if b < 4:
            to = self.ws.at[pl.ds(b * BLK, BLK)]
        elif b < 8:
            to = self.we.at[:, pl.ds((b - 4) * BLK, BLK)]
        else:
            to = self.w4.at[b - 8]
        return pltpu.make_async_copy(self.pool.at[b], to, self.k_s.at[b])

    def keep(self, pair):
        self.home(pair).wait_recv()
        for b in (2 * pair, 2 * pair + 1):
            self.keep_copy(b).start()

    def finish(self):
        for pair in range(NB // 2):
            self.home(pair).wait_send()
        for b in range(NB):
            self.keep_copy(b).wait()

    def tick(self, t):
        for k in reversed(range(len(self.stages))):
            b = t - k
            when(0 <= b < NP if isinstance(b, int) else (b >= 0) & (b < NP), lambda: getattr(self, self.stages[k])(b))

    def vec_copy(self, k):
        s, z, y, x = coords()
        odd = lax.rem(z, 2)
        to = (self.core, dev(s, z, y, 1 - x), dev(s, z, 1 - y, x), dev(s, z + 1 - 2 * odd, y, x), dev(s, jnp.clip(3 - z, 1, 2), y, x),
              dev(s, jnp.where(z == 1, 0, 3), y, x))[k]
        src = self.vec.at[1 - s] if k == 0 else self.vcur.at[(k - 1) % 2]
        return self.remote(src, self.vrecv.at[k], self.v_s.at[k], self.v_r.at[k], to)

    def vec_step(self, k):
        inner = (self.p == 1) | (self.p == 2)
        if k < 4:
            self.vec_copy(k).wait()
            before = self.vec[self.s] if k == 0 else self.vcur[(k - 1) % 2]
            self.vcur[k % 2] = before + self.vrecv[k]
            if k < 3:
                self.vec_copy(k + 1).start()
            else:
                pl.when(inner)(lambda: self.vec_copy(4).start())
        elif k == 4:
            @pl.when(inner)
            def _():
                self.vec_copy(4).wait()
                self.vcur[0] = self.vcur[1] + self.vrecv[4]
                self.vec_copy(5).start()
        else:
            pl.when(inner)(lambda: self.vec_copy(5).wait_send())

            @pl.when((self.p == 0) | (self.p == 3))
            def _():
                self.vec_copy(5).wait_recv()
                self.vcur[0] = self.vrecv[5]


def comm_scratch():
    bf = jnp.bfloat16
    dma = pltpu.SemaphoreType.DMA
    return dict(
        lda=pltpu.VMEM((2, PART, COL), bf), x1=pltpu.VMEM((2, XS, HALF, COL), bf), ldp=pltpu.VMEM((2, PART, COL), bf),
        r1=pltpu.VMEM((2, RS, HALF, COL), bf), zbuf=pltpu.VMEM((2, ZS, HALF, COL), bf),
        ru=pltpu.VMEM((2, 3, 3 * CH, COL), bf), rd=pltpu.VMEM((2, 3, 3 * CH, COL), bf),
        r3=pltpu.VMEM((2, 2, CH, COL), bf), fin=pltpu.VMEM((2, FS, CH, COL), bf),
        vcur=pltpu.VMEM((2, 16, BLK), jnp.float32), vrecv=pltpu.VMEM((6, 16, BLK), jnp.float32),
        prt_s=dma((NB,)), prt_r=dma((NB,)), h_s=dma((NB // 2,)), h_r=dma((NB // 2,)), k_s=dma((NB,)), ld_sem=dma((2, 2)), r1_s=dma((2, RS)), r1_r=dma((2, RS)),
        ru_s=dma((2, 4)), ru_r=dma((2, 4)), rd_s=dma((2, 4)), rd_r=dma((2, 4)), r3_s=dma((2, 2)), r3_r=dma((2, 2)),
        ag_s=dma((2, 3, 4, 4)), fin_s=dma((2, 4)), zr=dma((2, NP, 4)), xr=dma((2, NP, 4)), v_s=dma((6,)), v_r=dma((6,)),
    )


def scoped(name, fn, *args):
    with jax.named_scope(name):
        fn(*args)


class Program(Net):
    def __init__(self, refs, chips):
        super().__init__(refs)
        self.chips = chips
        self.s = lax.axis_index("section")
        self.core = (1 - self.s, lax.axis_index("batch"))
        self.comm = Comm(refs) if chips == 16 else None
        self.sent = []
        self.ticks = 0
        self.plan = {}

    def here(self, l, yes, no):
        pl.when(self.s == l)(yes)
        pl.when(self.s != l)(no)

    def remote(self, src, dst, ss, rs):
        return pltpu.make_async_remote_copy(src_ref=src, dst_ref=dst, send_sem=ss, recv_sem=rs, device_id=self.core, device_id_type=MESH)

    def barrier(self):
        if self.comm:
            self.comm.barrier()
        else:
            bar = pltpu.get_barrier_semaphore()
            pl.semaphore_signal(bar, inc=1, device_id=self.core, device_id_type=MESH)
            pl.semaphore_wait(bar, 1)

    def swap(self, m):
        return self.remote(self.own[m], self.other[m], self.wx_s.at[m], self.wx_r.at[m])

    def swap_par(self):
        return self.remote(self.par.at[self.s], self.par.at[self.s], self.wx_s.at[6], self.wx_r.at[6])

    def held(self, m):
        return self.w4.at[m] if m < 4 else (self.we, self.ws)[m - 4]

    def first_refs(self, m):
        if m < 5:
            return self.own[m], self.held(m)
        rows = (pl.ds(0, FF // 2), pl.ds(FF // 2, FF // 4), pl.ds(3 * FF // 4, FF // 4))[m - 5]
        return self.own[5].at[rows], self.ws.at[rows]

    def direct(self, m):
        to = self.comm.cross[m - 6] if self.comm and m > 5 else self.core
        src, dst = self.first_refs(m)
        return pltpu.make_async_remote_copy(src_ref=src, dst_ref=dst, send_sem=self.dx_s.at[m], recv_sem=self.dx_r.at[m], device_id=to,
                                            device_id_type=MESH)

    def first_near(self, m):
        return pltpu.make_async_copy(*self.first_refs(m), self.w_sem.at[m])

    def near(self, m):
        return pltpu.make_async_copy(self.own[m], self.held(m), self.w_sem.at[m])

    def wait_first(self, m):
        for i in (m,) if m < 6 else (6, 7):
            self.here(0, lambda: self.first_near(i).wait(), lambda: self.direct(i).wait_recv())
        if m != 5:
            pl.when(self.s == 1)(lambda: self.save(min(m, 5)).start())

    def save(self, m):
        return pltpu.make_async_copy(self.held(m), self.other[m], self.sv_sem.at[m])

    def load(self, l, m):
        def mine():
            if l == 1:
                self.save(m).wait()
            self.near(m).start()

        def theirs():
            if l == 1:
                self.swap(m).wait_recv()
            pltpu.make_async_copy(self.other[m], self.held(m), self.w_sem.at[m]).start()
        self.here(l, mine, theirs)

    def wait_load(self, m):
        self.near(m).wait()

    def aside(self, k, out):
        a, b = (self.probs, self.inner, self.act, self.q, self.k, self.v)[k], self.sp[k]
        return pltpu.make_async_copy(*((a, b) if out else (b, a)), self.sp_sem.at[k])

    def rows_near(self, k, l, src):
        return pltpu.make_async_copy(src, self.rows_at(k), self.ro_s.at[k, l])

    def rows_far(self, k, l, src):
        return self.remote(src, self.rows_at(k), self.ro_s.at[k, l], self.ro_r.at[k])

    def rows_at(self, k):
        return (self.lo, self.gi)[k].at[pl.ds(pl.multiple_of(self.s * T, T), T)]

    def put_rows(self, k, l, src):
        self.here(l, lambda: self.rows_near(k, l, src).start(), lambda: self.rows_far(k, l, src).start())

    def wait_rows(self, k, l, src):
        self.here(l, lambda: self.rows_near(k, l, src).wait(), lambda: self.rows_far(k, l, src).wait_send())

    def out_near(self, i, slot):
        return pltpu.make_async_copy(self.stage.at[slot], self.acc.at[i], self.st_sem.at[slot])

    def out_far(self, i, slot):
        return self.remote(self.stage.at[slot], self.prt.at[i], self.st_sem.at[slot], self.prt_r.at[i])

    def free_slot(self):
        if len(self.sent) < SLOTS:
            return len(self.sent)
        i, has, slot, done = self.sent[-SLOTS]
        if not done:
            self.settle(i)
        pl.when(self.s != has)(lambda: self.out_far(i, slot).wait_send())
        return slot

    def emit_out(self, l, b, slot):
        i = pair_place(l, b)
        self.here(b % 2, lambda: self.out_near(i, slot).start(), lambda: self.out_far(i, slot).start())
        self.sent.append([i, b % 2, slot, False])

    def settle(self, upto):
        for entry in self.sent:
            if entry[0] <= upto and not entry[3]:
                entry[3] = True
                pl.when(self.s == entry[1])(lambda: self.out_near(entry[0], entry[2]).wait())

    def point(self, name):
        if self.comm is None:
            return
        for _ in range(self.plan.get((self.layer, name), 0)):
            assert self.ticks >= NP or len(self.sent) >= 2 * (self.ticks // 2 + 1)
            self.settle(self.ticks // 2)
            scoped("tick", self.comm.tick, self.ticks)
            self.ticks += 1

    def forward(self, l, low):
        self.layer = l
        ready = self.wait_first if l == 0 else self.wait_load
        if l == 1:
            for k in (3, 4, 5):
                self.aside(k, True).wait()
        scoped("qkv", self.qkv, l, ready)
        if l == 1:
            self.aside(0, True).wait()
        scoped("attend", self.attend, l)
        if l == 1:
            self.load(1, 5)
        if l == 0:
            for m in range(3):
                self.load(1, m)
            for k in (3, 4, 5, 0):
                self.aside(k, True).start()
        ready(3)
        scoped("mix", self.mix, l)
        if l == 0:
            self.load(1, 3)
        else:
            self.aside(1, True).wait()
            self.aside(2, True).wait()
        ready(4)
        scoped("expand", self.expand, l)
        if l == 0:
            self.load(1, 4)
            self.aside(1, True).start()
            self.aside(2, True).start()
        scoped("shrink", self.shrink, l, low, ready)

    def backward(self, l):
        self.layer = l
        again = l == 1
        if not again:
            self.aside(2, False).wait()
        scoped("top_back", self.top_back, l, lambda rows: self.gin[rows].astype(F32))
        if again:
            self.aside(2, False).start()
        else:
            self.load(0, 3)
            for m in range(3):
                self.load(0, m)
            self.aside(1, False).wait()
            self.wait_load(5)
        scoped("inner_back", self.inner_back, l, lambda: again and self.aside(1, False).start(), lambda: again or self.wait_load(4))
        if again:
            self.wait_rows(0, 1, self.ag)
        else:
            self.wait_load(3)
        scoped("mid_back", self.mid_back, l)
        if not again:
            for k in (0, 3, 4, 5):
                self.aside(k, False).wait()
        scoped("attend_back", self.attend_back, l)
        if again:
            for k in (0, 3, 4, 5):
                self.aside(k, False).start()
        else:
            for m in range(3):
                self.wait_load(m)
            self.wait_rows(1, 1, self.gin)
        scoped("low_back", self.low_back, l, self.gin)
        if again:
            self.load(0, 5)
            self.load(0, 4)
        self.put_rows(1, l, self.gin)

    def run(self):
        s = self.s
        rows = pl.ds(pl.multiple_of(s * T, T), T)
        first = (pltpu.make_async_copy(self.tokens.at[rows], self.h.at[0], self.in_sem.at[0]),
                 pltpu.make_async_copy(self.cotangent.at[rows], self.gin, self.in_sem.at[1]))
        first[0].start()
        for m in range(8):
            pl.when(s == 0)(lambda: self.first_near(m).start())
        first[1].start()
        for r, ref in enumerate(self.small[:8]):
            self.par[s, r:r + 1, :] = ref[...]
        for j in range(4):
            self.par[s, EB + j:EB + j + 1, :] = self.small[8][:, j * D:(j + 1) * D]
        self.barrier()

        @pl.when(s == 0)
        def _():
            self.direct(0).start()
            self.swap_par().start()
            for m in (6, 7, 1, 2, 3, 4, 5):
                self.direct(m).start()

        @pl.when(s == 1)
        def _():
            self.swap_par().start()
            for m in range(6):
                self.swap(m).start()
        self.vec[...] = jnp.zeros_like(self.vec)
        self.labels(jnp.where(s == 0, self.ids[0:4, :], self.ids[4:8, :]))
        for c in first:
            c.wait()
        pl.when(s == 1)(lambda: self.swap_par().wait_recv())
        self.forward(0, self.h.at[1])
        self.put_rows(0, 0, self.h.at[1])
        pl.when(s == 0)(lambda: self.swap_par().wait_recv())
        self.forward(1, self.ag)
        self.put_rows(0, 1, self.ag)
        self.backward(1)
        self.point("done")
        self.backward(0)
        self.settle(NB)
        for i, has, slot, _ in self.sent[-SLOTS:]:
            pl.when(s != has)(lambda: self.out_far(i, slot).wait_send())
        if self.comm:
            self.comm.vec_copy(0).start()

            def step(t, c):
                scoped("tick", self.comm.tick, t)
                for k in range(6):
                    pl.when(t == VEC_TICK + k)(functools.partial(self.comm.vec_step, k))
                for k in range(NB // 2 - 1):
                    pl.when(t == LEG + len(Comm.stages) + 2 * k + 1)(functools.partial(self.comm.keep, k))
                return c
            lax.fori_loop(self.ticks, TICKS, step, 0)
            self.vec_out[...] = self.comm.vcur[0]
            self.comm.keep(NB // 2 - 1)
            self.comm.finish()
        else:
            for i in range(NB):
                self.out_far(i, 0).wait_recv()
            self.vec_out[...] = self.vec[...]
        for m in range(6):
            pl.when(s == 1)(lambda: self.swap(m).wait_send())
        for m in range(8):
            pl.when(s == 0)(lambda: self.direct(m).wait_send())
        self.swap_par().wait_send()
        self.wait_rows(0, 0, self.h.at[1])
        self.wait_rows(1, 0, self.gin)
        for k in (0, 1):
            self.rows_far(k, 0, self.gin).wait_recv()


def kernel(chips, names, plan, *refs):
    tokens, cotangent, ids = refs[0:3]
    weights = refs[3:9]
    small = refs[9:18]
    lo, gi, pool, vec_out, acc, prt, o4, oe, os_ = refs[18:27]
    named = dict(zip(names, refs[33:]))
    named.update(tokens=tokens, cotangent=cotangent, ids=ids, own=[w.at[0] for w in weights], small=small, lo=lo, gi=gi, pool=pool,
                 vec_out=vec_out, acc=acc, prt=prt, other=[o4.at[0], o4.at[1], o4.at[2], o4.at[3], oe, os_],
                 sp=refs[27:33])
    p = Program(named, chips)
    p.plan = plan
    p.run()


TICKS = NP + len(Comm.stages) - 1
VEC_TICK = TICKS - 7
PLAN = {(1, name): 1 for name in ("e1", "e2", "e3", "inner", "e7", "first", "mixer", "heads", "e9", "e11")}
PLAN.update({(0, name): 1 for name in ("e0", "e2", "inner", "e6", "first", "mixer", "heads", "attend", "e9", "e11")})


def both_layers(chips, tokens, cotangent, ids, weights, small):
    S = jax.ShapeDtypeStruct
    dma = pltpu.SemaphoreType.DMA
    sc = net_scratch()
    sc.update(comm_scratch())
    sc.update(wx_s=dma((7,)), wx_r=dma((7,)), dx_s=dma((8,)), dx_r=dma((8,)), w_sem=dma((8,)), sv_sem=dma((6,)), sp_sem=dma((6,)), ro_s=dma((2, 2)), ro_r=dma((2,)), st_sem=dma((SLOTS,)),
              in_sem=dma((2,)))
    hbm, vm = pl.BlockSpec(memory_space=pl.ANY), pl.BlockSpec(memory_space=pltpu.VMEM)
    kept = dict(w4=pltpu.VMEM((4, D, D), BF16), we=pltpu.VMEM((D, FF), BF16), ws=pltpu.VMEM((FF, D), BF16))
    here = chips == 16
    if not here:
        sc.update(kept)
    mem, rows_spec = (pltpu.VMEM, vm) if here else (S, hbm)
    rows = mem((2 * T, D), BF16)
    out = pl.pallas_call(
        functools.partial(kernel, chips, (tuple(kept) if here else ()) + tuple(sc), PLAN),
        out_shape=(rows, rows, S((NB + NB // 2, D, D), BF16), mem((16, D) if here else (2, 16, D), F32), S((NB, D, D), BF16),
                   S((NB, D, D), BF16), S((4, D, D), BF16), S((D, FF), BF16), S((FF, D), BF16), S((HEADS, T, T), BF16), S((T, FF), BF16),
                   S((T, FF), BF16)) + (S((T, D), BF16),) * 3 + (tuple(kept.values()) if here else ()),
        in_specs=[hbm, hbm, vm] + [hbm] * 6 + [vm] * 9,
        out_specs=(rows_spec, rows_spec, hbm, vm) + (hbm,) * 11 + ((vm,) * 3 if here else ()),
        scratch_shapes=list(sc.values()),
        compiler_params=pltpu.CompilerParams(collective_id=0, has_side_effects=True, vmem_limit_bytes=(47 if here else 63) * 2**20),
    )(tokens, cotangent, ids, *weights, *small)
    return out[:6] + (out[-3:] if here else (None,) * 3)


WROWS, WBUFS = 768, 4


def widen_kernel(rest_in, ex_in, sh_in, vec, lo, gi, sh, ex, mi, q, k, v, lo_out, gi_out, *rest):
    small, (low, wide, in_sem, out_sem, row_buf, row_sem, vec_buf, vec_sem) = rest[:9], rest[9:]
    vec_in = pltpu.make_async_copy(vec, vec_buf, vec_sem)
    rows_in = [pltpu.make_async_copy(a, row_buf.at[i], row_sem.at[i]) for i, a in enumerate((lo, gi))]
    rows_out = [pltpu.make_async_copy(row_buf.at[i], a.at[0], row_sem.at[i]) for i, a in enumerate((lo_out, gi_out))]
    per = D // WROWS
    count = NB * per

    def take(i):
        b, r = i // per, (i % per) * WROWS
        if b < 4:
            src = sh_in.at[pl.ds(b * D + r, WROWS)]
        elif b < 8:
            src = ex_in.at[pl.ds(r, WROWS), pl.ds((b - 4) * D, D)]
        else:
            src = rest_in.at[b - 8, pl.ds(r, WROWS)]
        return pltpu.make_async_copy(src, low.at[i % WBUFS], in_sem.at[i % WBUFS])

    def put(i):
        b, r = i // per, (i % per) * WROWS
        if b < 4:
            to = sh.at[0, pl.ds(b * D + r, WROWS)]
        elif b < 8:
            to = ex.at[0, pl.ds(r, WROWS), pl.ds((b - 4) * D, D)]
        else:
            to = (mi, q, k, v)[b - 8].at[0, pl.ds(r, WROWS)]
        return pltpu.make_async_copy(wide.at[i % WBUFS], to, out_sem.at[i % WBUFS])

    for i in range(WBUFS):
        take(i).start()
    vec_in.start()
    for c in rows_in:
        c.start()
    vec_in.wait()
    for r in range(8):
        small[r][...] = vec_buf[r:r + 1, :]
    for j in range(4):
        small[8][:, j * D:(j + 1) * D] = vec_buf[EB + j:EB + j + 1, :]
    for i in range(count):
        take(i).wait()
        if i >= WBUFS:
            put(i - WBUFS).wait()

        def convert(j, c):
            rows = tile(j, 32)
            wide[i % WBUFS, rows] = low[i % WBUFS, rows].astype(F32)
            return c
        lax.fori_loop(0, WROWS // 32, convert, 0, unroll=4)
        put(i).start()
        if i == 1:
            for a, b in zip(rows_in, rows_out):
                a.wait()
                b.start()
        if i + WBUFS < count:
            take(i + WBUFS).start()
    for i in range(count - WBUFS, count):
        put(i).wait()
    for c in rows_out:
        c.wait()


def widen(rest_in, ex_in, sh_in, vec, lo, gi):
    S = jax.ShapeDtypeStruct
    hbm, vm = pl.BlockSpec(memory_space=pl.ANY), pl.BlockSpec(memory_space=pltpu.VMEM)
    square, row = S((1, D, D), F32), S((1, D), F32)
    return pl.pallas_call(
        widen_kernel,
        out_shape=(S((1, FF, D), F32), S((1, D, FF), F32), square, square, square, square, S((1, 2 * T, D), BF16), S((1, 2 * T, D), BF16)) + (row,) * 8 + (S((1, FF), F32),),
        in_specs=[hbm] * 6, out_specs=(hbm,) * 8 + (vm,) * 9,
        scratch_shapes=[pltpu.VMEM((WBUFS, WROWS, D), BF16), pltpu.VMEM((WBUFS, WROWS, D), F32),
                        pltpu.SemaphoreType.DMA((WBUFS,)), pltpu.SemaphoreType.DMA((WBUFS,)), pltpu.VMEM((2, 2 * T, D), BF16), pltpu.SemaphoreType.DMA((2,)), pltpu.VMEM((16, D), F32), pltpu.SemaphoreType.DMA],
        compiler_params=pltpu.CompilerParams(vmem_limit_bytes=24 * 2**20),
    )(rest_in, ex_in, sh_in, vec, lo, gi)


def body(tokens, cotangent, sentence_ids, *stored):
    (query_w, query_b, keys_w, value_w, value_b, mixer_w, mixer_b, gain_one, shift_one, expand_w, expand_b, shrink_w, shrink_b, gain_two,
     shift_two) = stored
    chips = lax.axis_size("batch")
    lo, gi, pool, vec, acc, prt, rest, ex, sh = both_layers(
        chips, tokens, cotangent, sentence_ids.reshape(8, PAIR), (query_w, keys_w, value_w, mixer_w, expand_w, shrink_w),
        (query_b, value_b, mixer_b, gain_one, shift_one, shrink_b, gain_two, shift_two, expand_b))
    if chips != 16:
        s = lax.axis_index("section")
        part = acc.astype(F32) + prt.astype(F32)
        part = part.reshape(2, NB // 2, 1, D, D)
        pairs = jnp.where(lax.broadcasted_iota(jnp.int32, (1, 1, 2, 1, 1), 2) == s, part, 0.0)
        both = lax.psum(pairs, ("section", "batch")).reshape(2, NB, D, D)
        pool = lax.dynamic_index_in_dim(both, 1 - s, 0, keepdims=False).astype(BF16)
        sh, ex, rest = pool[:4].reshape(FF, D), pool[4:8].transpose(1, 0, 2).reshape(D, FF), pool[8:]
        vec = lax.dynamic_index_in_dim(lax.psum(vec, ("section", "batch")), s, 0, keepdims=False)
    sh, ex, mi, q, k, v, lo, gi, qb, vb, mb, g1, s1, sb, g2, s2, eb = widen(rest, ex, sh, vec, lo, gi)
    return (lo, gi, q, qb, k, v, vb, mi, mb, g1, s1, ex, eb, sh, sb, g2, s2)


def solution(mesh):
    placed = (
        P("batch", None),
        P("batch", None),
        P("batch"),
        P("section", None, None),
        P("section", None),
        P("section", None, None),
        P("section", None, None),
        P("section", None),
        P("section", None, None),
        P("section", None),
        P("section", None),
        P("section", None),
        P("section", None, None),
        P("section", None),
        P("section", None, None),
        P("section", None),
        P("section", None),
        P("section", None),
    )
    return jax.shard_map(
        body,
        mesh=mesh,
        in_specs=placed,
        out_specs=(
            P("section", "batch", None),
            P("section", "batch", None),
            P("section", None, None),
            P("section", None),
            P("section", None, None),
            P("section", None, None),
            P("section", None),
            P("section", None, None),
            P("section", None),
            P("section", None),
            P("section", None),
            P("section", None, None),
            P("section", None),
            P("section", None, None),
            P("section", None),
            P("section", None),
            P("section", None),
        ),
        check_vma=False,
    )
```
